128 devices in a mesh: segment: 4 (over z), dp: 32 (over x, y, core).
Axes of the slice: x: 4, y: 4, z: 4, core: 2. Of those that a mesh axis runs over, the one named last changes fastest.
Arguments:
- tokens: float32 [1024, 16, 1536], P('dp', 'segment'), may hold values from -21 to 21
- cotangent: float32 [1024, 16, 1536], P('dp', 'segment'), may hold values from -6 to 6
- image_size: int32 [1024, 2], replicated, may hold values from 4 to 16, as said below
- slot_image: int32 [1024], P('dp'), may hold values from 0 to 1023, each once
- slot_batch: int32 [1024], P('dp'), may hold values from 0 to 3, as said below
- norm_gains: float32 [2, 4, 96], replicated, may hold values from 0.5 to 1.5
- biases: float32 [2, 12, 96], replicated, may hold values from -3 to 3
- depth_taps: float32 [2, 9, 96], replicated, may hold values from -2 to 2
- spread_taps: float32 [2, 4, 96], replicated, may hold values from -4 to 4
- point_first: float32 [2, 96, 96], replicated, may hold values from -0.625 to 0.625
- point_second: float32 [2, 96, 96], replicated, may hold values from -0.625 to 0.625
- mixer_weight: float32 [2, 96, 288], replicated, may hold values from -1.25 to 1.25
- output_weight: float32 [2, 96, 96], replicated, may hold values from -0.625 to 0.625
- expand_weight: float32 [2, 96, 384], replicated, may hold values from -0.625 to 0.625
- expand_bias: float32 [2, 384], replicated, may hold values from -3 to 3
- reduce_weight: float32 [2, 384, 96], replicated, may hold values from -0.3125 to 0.3125
Outputs:
- activations: float32 [1024, 16, 1536], P('dp', 'segment')
- input_grad: float32 [1024, 16, 1536], P('dp', 'segment')
- grad_gains: float32 [2, 4, 96], replicated
- grad_biases: float32 [2, 12, 96], replicated
- grad_depth: float32 [2, 9, 96], replicated
- grad_spread: float32 [2, 4, 96], replicated
- grad_point_first: float32 [2, 96, 96], replicated
- grad_point_second: float32 [2, 96, 96], replicated
- grad_mixer: float32 [2, 96, 288], replicated
- grad_output: float32 [2, 96, 96], replicated
- grad_expand: float32 [2, 96, 384], replicated
- grad_expand_bias: float32 [2, 384], replicated
- grad_reduce: float32 [2, 384, 96], replicated
The draws below stay inside these ranges and needn't reach their ends.
Inputs may be any that keep to these rules, and one draw needn't show every extreme that they name: `image_size`: heights and widths are even; some image is 16 by 16. `slot_image`: every image sits in exactly one slot. `slot_batch`: the 32 slots of one index of dp hold each micro-batch exactly 8 times.
All inputs are finite; a program needn't handle non-finite values.
Results may differ from the reference program's by a relative error of at most 0.0003.
Values sent between devices are 32-bit elements; how exact they have to be, the bound alone decides.
A program may use at most 320 MiB of HBM per device.

```python
import math
import jax
import jax.numpy as jnp
from jax import lax

D = 96
HEADS = 2
FF = 384
LAYERS = 2
MICRO = 4
SIDE = 16
IMG_MB = 8
SLOTS = 1024
IMAGES = 1024
N_DP = 32


def batch_labels(key):
    row_keys = jax.random.split(jax.random.fold_in(key, 17), N_DP)
    base_labels = jnp.arange(MICRO * IMG_MB, dtype=jnp.int32) % MICRO
    shuffled = jax.vmap(lambda row_key: jax.random.permutation(row_key, base_labels))(row_keys)
    return shuffled.reshape(-1).astype(jnp.int32)


def draw_slot_batch(key, part):
    labels = batch_labels(key)
    return labels


def draw_tokens(key, part):
    labels = batch_labels(key)
    key = jax.random.fold_in(key, 5)
    scale_key, slot_key, noise_key, offset_key = jax.random.split(key, 4)
    group_scale = jnp.exp(jax.random.uniform(scale_key, (MICRO,), jnp.float32, math.log(0.3), math.log(3.0)))
    slot_scale = group_scale[labels] * jnp.exp(jax.random.uniform(slot_key, (SLOTS,), jnp.float32, math.log(0.7), math.log(1.4)))
    noise_field = jnp.clip(jax.random.normal(noise_key, (SLOTS, SIDE, SIDE, D), jnp.float32), -4.0, 4.0)
    offset = 0.5 * jnp.clip(jax.random.normal(offset_key, (SLOTS, 1, 1, D), jnp.float32), -2.0, 2.0)
    return ((noise_field + offset) * slot_scale[:, None, None, None]).reshape(SLOTS, SIDE, SIDE * D)


def draw_image_size(key, part):
    key = jax.random.fold_in(key, 7)
    base_key, jitter_key, pick_key = jax.random.split(key, 3)
    height_level = jax.random.randint(base_key, (IMAGES,), 0, 64)
    width_level = jnp.clip(height_level + jax.random.randint(jitter_key, (IMAGES,), -6, 7), 0, 63)
    chosen = jax.random.randint(pick_key, (), 0, IMAGES)
    is_top = jnp.arange(IMAGES) == chosen
    height_level = jnp.where(is_top, 63, height_level)
    width_level = jnp.where(is_top, 63, width_level)

    def measure(level_steps):
        return 2 * jnp.maximum(2, SIDE // 2 * (250047 - (63 - level_steps) ** 3) // 250047)
    return jnp.stack([measure(height_level), measure(width_level)], axis=1).astype(jnp.int32)


def shard_levels(rng, shape, pieces, smallest, top_value):
    gain, own = 1.0, jax.random.fold_in(rng, 6)
    for dim, shards_of in pieces:
        steps = jnp.exp(jax.random.uniform(jax.random.fold_in(own, dim), (shards_of,), jnp.float32, smallest / len(pieces), top_value / len(pieces)))
        gain = gain * jnp.repeat(steps, shape[dim] // shards_of).reshape([-1 if axis == dim else 1 for axis in range(len(shape))])
    return gain


def bell_draw(stream_key, extent, scale, most, pieces=(), kind=jnp.bfloat16):
    drawn = jax.random.normal(stream_key, extent, jnp.float32) * scale
    if len(pieces) > 0:
        drawn = shard_levels(stream_key, extent, pieces, -0.22, 0.18) * drawn
    return jnp.clip(drawn, min=-most, max=most).astype(kind)


def setup_inputs(seed: int = 0) -> dict:
    key_list = jax.random.split(jax.random.key(seed), 17)
    tokens = draw_tokens(jax.random.fold_in(key_list[16], 71), 0)
    cotangent = bell_draw(key_list[1], (SLOTS, SIDE, SIDE * D), 1.0, 6.0, ((0, 32), (1, 4)), jnp.float32)
    image_size = draw_image_size(jax.random.fold_in(key_list[16], 71), 0)
    slot_image = jax.random.permutation(key_list[3], SLOTS).astype(jnp.int32)
    slot_batch = draw_slot_batch(jax.random.fold_in(key_list[16], 71), 0)
    norm_gains = jnp.clip(1.0 + 0.1 * jax.random.normal(key_list[5], (LAYERS, 4, D), jnp.float32), 0.5, 1.5)
    biases = bell_draw(key_list[6], (LAYERS, 12, D), 0.5, 3.0, (), jnp.float32)
    depth_taps = bell_draw(key_list[7], (LAYERS, 9, D), 9 ** -0.5, 2.0, (), jnp.float32)
    spread_taps = bell_draw(key_list[8], (LAYERS, 4, D), 1.0, 4.0, (), jnp.float32)
    point_first = bell_draw(key_list[9], (LAYERS, D, D), D ** -0.5, 0.625, (), jnp.float32)
    point_second = bell_draw(key_list[10], (LAYERS, D, D), D ** -0.5, 0.625, (), jnp.float32)
    mixer_weight = bell_draw(key_list[11], (LAYERS, D, 3 * D), (D // 4) ** -0.5, 1.25, (), jnp.float32)
    output_weight = bell_draw(key_list[12], (LAYERS, D, D), D ** -0.5, 0.625, (), jnp.float32)
    expand_weight = bell_draw(key_list[13], (LAYERS, D, FF), D ** -0.5, 0.625, (), jnp.float32)
    expand_bias = bell_draw(key_list[14], (LAYERS, FF), 0.5, 3.0, (), jnp.float32)
    reduce_weight = bell_draw(key_list[15], (LAYERS, FF, D), FF ** -0.5, 0.3125, (), jnp.float32)
    return {"tokens": tokens, "cotangent": cotangent, "image_size": image_size, "slot_image": slot_image, "slot_batch": slot_batch, "norm_gains": norm_gains, "biases": biases, "depth_taps": depth_taps, "spread_taps": spread_taps, "point_first": point_first, "point_second": point_second, "mixer_weight": mixer_weight, "output_weight": output_weight, "expand_weight": expand_weight, "expand_bias": expand_bias, "reduce_weight": reduce_weight}


EPSILON = 1e-05
HIGHEST = lax.Precision.HIGHEST
MASKED_SCORE = -1000000000.0

@jax.custom_vjp
def low(v):
    return lax.optimization_barrier(v.astype(jnp.bfloat16)).astype(jnp.float32)

@jax.custom_vjp
def low_back(v):
    return v

def low_keep(v):
    return (low(v), None)

def low_pass(kept, grad):
    return (grad,)

def back_keep(v):
    return (v, None)

def back_low(kept, grad):
    return (low(grad),)
low.defvjp(low_keep, low_pass)
low_back.defvjp(back_keep, back_low)

def linear_map(values, matrix):
    return jnp.dot(values, matrix, precision=HIGHEST, preferred_element_type=jnp.float32)

def layer_norm(values, gain_row, shift_row):
    centre = values - lax.optimization_barrier(jnp.mean(values, axis=-1, keepdims=True))
    variance = lax.optimization_barrier(jnp.mean(centre * centre, axis=-1, keepdims=True))
    return centre * lax.rsqrt(variance + EPSILON) * gain_row + shift_row

def depthwise(planes, tap_rows, shift_row):
    height = planes.shape[1]
    width = planes.shape[2]
    padded = jnp.pad(planes, ((0, 0), (1, 1), (1, 1), (0, 0)))
    summed = jnp.zeros_like(planes) + shift_row
    for row_index in range(3):
        for col_index in range(3):
            window = padded[:, row_index:row_index + height, col_index:col_index + width]
            summed = summed + window * tap_rows[3 * row_index + col_index]
    return summed

def pooled_delegates(planes):
    batch_count, height, width, channels = planes.shape
    blocks = planes.reshape(batch_count, height // 2, 2, width // 2, 2, channels)
    return lax.optimization_barrier(jnp.mean(blocks, axis=(2, 4)))

def propagate(mixture, tap_rows, shift_row):
    batch_count, row_count, col_count, channels = mixture.shape
    tap_grid = tap_rows.reshape(2, 2, channels)
    spread = mixture[:, :, None, :, None, :] * tap_grid[None, None, :, None, :, :]
    return spread.reshape(batch_count, 2 * row_count, 2 * col_count, channels) + shift_row

def attend(delegates, delegate_mask, mixer_weight, query_bias, value_bias):
    batch_count, row_count, col_count, channels = delegates.shape
    head_size = channels // HEADS
    cells = row_count * col_count
    flattened = delegates.reshape(batch_count, cells, channels)
    mapped = linear_map(flattened, mixer_weight)
    queries = (mapped[..., :channels] + query_bias).reshape(batch_count, cells, HEADS, head_size)
    keyset = mapped[..., channels:2 * channels].reshape(batch_count, cells, HEADS, head_size)
    valueset = (mapped[..., 2 * channels:] + value_bias).reshape(batch_count, cells, HEADS, head_size)
    scores = jnp.einsum('bnhe,bmhe->bhnm', queries, keyset, precision=HIGHEST) / math.sqrt(head_size)
    scores = jnp.where(delegate_mask.reshape(batch_count, 1, 1, cells) > 0, scores, MASKED_SCORE)
    highest = lax.optimization_barrier(jnp.max(scores, axis=-1, keepdims=True))
    weights = jnp.exp(scores - highest)
    weights = weights / lax.optimization_barrier(jnp.sum(weights, axis=-1, keepdims=True))
    mixture = jnp.einsum('bhnm,bmhe->bnhe', weights, valueset, precision=HIGHEST)
    return mixture.reshape(batch_count, row_count, col_count, channels)

def local_apply(planes, token_mask, statistics, layer_params):
    norm_gains, biases, depth_taps = (layer_params[0], layer_params[1], layer_params[2])
    point_first, point_second = (layer_params[4], layer_params[5])
    channel_sums, squares, counts = statistics
    centre = channel_sums / counts
    variance = squares / counts - centre * centre
    normed = (planes - centre) * lax.rsqrt(variance + EPSILON) * norm_gains[0] + biases[0]
    first_map = (linear_map(normed, point_first) + biases[1]) * token_mask
    depth_map = depthwise(first_map, depth_taps, biases[2])
    return planes + token_mask * (linear_map(depth_map, point_second) + biases[3])

def global_apply(planes, token_mask, delegate_mask, layer_params):
    norm_gains, biases, spread_taps = (layer_params[0], layer_params[1], layer_params[3])
    mixer_weight, output_weight = (layer_params[6], layer_params[7])
    expand_weight, expand_bias, reduce_weight = (layer_params[8], layer_params[9], layer_params[10])
    normed = layer_norm(planes, norm_gains[1], biases[4])
    mixture = attend(pooled_delegates(normed), delegate_mask, mixer_weight, biases[5], biases[6])
    spread = layer_norm(propagate(mixture, spread_taps, biases[7]), norm_gains[2], biases[8])
    middle = planes + token_mask * (linear_map(spread, output_weight) + biases[9])
    hidden = jax.nn.gelu(linear_map(layer_norm(middle, norm_gains[3], biases[10]), expand_weight) + expand_bias, approximate=False)
    return middle + token_mask * (linear_map(hidden, reduce_weight) + biases[11])

def slot_masks(image_size, slot_image):
    onehot_table = (slot_image[:, None] == jnp.arange(image_size.shape[0], dtype=jnp.int32)[None, :]).astype(jnp.int32)
    chosen = jnp.dot(onehot_table, image_size)
    heights = chosen[:, 0]
    widths = chosen[:, 1]
    positions = jnp.arange(SIDE, dtype=jnp.int32)
    inside = (positions[None, :, None] < heights[:, None, None]) & (positions[None, None, :] < widths[:, None, None])
    token_mask = inside.astype(jnp.float32)[..., None]
    even_rows = 2 * jnp.arange(SIDE // 2, dtype=jnp.int32)
    delegate_mask = ((even_rows[None, :, None] < heights[:, None, None]) & (even_rows[None, None, :] < widths[:, None, None])).astype(jnp.int32)
    return (token_mask, delegate_mask)

def group_statistics(planes, token_mask, onehot, slot_batch):
    masked = planes * token_mask
    slot_sums = lax.optimization_barrier(jnp.sum(masked, axis=(1, 2)))
    slot_squares = lax.optimization_barrier(jnp.sum(masked * planes, axis=(1, 2)))
    slot_counts = lax.optimization_barrier(jnp.sum(token_mask, axis=(1, 2)))
    group_sums = lax.optimization_barrier(jnp.sum(onehot[:, :, None] * slot_sums[:, None, :], axis=0))
    group_squares = lax.optimization_barrier(jnp.sum(onehot[:, :, None] * slot_squares[:, None, :], axis=0))
    group_counts = lax.optimization_barrier(jnp.sum(onehot[:, :, None] * slot_counts[:, None, :], axis=0))
    return (group_sums[slot_batch][:, None, None, :], group_squares[slot_batch][:, None, None, :], group_counts[slot_batch][:, None, None, :])

def reference(tokens, cotangent, image_size, slot_image, slot_batch, norm_gains, biases, depth_taps, spread_taps, point_first, point_second, mixer_weight, output_weight, expand_weight, expand_bias, reduce_weight):
    token_mask, delegate_mask = slot_masks(image_size, slot_image)
    onehot = (slot_batch[:, None] == jnp.arange(MICRO, dtype=jnp.int32)[None, :]).astype(jnp.float32)
    start_planes = tokens.reshape(SLOTS, SIDE, SIDE, D)
    weights = (norm_gains, biases, depth_taps, spread_taps, point_first, point_second, mixer_weight, output_weight, expand_weight, expand_bias, reduce_weight)

    def global_part(planes, layer_params):
        return global_apply(planes, token_mask, delegate_mask, layer_params)

    def forward(start_values, weight_set):
        planes = start_values * token_mask
        for layer_index in range(LAYERS):
            layer_params = tuple((weight_array[layer_index] for weight_array in weight_set))
            statistics = group_statistics(planes, token_mask, onehot, slot_batch)
            planes = local_apply(planes, token_mask, statistics, layer_params)
            planes = jax.checkpoint(global_part)(planes, layer_params)
        return planes
    result, pullback = jax.vjp(forward, start_planes, weights)
    start_grad, weight_grads = pullback(cotangent.reshape(SLOTS, SIDE, SIDE, D))
    return (result.reshape(SLOTS, SIDE, SIDE * D), start_grad.reshape(SLOTS, SIDE, SIDE * D), weight_grads[0], weight_grads[1], weight_grads[2], weight_grads[3], weight_grads[4], weight_grads[5], weight_grads[6], weight_grads[7], weight_grads[8], weight_grads[9], weight_grads[10])
```

```python
import math

import jax
import jax.numpy as jnp
from jax import lax
from jax.sharding import PartitionSpec as P

D = 96
HEADS = 2
MICRO = 4
SIDE = 16
IMG_MB = 8


EPSILON = 1e-05
HIGHEST = lax.Precision.HIGHEST
MASKED_SCORE = -1000000000.0


def from_behind(value, axis, steps):
    count = lax.axis_size(axis)
    first, last = (max(0, -steps), min(count, count - steps))
    return lax.ppermute(value, axis, [(source, source + steps) for source in range(first, last)])


def linear_map(values, matrix):
    return jnp.dot(values, matrix, precision=HIGHEST, preferred_element_type=jnp.float32)


def layer_norm(values, gain_row, shift_row):
    centre = values - jnp.mean(values, axis=-1, keepdims=True)
    variance = jnp.mean(centre * centre, axis=-1, keepdims=True)
    return centre * lax.rsqrt(variance + EPSILON) * gain_row + shift_row


def depthwise(planes, tap_rows, shift_row):
    height = planes.shape[1]
    width = planes.shape[2]
    padded = jnp.pad(planes, ((0, 0), (1, 1), (1, 1), (0, 0)))
    summed = jnp.zeros_like(planes) + shift_row
    for row_index in range(3):
        for col_index in range(3):
            window = padded[:, row_index : row_index + height, col_index : col_index + width]
            summed = summed + window * tap_rows[3 * row_index + col_index]
    return summed


def pooled_delegates(planes):
    batch_count, height, width, channels = planes.shape
    blocks = planes.reshape(batch_count, height // 2, 2, width // 2, 2, channels)
    return jnp.mean(blocks, axis=(2, 4))


def propagate(mixture, tap_rows, shift_row):
    batch_count, row_count, col_count, channels = mixture.shape
    tap_grid = tap_rows.reshape(2, 2, channels)
    spread = mixture[:, :, None, :, None, :] * tap_grid[None, None, :, None, :, :]
    return spread.reshape(batch_count, 2 * row_count, 2 * col_count, channels) + shift_row


def attend(delegates, delegate_mask, mixer_weight, query_bias, value_bias):
    batch_count, row_count, col_count, channels = delegates.shape
    head_size = channels // HEADS
    cells = row_count * col_count
    flattened = delegates.reshape(batch_count, cells, channels)
    mapped = linear_map(flattened, mixer_weight)
    queries = (mapped[..., :channels] + query_bias).reshape(batch_count, cells, HEADS, head_size)
    keyset = mapped[..., channels : 2 * channels].reshape(batch_count, cells, HEADS, head_size)
    valueset = (mapped[..., 2 * channels :] + value_bias).reshape(
        batch_count, cells, HEADS, head_size
    )
    scores = jnp.einsum("bnhe,bmhe->bhnm", queries, keyset, precision=HIGHEST) / math.sqrt(
        head_size
    )
    scores = jnp.where(delegate_mask.reshape(batch_count, 1, 1, cells) > 0, scores, MASKED_SCORE)
    highest = jnp.max(scores, axis=-1, keepdims=True)
    weights = jnp.exp(scores - highest)
    weights = weights / jnp.sum(weights, axis=-1, keepdims=True)
    mixture = jnp.einsum("bhnm,bmhe->bnhe", weights, valueset, precision=HIGHEST)
    return mixture.reshape(batch_count, row_count, col_count, channels)


def local_apply(planes, token_mask, statistics, layer_params):
    norm_gains, biases, depth_taps = (layer_params[0], layer_params[1], layer_params[2])
    point_first, point_second = (layer_params[4], layer_params[5])
    channel_sums, squares, counts = statistics
    centre = channel_sums / counts
    variance = squares / counts - centre * centre
    normed = (planes - centre) * lax.rsqrt(variance + EPSILON) * norm_gains[0] + biases[0]
    first_map = (linear_map(normed, point_first) + biases[1]) * token_mask
    depth_map = depthwise(first_map, depth_taps, biases[2])
    return planes + token_mask * (linear_map(depth_map, point_second) + biases[3])


def global_apply(planes, token_mask, delegate_mask, layer_params):
    norm_gains, biases, spread_taps = (layer_params[0], layer_params[1], layer_params[3])
    mixer_weight, output_weight = (layer_params[6], layer_params[7])
    expand_weight, expand_bias, reduce_weight = (layer_params[8], layer_params[9], layer_params[10])
    normed = layer_norm(planes, norm_gains[1], biases[4])
    mixture = attend(pooled_delegates(normed), delegate_mask, mixer_weight, biases[5], biases[6])
    spread = layer_norm(propagate(mixture, spread_taps, biases[7]), norm_gains[2], biases[8])
    middle = planes + token_mask * (linear_map(spread, output_weight) + biases[9])
    hidden = jax.nn.gelu(
        linear_map(layer_norm(middle, norm_gains[3], biases[10]), expand_weight) + expand_bias,
        approximate=False,
    )
    return middle + token_mask * (linear_map(hidden, reduce_weight) + biases[11])


def slot_masks(image_size, slot_image):
    onehot_table = (
        slot_image[:, None] == jnp.arange(image_size.shape[0], dtype=jnp.int32)[None, :]
    ).astype(jnp.int32)
    chosen = jnp.dot(onehot_table, image_size)
    heights = chosen[:, 0]
    widths = chosen[:, 1]
    positions = jnp.arange(SIDE, dtype=jnp.int32)
    inside = (positions[None, :, None] < heights[:, None, None]) & (
        positions[None, None, :] < widths[:, None, None]
    )
    token_mask = inside.astype(jnp.float32)[..., None]
    even_rows = 2 * jnp.arange(SIDE // 2, dtype=jnp.int32)
    delegate_mask = (
        (even_rows[None, :, None] < heights[:, None, None])
        & (even_rows[None, None, :] < widths[:, None, None])
    ).astype(jnp.int32)
    return (token_mask, delegate_mask)


def onehot_stats(planes, token_mask, onehot):
    masked = planes * token_mask
    slot_sums = jnp.sum(masked, axis=(1, 2))
    slot_squares = jnp.sum(masked * planes, axis=(1, 2))
    slot_counts = jnp.sum(token_mask, axis=(1, 2))
    rows = jnp.concatenate([slot_sums, slot_squares, slot_counts], axis=1)
    groups = lax.psum(jnp.sum(onehot[:, :, None] * rows[:, None, :], axis=0), ("dp", "segment"))
    mine = jnp.sum(onehot[:, :, None] * groups[None], axis=1)[:, None, None, :]
    return mine[..., :D], mine[..., D : 2 * D], mine[..., 2 * D :]


def shards(tokens, cotangent, image_size, slot_image, slot_batch, *params):
    segments = lax.axis_size("segment")
    segment_index = lax.axis_index("segment")
    slot_count = slot_image.shape[0] // segments
    slot_image = lax.dynamic_slice_in_dim(slot_image, segment_index * slot_count, slot_count)
    slot_batch = lax.dynamic_slice_in_dim(slot_batch, segment_index * slot_count, slot_count)
    token_mask, delegate_mask = slot_masks(image_size, slot_image)
    onehot = (slot_batch[:, None] == jnp.arange(MICRO, dtype=jnp.int32)[None, :]).astype(jnp.float32)

    def gathered(rows):
        return lax.all_to_all(rows, "segment", 0, 1, tiled=True).reshape(slot_count, SIDE, SIDE, D)

    def scattered(planes):
        return lax.all_to_all(planes.reshape(slot_count, SIDE, SIDE * D), "segment", 1, 0, tiled=True)

    start = gathered(tokens) * token_mask
    upstream = gathered(cotangent)

    def forward(planes, weight_set):
        for layer_index in range(2):
            layer_params = tuple(weight_array[layer_index] for weight_array in weight_set)
            statistics = onehot_stats(planes, token_mask, onehot)
            planes = local_apply(planes, token_mask, statistics, layer_params)
            planes = global_apply(planes, token_mask, delegate_mask, layer_params)
        return planes

    result, pullback = jax.vjp(forward, start, params)
    start_grad, weight_grads = pullback(upstream)
    weight_sums = lax.psum(weight_grads, ("segment", "dp"))
    return (scattered(result), scattered(start_grad * token_mask)) + tuple(weight_sums)


def solution(mesh):
    placed = (
        P("dp", "segment", None),
        P("dp", "segment", None),
        P(),
        P("dp"),
        P("dp"),
        P(),
        P(),
        P(),
        P(),
        P(),
        P(),
        P(),
        P(),
        P(),
        P(),
        P(),
    )
    return jax.shard_map(
        shards,
        mesh=mesh,
        in_specs=placed,
        out_specs=(
            P("dp", "segment", None),
            P("dp", "segment", None),
            P(),
            P(),
            P(),
            P(),
            P(),
            P(),
            P(),
            P(),
            P(),
            P(),
            P(),
        ),
        check_vma=False,
    )
```

```python
import functools
import math
from types import SimpleNamespace

import jax
import jax.numpy as jnp
from jax import lax
from jax.experimental import pallas as pl
from jax.experimental.pallas import tpu as pltpu
from jax.sharding import PartitionSpec as P

D = 96
FF = 384
LAYERS = 2
MICRO = 4
SIDE = 16
EPSILON = 1e-05
MASKED_SCORE = -1000000000.0
LANES = 128
TILE = 256
CELLS = SIDE * LANES
DELEGATES = 512
PARAM_ROWS = 32
GRAD_ROWS = 1280
HIGHEST = lax.Precision.HIGHEST
f32 = jnp.float32
bf16 = jnp.bfloat16

NN = (((1,), (0,)), ((), ()))
NT = (((1,), (1,)), ((), ()))
TN = (((0,), (0,)), ((), ()))


def dot(a, b, dims=NN):
    return lax.dot_general(a, b, dims, preferred_element_type=f32)


def exact_dot(a, b, dims=NN):
    return lax.dot_general(a, b, dims, preferred_element_type=f32, precision=HIGHEST)


def halves(v):
    high = v.astype(bf16)
    return high, (v - high.astype(f32)).astype(bf16)


def split(v):
    return jnp.concatenate(halves(v), axis=0)


def mapped(weight_pair, pair):
    both = dot(weight_pair, pair)
    count = both.shape[0] // 2
    return both[:count] + both[count:]


def joined(both):
    count = both.shape[0] // 2
    return both[:count] + both[count:]


def wide(v):
    return jnp.concatenate([v, v], axis=1)


def folded(v):
    return v[:, :LANES] + v[:, LANES:]


def normalized(v):
    centre = v - jnp.sum(v, axis=0, keepdims=True) * (1.0 / D)
    rate = lax.rsqrt(jnp.sum(centre * centre, axis=0, keepdims=True) * (1.0 / D) + EPSILON)
    return centre * rate, rate


def norm_pullback(dn, unit, rate):
    mean = jnp.sum(dn, axis=0, keepdims=True) * (1.0 / D)
    slope = jnp.sum(dn * unit, axis=0, keepdims=True) * (1.0 / D)
    return rate * (dn - mean - unit * slope)


def lane_iota(shape, dim):
    return lax.broadcasted_iota(jnp.int32, shape, dim)


def lane_slot(lane):
    return (lane & 31) >> 2


def lane_row(lane):
    return ((lane >> 5) << 2) + (lane & 3)


def from_row_before(v, lane):
    near, far = pltpu.roll(v, 1, 1), pltpu.roll(v, 29, 1)
    return jnp.where((lane & 3) > 0, near, jnp.where(lane >= 32, far, 0.0))


def from_row_after(v, lane):
    near, far = pltpu.roll(v, LANES - 1, 1), pltpu.roll(v, LANES - 29, 1)
    return jnp.where((lane & 3) < 3, near, jnp.where(lane < 96, far, 0.0))


def tile_at(j):
    return pl.ds(pl.multiple_of(j * TILE, TILE), TILE)


def lanes_at(j):
    return pl.ds(pl.multiple_of(j * LANES, LANES), LANES)


def loop(count, body, unroll=1):
    def step(index, carry):
        body(index)
        return carry

    lax.fori_loop(0, count, step, 0, unroll=unroll)


def prepare_weights(r):
    def left_pair(dst, w):
        n, k = w.shape
        high, low = halves(w)
        dst[0:n, 0:k] = high
        dst[0:n, k : 2 * k] = high
        dst[n : 2 * n, 0:k] = low
        dst[n : 2 * n, k : 2 * k] = low

    for l in range(LAYERS):
        for name in ("first", "second", "mixer", "output", "expand"):
            w = getattr(r, name)[l]
            left_pair(getattr(r, name + "_t").at[l], jnp.transpose(w))
            left_pair(getattr(r, name + "_n").at[l], w)
        left_pair(r.reduce_t.at[l], r.reduce[l])
        left_pair(r.reduce_n.at[l], jnp.transpose(r.reduce[l]))
        r.rows[...] = jnp.zeros((PARAM_ROWS, LANES), f32)
        r.rows[0:4, 0:D] = r.gains[l]
        r.rows[4:16, 0:D] = r.biases[:, l]
        r.rows[16:25, 0:D] = r.depth[:, l]
        r.rows[25:29, 0:D] = r.spread[l]
        for t in range(3):
            r.rows[29 + t : 30 + t, :] = r.ebias[l : l + 1, t * LANES : (t + 1) * LANES]
        columns = jnp.transpose(r.rows[...])
        for k in range(29):
            r.par[l, k] = jnp.broadcast_to(columns[0:D, k : k + 1], (D, LANES))
        for t in range(3):
            r.epar[l, t * LANES : (t + 1) * LANES] = jnp.broadcast_to(
                columns[:, 29 + t : 30 + t], (LANES, LANES)
            )
        lane = lane_iota((D, LANES), 1)
        for b in range(2):
            r.taps[l, b] = jnp.where((lane & 1) == 0, r.par[l, 25 + b], r.par[l, 27 + b])
    r.acc[...] = jnp.zeros_like(r.acc)
    r.eacc[...] = jnp.zeros_like(r.eacc)


def prepare_masks(r, first_slot):
    lane = lane_iota((8, LANES), 1)
    slot_ids = jnp.zeros((8, 1024), jnp.int32)
    slot_row = lane_iota((8, 1024), 0)
    batch = jnp.zeros((8, LANES), jnp.int32)
    for s in range(8):
        slot_ids = jnp.where(slot_row == s, r.slot_image[first_slot + s], slot_ids)
        batch = jnp.where(lane_slot(lane) == s, r.slot_batch[first_slot + s], batch)
    chosen = (slot_ids == lane_iota((8, 1024), 1)).astype(f32).astype(bf16)
    sizes = jnp.concatenate([r.sizes[...].astype(f32), jnp.zeros((6, 1024), f32)], axis=0).astype(bf16)
    by_slot = dot(sizes, chosen, NT).astype(bf16)
    per_lane = dot(by_slot, (lane_slot(lane) == lane_iota((8, LANES), 0)).astype(f32).astype(bf16))
    height = jnp.broadcast_to(per_lane[0:1], (8, LANES))
    width = jnp.broadcast_to(per_lane[1:2], (8, LANES))
    rows_in = lane_row(lane).astype(f32) < height
    for x in range(SIDE):
        r.mask[:, x * LANES : (x + 1) * LANES] = (rows_in & (width > float(x))).astype(f32)
    r.counts[...] = jnp.where(rows_in, width, 0.0)
    micro = lane_iota((8, LANES), 0)
    r.onehot[0:8] = ((batch == micro) & (micro < MICRO)).astype(f32)
    r.onehot[8:16] = ((batch == micro - MICRO) & (micro >= MICRO)).astype(f32)
    place = lane_iota((8, DELEGATES), 1)
    of_slot = (place >> 6) == lane_iota((8, DELEGATES), 0)
    per_delegate = dot(by_slot, of_slot.astype(f32).astype(bf16))
    inside = (
        (2 * (place & 7)).astype(f32) < jnp.broadcast_to(per_delegate[0:1], (8, DELEGATES))
    ) & ((2 * ((place >> 3) & 7)).astype(f32) < jnp.broadcast_to(per_delegate[1:2], (8, DELEGATES)))
    inside = inside.astype(f32)
    key, query = lane_iota((LANES, LANES), 0), lane_iota((LANES, LANES), 1)
    for p in range(4):
        column = jnp.transpose(inside[:, p * LANES : (p + 1) * LANES])[:, 0:1]
        r.keep[p] = jnp.where((key >> 6) == (query >> 6), jnp.broadcast_to(column, (LANES, LANES)), 0.0)
    lane, place = lane_iota((LANES, DELEGATES), 0), lane_iota((LANES, DELEGATES), 1)
    same = ((place >> 6) == lane_slot(lane)) & ((place & 7) == (lane_row(lane) >> 1))
    for j in range(8):
        r.pool[j * LANES : (j + 1) * LANES] = (
            (same & (((place >> 3) & 7) == j)).astype(f32).astype(bf16)
        )


def take_rows(block, dst, mask):
    for k in range(12):
        at = slice(k * LANES, (k + 1) * LANES)
        rows = jnp.concatenate([block[z, :, :, at].reshape(32, LANES) for z in range(4)], axis=0)
        turned = jnp.transpose(rows)
        for x in range(SIDE):
            lo, hi = max(k * LANES, x * D), min((k + 1) * LANES, (x + 1) * D)
            if lo < hi:
                part = turned[lo - k * LANES : hi - k * LANES]
                dst[lo - x * D : hi - x * D, x * LANES : (x + 1) * LANES] = (
                    part * mask[0:1, x * LANES : (x + 1) * LANES]
                )


def give_rows(src, block):
    for k in range(12):
        parts = []
        for x in range(SIDE):
            lo, hi = max(k * LANES, x * D), min((k + 1) * LANES, (x + 1) * D)
            if lo < hi:
                parts.append(src[lo - x * D : hi - x * D, x * LANES : (x + 1) * LANES])
        turned = jnp.transpose(jnp.concatenate(parts, axis=0))
        for z in range(4):
            block[z, :, :, k * LANES : (k + 1) * LANES] = turned[z * 32 : (z + 1) * 32].reshape(8, 4, LANES)


def lane_sums(upper, lower, r):
    return exact_dot(r.onehot[0:8], upper, NT) + exact_dot(r.onehot[8:16], lower, NT)


def statistics_partial(r):
    total = jnp.concatenate([r.sums[0], r.counts[...], jnp.zeros((24, LANES), f32)], axis=0)
    square = jnp.concatenate([r.sums[1], jnp.zeros((32, LANES), f32)], axis=0)
    return lane_sums(total, square, r)


def per_lane(upper, lower, r):
    turned = jnp.transpose(jnp.concatenate([upper, lower], axis=0))
    return exact_dot(turned, r.onehot[0:8])[0:D], exact_dot(turned, r.onehot[8:16])[0:D]


def use_statistics(r, l, totals):
    count = totals[0:4, D : D + 1]
    centre = totals[0:4] / count
    variance = totals[4:8] / count - centre * centre
    rate = lax.rsqrt(variance + EPSILON)
    r.stat_rows[l, 0:4] = centre
    r.stat_rows[l, 4:8] = rate
    r.count_rows[...] = jnp.broadcast_to(count, (4, LANES))
    centre_lanes, rate_lanes = per_lane(centre, rate, r)
    r.centre[l] = centre_lanes
    r.rate[l] = rate_lanes


def use_statistics_grad(r, l, totals):
    centre, rate = r.stat_rows[l, 0:4], r.stat_rows[l, 4:8]
    count = r.count_rows[...]
    gain = jnp.concatenate([r.gains[l, 0:1], jnp.zeros((1, LANES - D), f32)], axis=1)
    dcentre = -rate * gain * totals[0:4]
    dvariance = -0.5 * rate * rate * rate * gain * totals[4:8]
    dsums = (dcentre - 2.0 * centre * dvariance) / count
    dsquares = dvariance / count
    r.dstat[0], r.dstat[1] = per_lane(dsums, 2.0 * dsquares, r)


def start_statistics(r):
    def body(j):
        v = r.x[0, :, tile_at(j)]
        r.sums[0] += folded(v)
        r.sums[1] += folded(v * v)

    r.sums[...] = jnp.zeros_like(r.sums)
    loop(8, body)


def forward_local(r, l):
    def first(j):
        v = r.x[l, :, tile_at(j)]
        normed = (v - wide(r.centre[l])) * wide(r.rate[l] * r.par[l, 0]) + wide(r.par[l, 4])
        pair = split(normed)
        r.n2[l, :, tile_at(j)] = pair
        out = mapped(r.first_t[l], pair) + wide(r.par[l, 5])
        r.fmap[l, :, pl.ds(pl.multiple_of(LANES + j * TILE, LANES), TILE)] = out * r.mask[0:1, tile_at(j)]

    r.fmap[l, :, 0:LANES] = jnp.zeros((D, LANES), f32)
    r.fmap[l, :, LANES + CELLS :] = jnp.zeros((D, LANES), f32)
    loop(8, first, 2)

    def conv(g):
        rows = pl.ds(pl.multiple_of(g * 8, 8), 8)
        lane = lane_iota((8, LANES), 1)
        taps = [r.par[l, 16 + t, rows, :] for t in range(9)]
        bias = r.par[l, 6, rows, :]
        cells = [r.fmap[l, rows, x * LANES : (x + 1) * LANES] for x in range(2)]
        for x in range(SIDE):
            cells.append(r.fmap[l, rows, (x + 2) * LANES : (x + 3) * LANES])
            sums = [sum(taps[3 * q + c] * cells[x + c] for c in range(3)) for q in range(3)]
            r.temp[rows, x * LANES : (x + 1) * LANES] = (
                bias + sums[1] + from_row_before(sums[0], lane) + from_row_after(sums[2], lane)
            )

    loop(12, conv)

    def second(j):
        pair = split(r.temp[:, tile_at(j)])
        r.d2[l, :, tile_at(j)] = pair
        out = mapped(r.second_t[l], pair) + wide(r.par[l, 7])
        local = r.x[l, :, tile_at(j)] + out * r.mask[0:1, tile_at(j)]
        r.local[:, tile_at(j)] = local
        unit, rate = normalized(local)
        r.unit1[l, :, tile_at(j)] = unit
        r.rates[l, 0:1, tile_at(j)] = rate
        r.pooled[:, lanes_at(j)] = split(
            0.25 * folded(unit * wide(r.par[l, 1]) + wide(r.par[l, 8]))
        )

    loop(8, second, 2)


def three_rows(v):
    high, low = halves(v)
    return jnp.concatenate([high, low, high], axis=0), jnp.concatenate([high, high, low], axis=0)


def three_columns(v):
    high, low = halves(v)
    return jnp.concatenate([high, low, high], axis=1), jnp.concatenate([high, high, low], axis=1)


HEAD = D // 2
SCALE = 1.0 / math.sqrt(HEAD)


def forward_mixer(r, l):
    delegates = joined(dot(r.pooled[...], r.pool[...]))
    pair = split(delegates)
    r.g2[l] = pair
    qkv = mapped(r.mixer_t[l], pair)
    queries, keys, values = qkv[0:D], qkv[D : 2 * D], qkv[2 * D :]
    for t in range(4):
        at = slice(t * LANES, (t + 1) * LANES)
        r.qkv[l, 0:D, at] = (queries[:, at] + r.par[l, 9]) * SCALE
        r.qkv[l, D : 2 * D, at] = keys[:, at]
        r.qkv[l, 2 * D :, at] = values[:, at] + r.par[l, 10]
    for p in range(4):
        for h in range(2):
            at = slice(p * LANES, (p + 1) * LANES)
            q, k, v = (r.qkv[l, part * D + h * HEAD : part * D + (h + 1) * HEAD, at] for part in range(3))
            scores = dot(three_rows(k)[0], three_rows(q)[1], TN)
            scores = jnp.where(r.keep[p] > 0.0, scores, MASKED_SCORE)
            weights = jnp.exp(scores - jnp.max(scores, axis=0, keepdims=True))
            probs = weights / jnp.sum(weights, axis=0, keepdims=True)
            r.probs[l, 2 * p + h] = probs
            r.mixture[h * HEAD : (h + 1) * HEAD, at] = dot(three_columns(v)[0], three_rows(probs)[1])
    r.mix2[...] = split(r.mixture[...])

    def spread(t):
        r.up[l, :, tile_at(t)] = joined(dot(r.mix2[...], r.pool[tile_at(t), :], NT))

    loop(4, spread)


def rest_forward(r, l, j):
    mask = r.mask[0:1, tile_at(j)]
    up = r.up[l, :, lanes_at(j)]
    spread = jnp.concatenate([up * r.taps[l, 0], up * r.taps[l, 1]], axis=1) + wide(r.par[l, 11])
    unit2, rate2 = normalized(spread)
    pair = split(unit2 * wide(r.par[l, 2]) + wide(r.par[l, 12]))
    r.s2[l, :, tile_at(j)] = pair
    middle = r.local[:, tile_at(j)] + mask * (mapped(r.output_t[l], pair) + wide(r.par[l, 13]))
    unit3, rate3 = normalized(middle)
    pair = split(unit3 * wide(r.par[l, 3]) + wide(r.par[l, 14]))
    r.e2[l, :, tile_at(j)] = pair
    before = mapped(r.expand_t[l], pair) + wide(r.epar[l])
    normal = 0.5 + 0.5 * lax.erf(before * math.sqrt(0.5))
    slope = normal + before * (jnp.exp(-0.5 * before * before) * (1.0 / math.sqrt(2.0 * math.pi)))
    hidden = split(before * normal)
    r.h2[l, :, tile_at(j)] = hidden
    out = middle + mask * (mapped(r.reduce_t[l], hidden) + wide(r.par[l, 15]))
    return out, unit2, rate2, unit3, rate3, slope


def rest_backward(r, l, j, dy, unit2, rate2, unit3, rate3, slope):
    def add(k, v):
        r.acc[l, k] += folded(v)

    pair = split(dy)
    r.dy2[:, tile_at(j)] = pair
    add(15, dy)
    dbefore = mapped(r.reduce_n[l], pair) * slope
    r.eacc[l] += folded(dbefore)
    pair = split(dbefore)
    r.dp2[:, tile_at(j)] = pair
    de = mapped(r.expand_n[l], pair)
    add(14, de)
    add(3, de * unit3)
    dmiddle = dy + norm_pullback(de * wide(r.par[l, 3]), unit3, rate3)
    r.local[:, tile_at(j)] = dmiddle
    add(13, dmiddle)
    pair = split(dmiddle)
    r.dm2[:, tile_at(j)] = pair
    ds = mapped(r.output_n[l], pair)
    add(12, ds)
    add(2, ds * unit2)
    dspread = norm_pullback(ds * wide(r.par[l, 2]), unit2, rate2)
    add(11, dspread)
    up = r.up[l, :, lanes_at(j)]
    r.acc[l, 25] += dspread[:, :LANES] * up
    r.acc[l, 26] += dspread[:, LANES:] * up
    r.pooled[:, lanes_at(j)] = split(
        dspread[:, :LANES] * r.taps[l, 0] + dspread[:, LANES:] * r.taps[l, 1]
    )


def forward_rest(r, l):
    def body(j):
        out, unit2, rate2, unit3, rate3, slope = rest_forward(r, l, j)
        r.unit2[:, tile_at(j)] = unit2
        r.unit3[:, tile_at(j)] = unit3
        r.rates2[0:1, tile_at(j)] = rate2
        r.rates2[1:2, tile_at(j)] = rate3
        r.slope[:, tile_at(j)] = slope
        r.x[l + 1, :, tile_at(j)] = out
        r.sums[0] += folded(out)
        r.sums[1] += folded(out * out)

    r.sums[...] = jnp.zeros_like(r.sums)
    loop(8, body)


def backward_rest(r, l):
    def body(j):
        rest_backward(
            r, l, j, r.dy[:, tile_at(j)], r.unit2[:, tile_at(j)], r.rates2[0:1, tile_at(j)],
            r.unit3[:, tile_at(j)], r.rates2[1:2, tile_at(j)], r.slope[:, tile_at(j)],
        )

    loop(8, body)


def turn_rest(r, l):
    def body(j):
        out, *kept = rest_forward(r, l, j)
        r.out[:, tile_at(j)] = out
        rest_backward(r, l, j, r.dy[:, tile_at(j)], *kept)

    loop(8, body)


def backward_mixer(r, l):
    r.mixture[...] = joined(dot(r.pooled[...], r.pool[...]))
    for p in range(4):
        for h in range(2):
            at = slice(p * LANES, (p + 1) * LANES)
            q, k, v = (r.qkv[l, part * D + h * HEAD : part * D + (h + 1) * HEAD, at] for part in range(3))
            dout = r.mixture[h * HEAD : (h + 1) * HEAD, at]
            probs = r.probs[l, 2 * p + h]
            dprobs = dot(three_rows(v)[0], three_rows(dout)[1], TN)
            dscores = probs * (dprobs - jnp.sum(probs * dprobs, axis=0, keepdims=True))
            probs_high, probs_low = halves(probs)
            probs_columns = jnp.concatenate([probs_high, probs_high, probs_low], axis=1)
            scores_high, scores_low = halves(dscores)
            scores_columns = jnp.concatenate([scores_high, scores_high, scores_low], axis=1)
            scores_rows = jnp.concatenate([scores_high, scores_high, scores_low], axis=0)
            dq = dot(three_columns(k)[0], scores_rows) * SCALE
            dk = dot(three_columns(q)[0], scores_columns, NT)
            dv = dot(three_columns(dout)[0], probs_columns, NT)
            for part, value in enumerate((dq, dk, dv)):
                r.dqkv[part * D + h * HEAD : part * D + (h + 1) * HEAD, at] = value
    dqkv = r.dqkv[...]
    for t in range(4):
        at = slice(t * LANES, (t + 1) * LANES)
        r.acc[l, 9] += dqkv[0:D, at]
        r.acc[l, 10] += dqkv[2 * D :, at]
    pair = split(dqkv)
    r.dq2[...] = pair
    r.mix2[...] = split(mapped(r.mixer_n[l], pair))

    def spread(t):
        r.dup[:, tile_at(t)] = 0.25 * joined(dot(r.mix2[...], r.pool[tile_at(t), :], NT))

    loop(4, spread)


def backward_local(r, l):
    def add(k, v):
        r.acc[l, k] += folded(v)

    def second(j):
        dup = wide(r.dup[:, lanes_at(j)])
        unit = r.unit1[l, :, tile_at(j)]
        add(8, dup)
        add(1, dup * unit)
        dlocal = r.local[:, tile_at(j)] + norm_pullback(
            dup * wide(r.par[l, 1]), unit, r.rates[l, 0:1, tile_at(j)]
        )
        r.local[:, tile_at(j)] = dlocal
        add(7, dlocal)
        pair = split(dlocal)
        r.dl2[:, tile_at(j)] = pair
        out = mapped(r.second_n[l], pair)
        add(6, out)
        r.dmap[:, pl.ds(pl.multiple_of(LANES + j * TILE, LANES), TILE)] = out

    r.dmap[:, 0:LANES] = jnp.zeros((D, LANES), f32)
    r.dmap[:, LANES + CELLS :] = jnp.zeros((D, LANES), f32)
    loop(8, second, 2)

    def conv(g):
        rows = pl.ds(pl.multiple_of(g * 8, 8), 8)
        lane = lane_iota((8, LANES), 1)
        taps = [r.par[l, 16 + t, rows, :] for t in range(9)]
        sums = [jnp.zeros((8, LANES), f32) for t in range(9)]

        def moved(place):
            v = r.dmap[rows, place * LANES : (place + 1) * LANES]
            return (from_row_after(v, lane), v, from_row_before(v, lane))

        zero = jnp.zeros((8, LANES), f32)
        window = [(zero, zero, zero), moved(1), None]
        for x in range(SIDE):
            window[2] = moved(x + 2) if x + 1 < SIDE else (zero, zero, zero)
            value = r.fmap[l, rows, (x + 1) * LANES : (x + 2) * LANES]
            out = zero
            for q in range(3):
                for c in range(3):
                    source = window[2 - c][q]
                    out = out + taps[3 * q + c] * source
                    sums[3 * q + c] = sums[3 * q + c] + source * value
            r.temp[rows, x * LANES : (x + 1) * LANES] = out
            window = [window[1], window[2], None]
        for t in range(9):
            r.acc[l, 16 + t, rows, :] = sums[t]

    loop(12, conv)

    def first(j):
        v = r.temp[:, tile_at(j)] * r.mask[0:1, tile_at(j)]
        add(5, v)
        pair = split(v)
        r.df2[:, tile_at(j)] = pair
        dnormed = mapped(r.first_n[l], pair)
        r.temp[:, tile_at(j)] = dnormed
        r.acc[l, 4] += folded(dnormed)
        r.acc[l, 0] += folded(dnormed * (r.x[l, :, tile_at(j)] - wide(r.centre[l])))

    loop(8, first, 2)


def statistics_grad_partial(r, l):
    pad = jnp.zeros((LANES - D, LANES), f32)
    return lane_sums(
        jnp.concatenate([r.acc[l, 4], pad], axis=0), jnp.concatenate([r.acc[l, 0], pad], axis=0), r
    )


def backward_input(r, l):
    def body(j):
        v = r.x[l, :, tile_at(j)]
        r.dy[:, tile_at(j)] = (
            r.temp[:, tile_at(j)] * wide(r.rate[l] * r.par[l, 0])
            + r.local[:, tile_at(j)]
            + r.mask[0:1, tile_at(j)] * (wide(r.dstat[0]) + v * wide(r.dstat[1]))
        )

    loop(8, body)


def weight_grads(r, l):
    def big(a, b, place):
        both = dot(a, b, NT)
        both = both[0:D] + both[D:]
        both = both[:, 0:FF] + both[:, FF:]
        for t in range(3):
            r.grads[l, place + t * D : place + (t + 1) * D] = both[:, t * LANES : (t + 1) * LANES]

    def small(a, b, place):
        both = dot(a, b, NT)
        both = both[0:D] + both[D:]
        r.grads[l, place : place + D, 0:D] = both[:, 0:D] + both[:, D:]

    big(r.e2[l], r.dp2[...], 0)
    big(r.dy2[...], r.h2[l], 288)
    small(r.n2[l], r.df2[...], 576)
    small(r.d2[l], r.dl2[...], 672)
    small(r.s2[l], r.dm2[...], 768)
    for t in range(3):
        part = jnp.concatenate(
            [r.dq2[t * D : (t + 1) * D], r.dq2[(3 + t) * D : (4 + t) * D]], axis=0
        )
        small(r.g2[l], part, 864 + t * D)

    r.acc[l, 0] = r.acc[l, 0] * r.rate[l]
    ones = jnp.ones((8, TILE), f32)
    even = ((lane_iota((8, TILE), 1) & 1) == 0).astype(f32)
    odd = (ones - even).astype(bf16)
    ones, even = ones.astype(bf16), even.astype(bf16)

    def row(kind, v, place, count):
        total = dot(kind, jnp.concatenate(halves(v), axis=1), NT)
        r.grads[l, 1152 + place : 1153 + place, 0:count] = total[0:1]

    for k in range(25):
        row(ones, r.acc[l, k], k, D)
    for b in range(2):
        row(even, r.acc[l, 25 + b], 25 + b, D)
        row(odd, r.acc[l, 25 + b], 27 + b, D)
    for t in range(3):
        row(ones, r.eacc[l, t * LANES : (t + 1) * LANES], 29 + t, LANES)


def scratch_list():
    L = LAYERS
    v = pltpu.VMEM
    return [
        ("first_t", v((L, 192, 192), bf16)),
        ("first_n", v((L, 192, 192), bf16)),
        ("second_t", v((L, 192, 192), bf16)),
        ("second_n", v((L, 192, 192), bf16)),
        ("mixer_t", v((L, 576, 192), bf16)),
        ("mixer_n", v((L, 192, 576), bf16)),
        ("output_t", v((L, 192, 192), bf16)),
        ("output_n", v((L, 192, 192), bf16)),
        ("expand_t", v((L, 768, 192), bf16)),
        ("expand_n", v((L, 192, 768), bf16)),
        ("reduce_t", v((L, 192, 768), bf16)),
        ("reduce_n", v((L, 768, 192), bf16)),
        ("rows", v((PARAM_ROWS, LANES), f32)),
        ("par", v((L, 29, D, LANES), f32)),
        ("epar", v((L, FF, LANES), f32)),
        ("taps", v((L, 2, D, LANES), f32)),
        ("acc", v((L, 27, D, LANES), f32)),
        ("eacc", v((L, FF, LANES), f32)),
        ("mask", v((8, CELLS), f32)),
        ("counts", v((8, LANES), f32)),
        ("onehot", v((16, LANES), f32)),
        ("keep", v((4, LANES, LANES), f32)),
        ("pool", v((8 * LANES, DELEGATES), bf16)),
        ("sums", v((2, D, LANES), f32)),
        ("stat_rows", v((L, 8, LANES), f32)),
        ("count_rows", v((4, LANES), f32)),
        ("centre", v((L, D, LANES), f32)),
        ("rate", v((L, D, LANES), f32)),
        ("dstat", v((2, D, LANES), f32)),
        ("x", v((L, D, CELLS), f32)),
        ("n2", v((L, 2 * D, CELLS), bf16)),
        ("fmap", v((L, D, CELLS + 2 * LANES), f32)),
        ("temp", v((D, CELLS), f32)),
        ("d2", v((L, 2 * D, CELLS), bf16)),
        ("local", v((D, CELLS), f32)),
        ("unit1", v((L, D, CELLS), f32)),
        ("rates", v((L, 1, CELLS), f32)),
        ("pooled", v((2 * D, 8 * LANES), bf16)),
        ("g2", v((L, 2 * D, DELEGATES), bf16)),
        ("qkv", v((L, 3 * D, DELEGATES), f32)),
        ("probs", v((L, 8, LANES, LANES), f32)),
        ("mixture", v((D, DELEGATES), f32)),
        ("mix2", v((2 * D, DELEGATES), bf16)),
        ("up", v((L, D, 8 * LANES), f32)),
        ("unit2", v((D, CELLS), f32)),
        ("s2", v((L, 2 * D, CELLS), bf16)),
        ("unit3", v((D, CELLS), f32)),
        ("rates2", v((8, CELLS), f32)),
        ("e2", v((L, 2 * D, CELLS), bf16)),
        ("slope", v((FF, CELLS), f32)),
        ("h2", v((L, 2 * FF, CELLS), bf16)),
        ("dy", v((D, CELLS), f32)),
        ("dy2", v((2 * D, CELLS), bf16)),
        ("dp2", v((2 * FF, CELLS), bf16)),
        ("out", v((D, CELLS), f32)),
        ("dm2", v((2 * D, CELLS), bf16)),
        ("dqkv", v((3 * D, DELEGATES), f32)),
        ("dq2", v((6 * D, DELEGATES), bf16)),
        ("dup", v((D, 8 * LANES), f32)),
        ("dl2", v((2 * D, CELLS), bf16)),
        ("dmap", v((D, CELLS + 2 * LANES), f32)),
        ("df2", v((2 * D, CELLS), bf16)),
        ("grads", v((L, GRAD_ROWS, LANES), f32)),
    ]


PARAMS = (
    "gains", "biases", "depth", "spread", "first", "second", "mixer", "output", "expand", "ebias", "reduce",
)

HALF = GRAD_ROWS // 2
PIECE = HALF // 16
OTHERS = 15
GROUP = 7


class Place:
    def __init__(self):
        dp = lax.axis_index("dp")
        self.z = lax.axis_index("segment")
        self.core = lax.rem(dp, 2)
        self.chip = lax.div(dp, 2)
        self.member = self.z * 2 + self.core

    def chip_after(self, d):
        return (self.z, lax.rem(self.chip + d, 16) * 2 + self.core)

    def member_after(self, d):
        member = lax.rem(self.member + d, 8)
        return (lax.div(member, 2), self.chip * 2 + lax.rem(member, 2))

    def z_after(self, d):
        return (lax.rem(self.z + d, 4), self.chip * 2 + self.core)

    def sibling(self):
        return (self.z, self.chip * 2 + 1 - self.core)


def remote(src, dst, sends, receives, index, device):
    return pltpu.make_async_remote_copy(
        src_ref=src,
        dst_ref=dst,
        send_sem=sends.at[index],
        recv_sem=receives.at[index],
        device_id=device,
        device_id_type=pl.DeviceIdType.MESH,
    )


def greet(me):
    barrier = pltpu.get_barrier_semaphore()
    for d in range(1, 16):
        pl.semaphore_signal(barrier, inc=1, device_id=me.chip_after(d), device_id_type=pl.DeviceIdType.MESH)
    for d in range(1, 8):
        pl.semaphore_signal(barrier, inc=1, device_id=me.member_after(d), device_id_type=pl.DeviceIdType.MESH)
    pl.semaphore_wait(barrier, OTHERS + GROUP)


class RowsIn:
    def __init__(self, r, me, src, dst, number):
        self.own = pltpu.make_async_copy(src.at[pl.ds(me.z * 8, 8)], dst.at[me.z], r.row_own.at[number])
        self.copies = [
            remote(
                src.at[pl.ds(lax.rem(me.z + d, 4) * 8, 8)], dst.at[me.z],
                r.row_send, r.row_recv, (number, d), me.z_after(d),
            )
            for d in range(1, 4)
        ]

    def start(self):
        for copy in self.copies:
            copy.start()
        self.own.start()

    def wait(self):
        self.own.wait()
        for copy in self.copies:
            copy.wait()


class RowsOut(RowsIn):
    def __init__(self, r, me, src, dst, number):
        slots = pl.ds(me.z * 8, 8)
        self.own = pltpu.make_async_copy(src.at[me.z], dst.at[slots], r.row_own.at[number])
        self.copies = [
            remote(
                src.at[lax.rem(me.z + d, 4)], dst.at[slots],
                r.row_send, r.row_recv, (number, d), me.z_after(d),
            )
            for d in range(1, 4)
        ]


class SmallSum:
    def __init__(self, r, me, number):
        self.r, self.me, self.number = r, me, number
        mine = r.chip_parts.at[number, me.chip]
        self.first = [
            remote(mine, mine, r.chip_send, r.chip_recv, (number, d), me.chip_after(d)) for d in range(1, 16)
        ]
        mine = r.group_parts.at[number, me.member]
        self.second = [
            remote(mine, mine, r.group_send, r.group_recv, (number, d), me.member_after(d))
            for d in range(1, 8)
        ]

    def start(self, value):
        self.r.chip_parts[self.number, self.me.chip] = value
        for copy in self.first:
            copy.start()

    def step(self):
        for copy in self.first:
            copy.wait()
        total = self.r.chip_parts[self.number, 0]
        for k in range(1, 16):
            total = total + self.r.chip_parts[self.number, k]
        self.r.group_parts[self.number, self.me.member] = total
        for copy in self.second:
            copy.start()

    def finish(self):
        for copy in self.second:
            copy.wait()
        total = self.r.group_parts[self.number, 0]
        for k in range(1, 8):
            total = total + self.r.group_parts[self.number, k]
        return total


class WeightSum:
    def __init__(self, r, me, l):
        self.r, self.me, self.l = r, me, l
        theirs = pl.ds(pl.multiple_of((1 - me.core) * HALF, 8), HALF)
        mine = pl.ds(pl.multiple_of(me.core * HALF, 8), HALF)
        self.mine = mine
        self.halves = remote(
            r.grads.at[l, theirs], r.half.at[l], r.half_send, r.half_recv, (l, 0), me.sibling()
        )

        def piece(chip):
            return pl.ds(pl.multiple_of(chip * PIECE, 8), PIECE)

        self.own_piece = piece(me.chip)
        self.pieces = [
            remote(
                r.half.at[l, piece(lax.rem(me.chip + d, 16))], r.pieces.at[l, me.chip],
                r.piece_send, r.piece_recv, (l, 0, d), me.chip_after(d),
            )
            for d in range(1, 16)
        ]
        self.planes = [
            remote(
                r.planes.at[l, me.z], r.planes.at[l, me.z], r.plane_send, r.plane_recv, (l, d), me.z_after(d)
            )
            for d in range(1, 4)
        ]
        self.place = pl.ds(pl.multiple_of(me.core * HALF + me.chip * PIECE, 8), PIECE)
        total = r.totals.at[l, self.place]
        self.gathers = [
            remote(total, total, r.piece_send, r.piece_recv, (l, 1, d), me.chip_after(d)) for d in range(1, 16)
        ]
        self.last = remote(
            r.totals.at[l, mine], r.totals.at[l, mine], r.half_send, r.half_recv, (l, 1), me.sibling()
        )

    def step(self, number):
        r, l, me = self.r, self.l, self.me
        if number == 0:
            self.halves.start()
        elif number == 1:
            self.halves.wait()
            r.half[l] = r.half[l] + r.grads[l, self.mine]
            r.pieces[l, me.chip] = r.half[l, self.own_piece]
            for copy in self.pieces:
                copy.start()
        elif number == 2:
            for copy in self.pieces:
                copy.wait()
            total = r.pieces[l, 0]
            for k in range(1, 16):
                total = total + r.pieces[l, k]
            r.planes[l, me.z] = total
            for copy in self.planes:
                copy.start()
        elif number == 3:
            for copy in self.planes:
                copy.wait()
            total = r.planes[l, 0]
            for k in range(1, 4):
                total = total + r.planes[l, k]
            r.totals[l, self.place] = total
            for copy in self.gathers:
                copy.start()
        elif number == 4:
            for copy in self.gathers:
                copy.wait()
            self.last.start()
        else:
            self.last.wait()


def comm_scratch():
    L = LAYERS
    v = pltpu.VMEM
    s = pltpu.SemaphoreType.DMA
    return [
        ("rows_in", v((2, 4, 8, 4, SIDE * D), f32)),
        ("rows_out", v((2, 4, 8, 4, SIDE * D), f32)),
        ("chip_parts", v((4, 16, 8, LANES), f32)),
        ("group_parts", v((4, 8, 8, LANES), f32)),
        ("half", v((L, HALF, LANES), f32)),
        ("pieces", v((L, 16, PIECE, LANES), f32)),
        ("planes", v((L, 4, PIECE, LANES), f32)),
        ("totals", v((L, GRAD_ROWS, LANES), f32)),
        ("row_own", s((4,))),
        ("row_send", s((4, 4))),
        ("row_recv", s((4, 4))),
        ("chip_send", s((4, 16))),
        ("chip_recv", s((4, 16))),
        ("group_send", s((4, 8))),
        ("group_recv", s((4, 8))),
        ("half_send", s((L, 2))),
        ("half_recv", s((L, 2))),
        ("piece_send", s((L, 2, 16))),
        ("piece_recv", s((L, 2, 16))),
        ("plane_send", s((L, 4))),
        ("plane_recv", s((L, 4))),
        ("out_sem", s((1,))),
    ]


def layers_kernel(names, *refs):
    r = SimpleNamespace(**dict(zip(names, refs)))
    me = Place()
    greet(me)
    tokens_in = RowsIn(r, me, r.tokens, r.rows_in.at[0], 0)
    upstream_in = RowsIn(r, me, r.cotangent, r.rows_in.at[1], 1)
    act_out = RowsOut(r, me, r.rows_out.at[0], r.act, 2)
    grad_out = RowsOut(r, me, r.rows_out.at[1], r.grad, 3)
    sums = [SmallSum(r, me, number) for number in range(4)]
    weights = [WeightSum(r, me, l) for l in range(LAYERS)]

    tokens_in.start()
    upstream_in.start()
    r.grads[...] = jnp.zeros_like(r.grads)
    prepare_weights(r)
    prepare_masks(r, me.z * 8)
    tokens_in.wait()
    take_rows(r.rows_in.at[0], r.x.at[0], r.mask)
    start_statistics(r)
    sums[0].start(statistics_partial(r))
    sums[0].step()
    use_statistics(r, 0, sums[0].finish())

    forward_local(r, 0)
    forward_mixer(r, 0)
    forward_rest(r, 0)
    sums[1].start(statistics_partial(r))
    sums[1].step()
    upstream_in.wait()
    take_rows(r.rows_in.at[1], r.dy, r.mask)
    use_statistics(r, 1, sums[1].finish())

    forward_local(r, 1)
    forward_mixer(r, 1)
    turn_rest(r, 1)
    give_rows(r.out, r.rows_out.at[0])
    act_out.start()
    backward_mixer(r, 1)
    backward_local(r, 1)
    sums[2].start(statistics_grad_partial(r, 1))
    sums[2].step()
    weight_grads(r, 1)
    weights[1].step(0)
    use_statistics_grad(r, 1, sums[2].finish())
    backward_input(r, 1)
    weights[1].step(1)

    backward_rest(r, 0)
    weights[1].step(2)
    backward_mixer(r, 0)
    weights[1].step(3)
    backward_local(r, 0)
    weights[1].step(4)
    sums[3].start(statistics_grad_partial(r, 0))
    sums[3].step()
    weight_grads(r, 0)
    weights[0].step(0)
    use_statistics_grad(r, 0, sums[3].finish())
    backward_input(r, 0)
    give_rows(r.dy, r.rows_out.at[1])
    grad_out.start()
    weights[1].step(5)
    for number in range(1, 6):
        weights[0].step(number)
    copy = pltpu.make_async_copy(r.totals, r.grad_sums, r.out_sem.at[0])
    copy.start()
    act_out.wait()
    grad_out.wait()
    copy.wait()


def unpack_kernel(totals, *outs):
    gains, biases, depth, spread, first, second, mixer, output, expand, ebias, reduce = outs
    for l in range(LAYERS):

        def rows(place, count, width=D):
            return totals[l, place : place + count, 0:width]

        gains[l] = rows(1152, 4)
        biases[:, l] = rows(1156, 12)
        depth[:, l] = rows(1168, 9)
        spread[l] = rows(1177, 4)
        first[l] = rows(576, D)
        second[l] = rows(672, D)
        output[l] = rows(768, D)
        for t in range(3):
            at = slice(t * LANES, (t + 1) * LANES)
            mixer[l, :, t * D : (t + 1) * D] = rows(864 + t * D, D)
            expand[l, :, at] = rows(t * D, D, LANES)
            reduce[l, :, at] = rows(288 + t * D, D, LANES)
            ebias[l : l + 1, at] = rows(1181 + t, 1, LANES)


def turned(params):
    gains, biases, depth, spread, *maps, ebias, reduce = params
    return (gains, jnp.swapaxes(biases, 0, 1), jnp.swapaxes(depth, 0, 1), spread, *maps, ebias,
            jnp.swapaxes(reduce, 1, 2))


def shards(tokens, cotangent, image_size, slot_image, slot_batch, *params):
    params = turned(params)
    scratch = scratch_list() + comm_scratch()
    ins = ("tokens", "cotangent", "sizes", "slot_image", "slot_batch") + PARAMS
    outs = ("act", "grad", "grad_sums")
    names = ins + outs + tuple(name for name, _ in scratch)
    anywhere = pl.BlockSpec(memory_space=pl.ANY)
    vmem = pl.BlockSpec(memory_space=pltpu.VMEM)
    smem = pl.BlockSpec(memory_space=pltpu.SMEM)
    act, grad, totals = pl.pallas_call(
        functools.partial(layers_kernel, names),
        out_shape=[
            jax.ShapeDtypeStruct(tokens.shape, f32),
            jax.ShapeDtypeStruct(tokens.shape, f32),
            jax.ShapeDtypeStruct((LAYERS, GRAD_ROWS, LANES), f32),
        ],
        in_specs=[anywhere, anywhere, vmem, smem, smem] + [vmem] * len(params),
        out_specs=[anywhere] * 3,
        scratch_shapes=[shape for _, shape in scratch],
        compiler_params=pltpu.CompilerParams(
            collective_id=0, has_side_effects=True, vmem_limit_bytes=63 * 2**20
        ),
        name="layers",
    )(tokens, cotangent, image_size.T, slot_image, slot_batch, *params)
    grads = pl.pallas_call(
        unpack_kernel,
        out_shape=[jax.ShapeDtypeStruct(p.shape, f32) for p in params],
        in_specs=[vmem],
        out_specs=[vmem] * len(params),
        compiler_params=pltpu.CompilerParams(vmem_limit_bytes=16 * 2**20),
        name="unpack",
    )(totals)
    return (act, grad) + turned(grads)


def solution(mesh):
    rows = P("dp", "segment", None)
    return jax.shard_map(
        shards,
        mesh=mesh,
        in_specs=(rows, rows, P(), P("dp"), P("dp")) + (P(),) * len(PARAMS),
        out_specs=(rows, rows) + (P(),) * len(PARAMS),
        check_vma=False,
    )
```

```python
import functools
import math
from types import SimpleNamespace

import jax
import jax.numpy as jnp
from jax import lax
from jax.experimental import pallas as pl
from jax.experimental.pallas import tpu as pltpu
from jax.sharding import PartitionSpec as P

D = 96
FF = 384
LAYERS = 2
MICRO = 4
SIDE = 16
EPSILON = 1e-05
MASKED_SCORE = -1000000000.0
LANES = 128
TILE = 256
CELLS = SIDE * LANES
DELEGATES = 512
PARAM_ROWS = 32
GRAD_ROWS = 1280
HIGHEST = lax.Precision.HIGHEST
f32 = jnp.float32
bf16 = jnp.bfloat16

NN = (((1,), (0,)), ((), ()))
NT = (((1,), (1,)), ((), ()))
TN = (((0,), (0,)), ((), ()))


def dot(a, b, dims=NN):
    return lax.dot_general(a, b, dims, preferred_element_type=f32)


def exact_dot(a, b, dims=NN):
    return lax.dot_general(a, b, dims, preferred_element_type=f32, precision=HIGHEST)


def halves(v):
    high = v.astype(bf16)
    return high, (v - high.astype(f32)).astype(bf16)


def split(v):
    return jnp.concatenate(halves(v), axis=0)


def mapped(weight_pair, pair):
    both = dot(weight_pair, pair)
    count = both.shape[0] // 2
    return both[:count] + both[count:]


def joined(both):
    count = both.shape[0] // 2
    return both[:count] + both[count:]


def wide(v):
    return jnp.concatenate([v, v], axis=1)


def folded(v):
    return v[:, :LANES] + v[:, LANES:]


def normalized(v):
    centre = v - jnp.sum(v, axis=0, keepdims=True) * (1.0 / D)
    rate = lax.rsqrt(jnp.sum(centre * centre, axis=0, keepdims=True) * (1.0 / D) + EPSILON)
    return centre * rate, rate


def norm_pullback(dn, unit, rate):
    mean = jnp.sum(dn, axis=0, keepdims=True) * (1.0 / D)
    slope = jnp.sum(dn * unit, axis=0, keepdims=True) * (1.0 / D)
    return rate * (dn - mean - unit * slope)


def lane_iota(shape, dim):
    return lax.broadcasted_iota(jnp.int32, shape, dim)


def lane_slot(lane):
    return lane >> 4


def lane_row(lane):
    return lane & 15


def from_row_before(v, lane):
    return jnp.where(lane_row(lane) > 0, pltpu.roll(v, 1, 1), 0.0)


def from_row_after(v, lane):
    return jnp.where(lane_row(lane) < 15, pltpu.roll(v, LANES - 1, 1), 0.0)


def tile_at(j):
    return pl.ds(pl.multiple_of(j * TILE, TILE), TILE)


def lanes_at(j):
    return pl.ds(pl.multiple_of(j * LANES, LANES), LANES)


def loop(count, body, unroll=1):
    def step(index, carry):
        body(index)
        return carry

    lax.fori_loop(0, count, step, 0, unroll=unroll)


def prepare_weights(r, l):
    def left_pair(dst, w):
        n, k = w.shape
        high, low = halves(w)
        dst[0:n, 0:k] = high
        dst[0:n, k : 2 * k] = high
        dst[n : 2 * n, 0:k] = low
        dst[n : 2 * n, k : 2 * k] = low

    for name in ("first", "second", "mixer", "output", "expand"):
        w = getattr(r, name)[l]
        left_pair(getattr(r, name + "_t").at[l], jnp.transpose(w))
        left_pair(getattr(r, name + "_n").at[l], w)
    left_pair(r.reduce_t.at[l], r.reduce[l])
    left_pair(r.reduce_n.at[l], jnp.transpose(r.reduce[l]))
    r.rows[...] = jnp.zeros((PARAM_ROWS, LANES), f32)
    r.rows[0:4, 0:D] = r.gains[l]
    r.rows[4:16, 0:D] = r.biases[:, l]
    r.rows[16:25, 0:D] = r.depth[:, l]
    r.rows[25:29, 0:D] = r.spread[l]
    for t in range(3):
        r.rows[29 + t : 30 + t, :] = r.ebias[l : l + 1, t * LANES : (t + 1) * LANES]
    columns = jnp.transpose(r.rows[...])
    for k in range(29):
        r.par[l, k] = jnp.broadcast_to(columns[0:D, k : k + 1], (D, LANES))
    for t in range(3):
        r.epar[l, t * LANES : (t + 1) * LANES] = jnp.broadcast_to(
            columns[:, 29 + t : 30 + t], (LANES, LANES)
        )
    lane = lane_iota((D, LANES), 1)
    for b in range(2):
        r.taps[l, b] = jnp.where((lane & 1) == 0, r.par[l, 25 + b], r.par[l, 27 + b])
    r.acc[l] = jnp.zeros((27, D, LANES), f32)
    r.eacc[l] = jnp.zeros((FF, LANES), f32)


def prepare_masks(r, z):
    lane = lane_iota((8, LANES), 1)
    slot_ids = jnp.zeros((32, LANES), jnp.int32)
    slot_row = lane_iota((32, LANES), 0)
    batch = jnp.zeros((8, LANES), jnp.int32)
    row_batch = jnp.zeros((8, LANES), jnp.int32)
    for s in range(32):
        slot_ids = jnp.where(slot_row == s, r.slot_image[s], slot_ids)
        row_batch = jnp.where((lane >> 2) == s, r.slot_batch[s], row_batch)
    for s in range(8):
        batch = jnp.where(lane_slot(lane) == s, r.slot_batch[z * 8 + s], batch)
    slot_ids = jnp.concatenate([slot_ids] * 8, axis=1)
    chosen = (slot_ids == lane_iota((32, 1024), 1)).astype(f32).astype(bf16)
    sizes = jnp.concatenate([r.sizes[...].astype(f32), jnp.zeros((6, 1024), f32)], axis=0).astype(bf16)
    by_slot = dot(sizes, chosen, NT).astype(bf16)

    def placed(slots, count):
        found = (slots == lane_iota((32, count), 0)).astype(f32).astype(bf16)
        per_place = dot(by_slot, found)
        return (jnp.broadcast_to(per_place[k : k + 1], (8, count)) for k in range(2))

    height, width = placed(lane_slot(lane_iota((32, LANES), 1)) + z * 8, LANES)
    rows_in = lane_row(lane).astype(f32) < height
    for x in range(SIDE):
        r.mask[:, x * LANES : (x + 1) * LANES] = (rows_in & (width > float(x))).astype(f32)
    r.counts[...] = jnp.where(rows_in, width, 0.0)
    row_height, row_width = placed(lane_iota((32, LANES), 1) >> 2, LANES)
    row_count = jnp.where(((lane & 3) + z * 4).astype(f32) < row_height, row_width, 0.0)
    r.row_limit[...] = jnp.broadcast_to(jnp.transpose(row_count)[:, 0:1] * float(D), (LANES, LANES))
    micro = lane_iota((8, LANES), 0)
    r.onehot[0:8] = ((batch == micro) & (micro < MICRO)).astype(f32)
    r.onehot[8:16] = ((batch == micro - MICRO) & (micro >= MICRO)).astype(f32)
    upper = ((row_batch == micro) & (micro < MICRO)).astype(f32)
    lower = ((row_batch == micro - MICRO) & (micro >= MICRO)).astype(f32)
    r.row_onehot[0:8] = upper
    r.row_onehot[8:16] = lower
    r.row_counts[...] = jnp.broadcast_to(jnp.sum(upper * row_count, axis=1, keepdims=True), (8, LANES))
    for k, kind in enumerate((upper, lower)):
        r.row_columns[k] = jnp.transpose(jnp.concatenate([kind] * 4, axis=0)).astype(bf16)
    place = lane_iota((8, DELEGATES), 1)
    height, width = placed((lane_iota((32, DELEGATES), 1) >> 6) + z * 8, DELEGATES)
    inside = ((2 * (place & 7)).astype(f32) < height) & ((2 * ((place >> 3) & 7)).astype(f32) < width)
    inside = inside.astype(f32)
    key, query = lane_iota((LANES, LANES), 0), lane_iota((LANES, LANES), 1)
    for p in range(4):
        column = jnp.transpose(inside[:, p * LANES : (p + 1) * LANES])[:, 0:1]
        r.keep[p] = jnp.where((key >> 6) == (query >> 6), jnp.broadcast_to(column, (LANES, LANES)), 0.0)
    lane, place = lane_iota((LANES, DELEGATES), 0), lane_iota((LANES, DELEGATES), 1)
    same = ((place >> 6) == lane_slot(lane)) & ((place & 7) == (lane_row(lane) >> 1))
    for j in range(8):
        r.pool[j * LANES : (j + 1) * LANES] = (
            (same & (((place >> 3) & 7) == j)).astype(f32).astype(bf16)
        )


def take_rows(block, dst, mask):
    for k in range(12):
        at = slice(k * LANES, (k + 1) * LANES)
        rows = jnp.concatenate([block[z, s, :, at] for s in range(8) for z in range(4)], axis=0)
        turned = jnp.transpose(rows)
        for x in range(SIDE):
            lo, hi = max(k * LANES, x * D), min((k + 1) * LANES, (x + 1) * D)
            if lo < hi:
                part = turned[lo - k * LANES : hi - k * LANES]
                dst[lo - x * D : hi - x * D, x * LANES : (x + 1) * LANES] = (
                    part * mask[0:1, x * LANES : (x + 1) * LANES]
                )


def give_rows(src, block):
    for k in range(12):
        parts = []
        for x in range(SIDE):
            lo, hi = max(k * LANES, x * D), min((k + 1) * LANES, (x + 1) * D)
            if lo < hi:
                parts.append(src[lo - x * D : hi - x * D, x * LANES : (x + 1) * LANES])
        turned = jnp.transpose(jnp.concatenate(parts, axis=0))
        for s in range(8):
            for z in range(4):
                place = 4 * (4 * s + z)
                block[z, s, :, k * LANES : (k + 1) * LANES] = turned[place : place + 4]


def lane_sums(upper, lower, r):
    return exact_dot(r.onehot[0:8], upper, NT) + exact_dot(r.onehot[8:16], lower, NT)


def three_parts(v):
    high, low = halves(v)
    rest = (v - high.astype(f32)) - low.astype(f32)
    return jnp.concatenate([high, low, rest.astype(bf16)], axis=0)


def row_mask(r, at):
    lane = lane_iota((LANES, TILE), 1).astype(f32) + float(at)
    return lane < wide(r.row_limit[...])


def row_statistics(r):
    upper = jnp.concatenate([r.row_onehot[0:8]] * 3, axis=1).astype(bf16)
    lower = jnp.concatenate([r.row_onehot[8:16]] * 3, axis=1).astype(bf16)
    for k in range(6):
        at = slice(k * TILE, (k + 1) * TILE)
        v = jnp.where(row_mask(r, k * TILE), r.own[:, :, at].reshape(LANES, TILE), 0.0)
        r.row_sums[:, at] = dot(upper, three_parts(v)) + dot(lower, three_parts(v * v))
    total = r.row_sums[:, 0:D]
    for x in range(1, SIDE):
        total = total + r.row_sums[:, x * D : (x + 1) * D]
    return jnp.concatenate([total, r.row_counts[:, 0 : LANES - D]], axis=1)


def corrected_rows(r, out):
    for x in range(SIDE):
        r.row_sums[:, x * D : (x + 1) * D] = r.dstat_rows[:, 0:D]
    zero = jnp.zeros((8, TILE), bf16)
    for k in range(6):
        at = slice(k * TILE, (k + 1) * TILE)
        parts = jnp.concatenate([three_parts(r.row_sums[:, at]), zero], axis=0)
        dsums, dsquares = dot(r.row_columns[0], parts), dot(r.row_columns[1], parts)
        v = r.arrived[:, :, at].reshape(LANES, TILE) + dsums + r.own[:, :, at].reshape(LANES, TILE) * dsquares
        out[:, :, at] = jnp.where(row_mask(r, k * TILE), v, 0.0).reshape(32, 4, TILE)


def statistics_partial(r):
    total = jnp.concatenate([r.sums[0], r.counts[...], jnp.zeros((24, LANES), f32)], axis=0)
    square = jnp.concatenate([r.sums[1], jnp.zeros((32, LANES), f32)], axis=0)
    return lane_sums(total, square, r)


def per_lane(upper, lower, r):
    turned = jnp.transpose(jnp.concatenate([upper, lower], axis=0))
    return exact_dot(turned, r.onehot[0:8])[0:D], exact_dot(turned, r.onehot[8:16])[0:D]


def use_statistics(r, l, totals):
    count = totals[0:4, D : D + 1]
    centre = totals[0:4] / count
    variance = totals[4:8] / count - centre * centre
    rate = lax.rsqrt(variance + EPSILON)
    r.stat_rows[l, 0:4] = centre
    r.stat_rows[l, 4:8] = rate
    r.count_rows[...] = jnp.broadcast_to(count, (4, LANES))
    centre_lanes, rate_lanes = per_lane(centre, rate, r)
    r.centre[l] = centre_lanes
    r.rate[l] = rate_lanes


def use_statistics_grad(r, l, totals):
    centre, rate = r.stat_rows[l, 0:4], r.stat_rows[l, 4:8]
    count = r.count_rows[...]
    gain = jnp.concatenate([r.gains[l, 0:1], jnp.zeros((1, LANES - D), f32)], axis=1)
    dcentre = -rate * gain * totals[0:4]
    dvariance = -0.5 * rate * rate * rate * gain * totals[4:8]
    dsums = (dcentre - 2.0 * centre * dvariance) / count
    dsquares = dvariance / count
    r.dstat_rows[0:4] = dsums
    r.dstat_rows[4:8] = 2.0 * dsquares
    if l > 0:
        r.dstat[0], r.dstat[1] = per_lane(dsums, 2.0 * dsquares, r)


def forward_first(r, l):
    def first(j):
        v = r.x[l, :, tile_at(j)]
        normed = (v - wide(r.centre[l])) * wide(r.rate[l] * r.par[l, 0]) + wide(r.par[l, 4])
        pair = split(normed)
        r.n2[l, :, tile_at(j)] = pair
        out = mapped(r.first_t[l], pair) + wide(r.par[l, 5])
        r.fmap[l, :, pl.ds(pl.multiple_of(LANES + j * TILE, LANES), TILE)] = out * r.mask[0:1, tile_at(j)]

    r.fmap[l, :, 0:LANES] = jnp.zeros((D, LANES), f32)
    r.fmap[l, :, LANES + CELLS :] = jnp.zeros((D, LANES), f32)
    loop(8, first, 2)


def forward_conv(r, l):
    def conv(g):
        rows = pl.ds(pl.multiple_of(g * 8, 8), 8)
        lane = lane_iota((8, LANES), 1)
        taps = [r.par[l, 16 + t, rows, :] for t in range(9)]
        bias = r.par[l, 6, rows, :]
        cells = [r.fmap[l, rows, x * LANES : (x + 1) * LANES] for x in range(2)]
        for x in range(SIDE):
            cells.append(r.fmap[l, rows, (x + 2) * LANES : (x + 3) * LANES])
            sums = [sum(taps[3 * q + c] * cells[x + c] for c in range(3)) for q in range(3)]
            r.temp[rows, x * LANES : (x + 1) * LANES] = (
                bias + sums[1] + from_row_before(sums[0], lane) + from_row_after(sums[2], lane)
            )

    loop(12, conv)


def forward_second(r, l):
    def second(j):
        pair = split(r.temp[:, tile_at(j)])
        r.d2[l, :, tile_at(j)] = pair
        out = mapped(r.second_t[l], pair) + wide(r.par[l, 7])
        local = r.x[l, :, tile_at(j)] + out * r.mask[0:1, tile_at(j)]
        r.local[:, tile_at(j)] = local
        unit, rate = normalized(local)
        r.unit1[l, :, tile_at(j)] = unit
        r.rates[l, 0:1, tile_at(j)] = rate
        r.pooled[:, lanes_at(j)] = split(
            0.25 * folded(unit * wide(r.par[l, 1]) + wide(r.par[l, 8]))
        )

    loop(8, second, 2)


def by_head(v):
    zero = jnp.zeros((HEAD, LANES), f32)
    return jnp.concatenate(
        [jnp.concatenate([v[0:HEAD], zero], axis=1), jnp.concatenate([zero, v[HEAD:]], axis=1)], axis=0
    )


def own_head(v):
    return jnp.concatenate([v[0:HEAD, 0:LANES], v[HEAD:, LANES:]], axis=0)


def left_rows(v):
    turned = jnp.transpose(jnp.concatenate([v, v], axis=0))
    return jnp.concatenate(halves(turned), axis=0)


def left_columns(v):
    high, low = halves(v)
    return jnp.concatenate(
        [jnp.concatenate([high, high], axis=1), jnp.concatenate([low, low], axis=1)], axis=0
    )


def column_product(a_pair, b_pair):
    both = joined(dot(a_pair, b_pair, NT))
    return folded(both)


HEAD = D // 2
SCALE = 1.0 / math.sqrt(HEAD)


def forward_local(r, l):
    forward_first(r, l)
    forward_conv(r, l)
    forward_second(r, l)


def forward_mixer(r, l):
    forward_queries(r, l)
    forward_attention(r, l)
    forward_spread(r, l)


def forward_queries(r, l):
    delegates = joined(dot(r.pooled[...], r.pool[...]))
    pair = split(delegates)
    r.g2[l] = pair
    qkv = mapped(r.mixer_t[l], pair)
    queries, keys, values = qkv[0:D], qkv[D : 2 * D], qkv[2 * D :]
    for t in range(4):
        at = slice(t * LANES, (t + 1) * LANES)
        r.qkv[l, 0:D, at] = (queries[:, at] + r.par[l, 9]) * SCALE
        r.qkv[l, D : 2 * D, at] = keys[:, at]
        r.qkv[l, 2 * D :, at] = values[:, at] + r.par[l, 10]


def forward_attention(r, l):
    for p in range(4):
        at = slice(p * LANES, (p + 1) * LANES)
        q, k, v = (r.qkv[l, part * D : (part + 1) * D, at] for part in range(3))
        scores = joined(dot(left_rows(k), split(by_head(q))))
        scores = jnp.where(wide(r.keep[p]) > 0.0, scores, MASKED_SCORE)
        weights = jnp.exp(scores - jnp.max(scores, axis=0, keepdims=True))
        probs = weights / jnp.sum(weights, axis=0, keepdims=True)
        r.probs[l, p] = probs
        r.mixture[:, at] = own_head(mapped(left_columns(v), split(probs)))


def forward_spread(r, l):
    r.mix2[...] = split(r.mixture[...])

    def spread(t):
        r.up[l, :, tile_at(t)] = joined(dot(r.mix2[...], r.pool[tile_at(t), :], NT))

    loop(4, spread)


def rest_forward(r, l, j):
    mask = r.mask[0:1, tile_at(j)]
    up = r.up[l, :, lanes_at(j)]
    spread = jnp.concatenate([up * r.taps[l, 0], up * r.taps[l, 1]], axis=1) + wide(r.par[l, 11])
    unit2, rate2 = normalized(spread)
    pair = split(unit2 * wide(r.par[l, 2]) + wide(r.par[l, 12]))
    r.s2[l, :, tile_at(j)] = pair
    middle = r.local[:, tile_at(j)] + mask * (mapped(r.output_t[l], pair) + wide(r.par[l, 13]))
    unit3, rate3 = normalized(middle)
    pair = split(unit3 * wide(r.par[l, 3]) + wide(r.par[l, 14]))
    r.e2[l, :, tile_at(j)] = pair
    before = mapped(r.expand_t[l], pair) + wide(r.epar[l])
    normal = 0.5 + 0.5 * lax.erf(before * math.sqrt(0.5))
    slope = normal + before * (jnp.exp(-0.5 * before * before) * (1.0 / math.sqrt(2.0 * math.pi)))
    hidden = split(before * normal)
    r.h2[l, :, tile_at(j)] = hidden
    out = middle + mask * (mapped(r.reduce_t[l], hidden) + wide(r.par[l, 15]))
    return out, unit2, rate2, unit3, rate3, slope


def rest_backward(r, l, j, dy, unit2, rate2, unit3, rate3, slope):
    def add(k, v):
        r.acc[l, k] += folded(v)

    pair = split(dy)
    r.dy2[:, tile_at(j)] = pair
    add(15, dy)
    dbefore = mapped(r.reduce_n[l], pair) * slope
    r.eacc[l] += folded(dbefore)
    pair = split(dbefore)
    r.dp2[:, tile_at(j)] = pair
    de = mapped(r.expand_n[l], pair)
    add(14, de)
    add(3, de * unit3)
    dmiddle = dy + norm_pullback(de * wide(r.par[l, 3]), unit3, rate3)
    r.local[:, tile_at(j)] = dmiddle
    add(13, dmiddle)
    pair = split(dmiddle)
    r.dm2[:, tile_at(j)] = pair
    ds = mapped(r.output_n[l], pair)
    add(12, ds)
    add(2, ds * unit2)
    dspread = norm_pullback(ds * wide(r.par[l, 2]), unit2, rate2)
    add(11, dspread)
    up = r.up[l, :, lanes_at(j)]
    r.acc[l, 25] += dspread[:, :LANES] * up
    r.acc[l, 26] += dspread[:, LANES:] * up
    r.pooled[:, lanes_at(j)] = split(
        dspread[:, :LANES] * r.taps[l, 0] + dspread[:, LANES:] * r.taps[l, 1]
    )


def forward_rest(r, l):
    def body(j):
        out, unit2, rate2, unit3, rate3, slope = rest_forward(r, l, j)
        r.unit2[:, tile_at(j)] = unit2
        r.unit3[:, tile_at(j)] = unit3
        r.rates2[0:1, tile_at(j)] = rate2
        r.rates2[1:2, tile_at(j)] = rate3
        r.slope[:, tile_at(j)] = slope
        r.x[l + 1, :, tile_at(j)] = out
        r.sums[0] += folded(out)
        r.sums[1] += folded(out * out)

    r.sums[...] = jnp.zeros_like(r.sums)
    loop(8, body, 2)


def backward_rest(r, l):
    def body(j):
        rest_backward(
            r, l, j, r.dy[:, tile_at(j)], r.unit2[:, tile_at(j)], r.rates2[0:1, tile_at(j)],
            r.unit3[:, tile_at(j)], r.rates2[1:2, tile_at(j)], r.slope[:, tile_at(j)],
        )

    loop(8, body, 2)


def turn_rest(r, l):
    def body(j):
        out, *kept = rest_forward(r, l, j)
        r.out[:, tile_at(j)] = out
        rest_backward(r, l, j, r.dy[:, tile_at(j)], *kept)

    loop(8, body, 2)


def backward_mixer(r, l):
    backward_gather(r, l)
    backward_attention(r, l)
    backward_queries(r, l)
    backward_spread(r, l)


def backward_gather(r, l):
    r.mixture[...] = joined(dot(r.pooled[...], r.pool[...]))


def backward_attention(r, l):
    for p in range(4):
        at = slice(p * LANES, (p + 1) * LANES)
        q, k, v = (r.qkv[l, part * D : (part + 1) * D, at] for part in range(3))
        probs = r.probs[l, p]
        dout = split(by_head(r.mixture[:, at]))
        dprobs = joined(dot(left_rows(v), dout))
        dscores = split(probs * (dprobs - jnp.sum(probs * dprobs, axis=0, keepdims=True)))
        r.dqkv[0:D, at] = own_head(mapped(left_columns(k), dscores)) * SCALE
        r.dqkv[D : 2 * D, at] = column_product(split(by_head(q)), dscores)
        r.dqkv[2 * D :, at] = column_product(dout, split(probs))


def backward_queries(r, l):
    dqkv = r.dqkv[...]
    for t in range(4):
        at = slice(t * LANES, (t + 1) * LANES)
        r.acc[l, 9] += dqkv[0:D, at]
        r.acc[l, 10] += dqkv[2 * D :, at]
    pair = split(dqkv)
    r.dq2[...] = pair
    r.mix2[...] = split(mapped(r.mixer_n[l], pair))


def backward_spread(r, l):
    def spread(t):
        r.dup[:, tile_at(t)] = 0.25 * joined(dot(r.mix2[...], r.pool[tile_at(t), :], NT))

    loop(4, spread)


def backward_local(r, l):
    backward_second(r, l)
    backward_conv(r, l)
    backward_first(r, l)


def backward_second(r, l):
    def add(k, v):
        r.acc[l, k] += folded(v)

    def second(j):
        dup = wide(r.dup[:, lanes_at(j)])
        unit = r.unit1[l, :, tile_at(j)]
        add(8, dup)
        add(1, dup * unit)
        dlocal = r.local[:, tile_at(j)] + norm_pullback(
            dup * wide(r.par[l, 1]), unit, r.rates[l, 0:1, tile_at(j)]
        )
        r.local[:, tile_at(j)] = dlocal
        add(7, dlocal)
        pair = split(dlocal)
        r.dl2[:, tile_at(j)] = pair
        out = mapped(r.second_n[l], pair)
        add(6, out)
        r.dmap[:, pl.ds(pl.multiple_of(LANES + j * TILE, LANES), TILE)] = out

    r.dmap[:, 0:LANES] = jnp.zeros((D, LANES), f32)
    r.dmap[:, LANES + CELLS :] = jnp.zeros((D, LANES), f32)
    loop(8, second, 2)


def backward_conv(r, l):
    def conv(g):
        rows = pl.ds(pl.multiple_of(g * 8, 8), 8)
        lane = lane_iota((8, LANES), 1)
        taps = [r.par[l, 16 + t, rows, :] for t in range(9)]
        sums = [jnp.zeros((8, LANES), f32) for t in range(9)]

        def moved(place):
            v = r.dmap[rows, place * LANES : (place + 1) * LANES]
            return (from_row_after(v, lane), v, from_row_before(v, lane))

        zero = jnp.zeros((8, LANES), f32)
        window = [(zero, zero, zero), moved(1), None]
        for x in range(SIDE):
            window[2] = moved(x + 2) if x + 1 < SIDE else (zero, zero, zero)
            value = r.fmap[l, rows, (x + 1) * LANES : (x + 2) * LANES]
            out = zero
            for q in range(3):
                for c in range(3):
                    source = window[2 - c][q]
                    out = out + taps[3 * q + c] * source
                    sums[3 * q + c] = sums[3 * q + c] + source * value
            r.temp[rows, x * LANES : (x + 1) * LANES] = out
            window = [window[1], window[2], None]
        for t in range(9):
            r.acc[l, 16 + t, rows, :] = sums[t]

    loop(12, conv)


def backward_first(r, l):
    def add(k, v):
        r.acc[l, k] += folded(v)

    def first(j):
        v = r.temp[:, tile_at(j)] * r.mask[0:1, tile_at(j)]
        add(5, v)
        pair = split(v)
        r.df2[:, tile_at(j)] = pair
        dnormed = mapped(r.first_n[l], pair)
        r.temp[:, tile_at(j)] = dnormed
        r.acc[l, 4] += folded(dnormed)
        r.acc[l, 0] += folded(dnormed * (r.x[l, :, tile_at(j)] - wide(r.centre[l])))

    loop(8, first, 2)


def statistics_grad_partial(r, l):
    pad = jnp.zeros((LANES - D, LANES), f32)
    return lane_sums(
        jnp.concatenate([r.acc[l, 4], pad], axis=0), jnp.concatenate([r.acc[l, 0], pad], axis=0), r
    )


def backward_input(r, l):
    def body(j):
        v = r.x[l, :, tile_at(j)]
        r.dy[:, tile_at(j)] = (
            r.temp[:, tile_at(j)] * wide(r.rate[l] * r.par[l, 0])
            + r.local[:, tile_at(j)]
            + r.mask[0:1, tile_at(j)] * (wide(r.dstat[0]) + v * wide(r.dstat[1]))
        )

    loop(8, body, 2)


def partial_input(r, l):
    def body(j):
        r.dy[:, tile_at(j)] = (
            r.temp[:, tile_at(j)] * wide(r.rate[l] * r.par[l, 0]) + r.local[:, tile_at(j)]
        )

    loop(8, body, 2)


def big_product(r, l, a, b, place):
    both = dot(a, b, NT)
    both = both[0:D] + both[D:]
    both = both[:, 0:FF] + both[:, FF:]
    for t in range(3):
        r.grads[l, place + t * D : place + (t + 1) * D] = both[:, t * LANES : (t + 1) * LANES]


def small_product(r, l, a, b, place):
    both = dot(a, b, NT)
    both = both[0:D] + both[D:]
    r.grads[l, place : place + D, 0:D] = both[:, 0:D] + both[:, D:]


def feed_forward_grads(r, l):
    big_product(r, l, r.e2[l], r.dp2[...], 0)
    big_product(r, l, r.dy2[...], r.h2[l], 288)


def mixer_grads(r, l):
    small_product(r, l, r.s2[l], r.dm2[...], 576)
    for t in range(3):
        part = jnp.concatenate(
            [r.dq2[t * D : (t + 1) * D], r.dq2[(3 + t) * D : (4 + t) * D]], axis=0
        )
        small_product(r, l, r.g2[l], part, 672 + t * D)


def local_grads(r, l):
    small_product(r, l, r.n2[l], r.df2[...], 1024)
    small_product(r, l, r.d2[l], r.dl2[...], 1120)


def vector_grads(r, l):
    r.acc[l, 0] = r.acc[l, 0] * r.rate[l]
    ones = jnp.ones((8, TILE), f32)
    even = ((lane_iota((8, TILE), 1) & 1) == 0).astype(f32)
    odd = (ones - even).astype(bf16)
    ones, even = ones.astype(bf16), even.astype(bf16)

    def row(kind, v, place, count):
        total = dot(kind, jnp.concatenate(halves(v), axis=1), NT)
        r.grads[l, 1216 + place : 1217 + place, 0:count] = total[0:1]

    for k in range(25):
        row(ones, r.acc[l, k], k, D)
    for b in range(2):
        row(even, r.acc[l, 25 + b], 25 + b, D)
        row(odd, r.acc[l, 25 + b], 27 + b, D)
    for t in range(3):
        row(ones, r.eacc[l, t * LANES : (t + 1) * LANES], 29 + t, LANES)


def weight_grads(r, l):
    feed_forward_grads(r, l)
    mixer_grads(r, l)
    local_grads(r, l)
    vector_grads(r, l)


def scratch_list():
    L = LAYERS
    v = pltpu.VMEM
    return [
        ("first_t", v((L, 192, 192), bf16)),
        ("first_n", v((L, 192, 192), bf16)),
        ("second_t", v((L, 192, 192), bf16)),
        ("second_n", v((L, 192, 192), bf16)),
        ("mixer_t", v((L, 576, 192), bf16)),
        ("mixer_n", v((L, 192, 576), bf16)),
        ("output_t", v((L, 192, 192), bf16)),
        ("output_n", v((L, 192, 192), bf16)),
        ("expand_t", v((L, 768, 192), bf16)),
        ("expand_n", v((L, 192, 768), bf16)),
        ("reduce_t", v((L, 192, 768), bf16)),
        ("reduce_n", v((L, 768, 192), bf16)),
        ("rows", v((PARAM_ROWS, LANES), f32)),
        ("par", v((L, 29, D, LANES), f32)),
        ("epar", v((L, FF, LANES), f32)),
        ("taps", v((L, 2, D, LANES), f32)),
        ("acc", v((L, 27, D, LANES), f32)),
        ("eacc", v((L, FF, LANES), f32)),
        ("mask", v((8, CELLS), f32)),
        ("counts", v((8, LANES), f32)),
        ("onehot", v((16, LANES), f32)),
        ("keep", v((4, LANES, LANES), f32)),
        ("pool", v((8 * LANES, DELEGATES), bf16)),
        ("sums", v((2, D, LANES), f32)),
        ("own", v((32, 4, SIDE * D), f32)),
        ("row_limit", v((LANES, LANES), f32)),
        ("row_onehot", v((16, LANES), f32)),
        ("row_counts", v((8, LANES), f32)),
        ("row_columns", v((2, LANES, 32), bf16)),
        ("row_sums", v((8, SIDE * D), f32)),
        ("dstat_rows", v((8, LANES), f32)),
        ("stat_rows", v((L, 8, LANES), f32)),
        ("count_rows", v((4, LANES), f32)),
        ("centre", v((L, D, LANES), f32)),
        ("rate", v((L, D, LANES), f32)),
        ("dstat", v((2, D, LANES), f32)),
        ("x", v((L, D, CELLS), f32)),
        ("n2", v((L, 2 * D, CELLS), bf16)),
        ("fmap", v((L, D, CELLS + 2 * LANES), f32)),
        ("temp", v((D, CELLS), f32)),
        ("d2", v((L, 2 * D, CELLS), bf16)),
        ("local", v((D, CELLS), f32)),
        ("unit1", v((L, D, CELLS), f32)),
        ("rates", v((L, 1, CELLS), f32)),
        ("pooled", v((2 * D, 8 * LANES), bf16)),
        ("g2", v((L, 2 * D, DELEGATES), bf16)),
        ("qkv", v((L, 3 * D, DELEGATES), f32)),
        ("probs", v((L, 4, LANES, TILE), f32)),
        ("mixture", v((D, DELEGATES), f32)),
        ("mix2", v((2 * D, DELEGATES), bf16)),
        ("up", v((L, D, 8 * LANES), f32)),
        ("unit2", v((D, CELLS), f32)),
        ("s2", v((L, 2 * D, CELLS), bf16)),
        ("unit3", v((D, CELLS), f32)),
        ("rates2", v((8, CELLS), f32)),
        ("e2", v((L, 2 * D, CELLS), bf16)),
        ("slope", v((FF, CELLS), f32)),
        ("h2", v((L, 2 * FF, CELLS), bf16)),
        ("dy", v((D, CELLS), f32)),
        ("dy2", v((2 * D, CELLS), bf16)),
        ("dp2", v((2 * FF, CELLS), bf16)),
        ("out", v((D, CELLS), f32)),
        ("dm2", v((2 * D, CELLS), bf16)),
        ("dqkv", v((3 * D, DELEGATES), f32)),
        ("dq2", v((6 * D, DELEGATES), bf16)),
        ("dup", v((D, 8 * LANES), f32)),
        ("dl2", v((2 * D, CELLS), bf16)),
        ("dmap", v((D, CELLS + 2 * LANES), f32)),
        ("df2", v((2 * D, CELLS), bf16)),
        ("grads", v((L, GRAD_ROWS, LANES), f32)),
    ]


PARAMS = (
    "gains", "biases", "depth", "spread", "first", "second", "mixer", "output", "expand", "ebias", "reduce",
)

OTHERS = 15
GROUP = 7
STEPS = sorted(
    [(x, y) for x in range(4) for y in range(4) if x + y > 0],
    key=lambda step: -min(step[0], 4 - step[0]) - min(step[1], 4 - step[1]),
)
PARCELS = ((0, 0, 1024), (0, 1024, 256), (1, 0, 1280))


class Place:
    def __init__(self):
        dp = lax.axis_index("dp")
        self.z = lax.axis_index("segment")
        self.core = lax.rem(dp, 2)
        self.chip = lax.div(dp, 2)
        self.member = self.z * 2 + self.core

    def chip_at(self, d):
        x, y = STEPS[d - 1]
        return lax.rem(lax.div(self.chip, 4) + x, 4) * 4 + lax.rem(lax.rem(self.chip, 4) + y, 4)

    def chip_after(self, d):
        return (self.z, self.chip_at(d) * 2 + self.core)

    def member_after(self, d):
        member = lax.rem(self.member + d, 8)
        return (lax.div(member, 2), self.chip * 2 + lax.rem(member, 2))

    def z_after(self, d):
        return (lax.rem(self.z + d, 4), self.chip * 2 + self.core)

    def sibling(self):
        return (self.z, self.chip * 2 + 1 - self.core)


def remote(src, dst, sends, receives, index, device):
    return pltpu.make_async_remote_copy(
        src_ref=src,
        dst_ref=dst,
        send_sem=sends.at[index],
        recv_sem=receives.at[index],
        device_id=device,
        device_id_type=pl.DeviceIdType.MESH,
    )


def greet(me):
    barrier = pltpu.get_barrier_semaphore()
    for d in range(1, 16):
        pl.semaphore_signal(barrier, inc=1, device_id=me.chip_after(d), device_id_type=pl.DeviceIdType.MESH)
    for d in range(1, 8):
        pl.semaphore_signal(barrier, inc=1, device_id=me.member_after(d), device_id_type=pl.DeviceIdType.MESH)
    return barrier


class RowsIn:
    def __init__(self, r, me, src, dst, number):
        self.own = pltpu.make_async_copy(src.at[pl.ds(me.z * 8, 8)], dst.at[me.z], r.row_own.at[number])
        self.copies = [
            remote(
                src.at[pl.ds(lax.rem(me.z + d, 4) * 8, 8)], dst.at[me.z],
                r.row_send, r.row_recv, (number, d), me.z_after(d),
            )
            for d in range(1, 4)
        ]

    def start(self):
        for copy in self.copies:
            copy.start()
        self.own.start()

    def wait(self):
        self.own.wait()
        for copy in self.copies:
            copy.wait()


class RowsOut(RowsIn):
    def __init__(self, r, me, src, dst, number, slots):
        self.own = pltpu.make_async_copy(src.at[me.z], dst.at[slots], r.row_own.at[number])
        self.copies = [
            remote(
                src.at[lax.rem(me.z + d, 4)], dst.at[slots],
                r.row_send, r.row_recv, (number, d), me.z_after(d),
            )
            for d in range(1, 4)
        ]


class SmallSum:
    def __init__(self, r, me, number):
        self.r, self.me, self.number = r, me, number
        mine = r.chip_parts.at[number, me.chip]
        self.first = [
            remote(mine, mine, r.chip_send, r.chip_recv, (number, d), me.chip_after(d)) for d in range(1, 16)
        ]
        mine = r.group_parts.at[number, me.member]
        self.second = [
            remote(mine, mine, r.group_send, r.group_recv, (number, d), me.member_after(d))
            for d in range(1, 8)
        ]

    def start(self, value):
        self.r.chip_parts[self.number, self.me.chip] = value
        for copy in self.first:
            copy.start()

    def step(self):
        for copy in self.first:
            copy.wait()
        total = self.r.chip_parts[self.number, 0]
        for k in range(1, 16):
            total = total + self.r.chip_parts[self.number, k]
        self.r.group_parts[self.number, self.me.member] = total
        for copy in self.second:
            copy.start()

    def finish(self):
        for copy in self.second:
            copy.wait()
        total = self.r.group_parts[self.number, 0]
        for k in range(1, 8):
            total = total + self.r.group_parts[self.number, k]
        return total


class WeightSum:
    def __init__(self, r, me, number):
        self.r, self.me, self.number = r, me, number
        layer, start, rows = PARCELS[number]
        count, size = rows // 2, rows // 32
        grads, totals = r.grads.at[layer], r.totals.at[layer]
        self.half, self.parts, self.planes = (
            getattr(r, kind + str(number)) for kind in ("half", "parts", "planes")
        )

        def half_of(core):
            return pl.ds(pl.multiple_of(start + core * count, 8), count)

        def piece_of(chip):
            return pl.ds(pl.multiple_of(chip * size, 8), size)

        self.mine = grads.at[half_of(me.core)]
        self.own_piece = self.half.at[piece_of(me.chip)]
        self.halves = remote(
            grads.at[half_of(1 - me.core)], self.half, r.half_send, r.half_recv, (number, 0), me.sibling()
        )
        self.pieces = [
            remote(
                self.half.at[piece_of(me.chip_at(d))], self.parts.at[me.chip],
                r.piece_send, r.piece_recv, (number, 0, d), me.chip_after(d),
            )
            for d in range(1, 16)
        ]
        plane = self.planes.at[me.z]
        self.exchange = [
            remote(plane, plane, r.plane_send, r.plane_recv, (number, d), me.z_after(d)) for d in range(1, 4)
        ]
        self.total = totals.at[pl.ds(pl.multiple_of(start + me.core * count + me.chip * size, 8), size)]
        self.gathers = [
            remote(self.total, self.total, r.piece_send, r.piece_recv, (number, 1, d), me.chip_after(d))
            for d in range(1, 16)
        ]
        whole = totals.at[half_of(me.core)]
        self.last = remote(whole, whole, r.half_send, r.half_recv, (number, 1), me.sibling())

    def step(self, number):
        me = self.me
        if number == 0:
            self.halves.start()
        elif number == 1:
            self.halves.wait()
            self.half[...] = self.half[...] + self.mine[...]
            self.parts[me.chip] = self.own_piece[...]
            for copy in self.pieces:
                copy.start()
        elif number == 2:
            for copy in self.pieces:
                copy.wait()
            total = self.parts[0]
            for k in range(1, 16):
                total = total + self.parts[k]
            self.planes[me.z] = total
            for copy in self.exchange:
                copy.start()
        elif number == 3:
            for copy in self.exchange:
                copy.wait()
            self.total[...] = (self.planes[0] + self.planes[1]) + (self.planes[2] + self.planes[3])
            for copy in self.gathers:
                copy.start()
        elif number == 4:
            for copy in self.gathers:
                copy.wait()
            self.last.start()
        else:
            self.last.wait()


def comm_scratch():
    L = LAYERS
    v = pltpu.VMEM
    s = pltpu.SemaphoreType.DMA
    return [
        ("rows_in", v((2, 4, 8, 4, SIDE * D), f32)),
        ("rows_out", v((4, 8, 4, SIDE * D), f32)),
        ("rows_back", v((4, 8, 4, SIDE * D), f32)),
        ("arrived", v((32, 4, SIDE * D), f32)),
        ("chip_parts", v((4, 16, 8, LANES), f32)),
        ("group_parts", v((4, 8, 8, LANES), f32)),
        ("totals", v((L, GRAD_ROWS, LANES), f32)),
        ("row_own", s((5,))),
        ("row_send", s((4, 4))),
        ("row_recv", s((4, 4))),
        ("chip_send", s((4, 16))),
        ("chip_recv", s((4, 16))),
        ("group_send", s((4, 8))),
        ("group_recv", s((4, 8))),
        ("half_send", s((len(PARCELS), 2))),
        ("half_recv", s((len(PARCELS), 2))),
        ("piece_send", s((len(PARCELS), 2, 16))),
        ("piece_recv", s((len(PARCELS), 2, 16))),
        ("plane_send", s((len(PARCELS), 4))),
        ("plane_recv", s((len(PARCELS), 4))),
        ("out_sem", s((2,))),
    ] + [
        (kind + str(number), v(lead + (rows // share, LANES), f32))
        for number, (_, _, rows) in enumerate(PARCELS)
        for kind, lead, share in (("half", (), 2), ("parts", (16,), 32), ("planes", (4,), 32))
    ]


def layers_kernel(names, *refs):
    r = SimpleNamespace(**dict(zip(names, refs)))
    me = Place()
    barrier = greet(me)
    own_rows = pltpu.make_async_copy(r.tokens, r.own, r.row_own.at[4])
    own_rows.start()
    mine = pl.ds(me.z * 8, 8)
    tokens_in = RowsIn(r, me, r.tokens, r.rows_in.at[0], 0)
    upstream_in = RowsIn(r, me, r.cotangent, r.rows_in.at[1], 1)
    act_out = RowsOut(r, me, r.rows_out, r.act, 2, mine)
    grad_out = RowsOut(r, me, r.rows_back, r.arrived, 3, mine)
    sums = [SmallSum(r, me, number) for number in range(4)]
    late, last, early = (WeightSum(r, me, number) for number in range(3))

    prepare_masks(r, me.z)
    own_rows.wait()
    pl.semaphore_wait(barrier, OTHERS + GROUP)
    tokens_in.start()
    sums[0].start(row_statistics(r))
    prepare_weights(r, 0)
    sums[0].step()
    r.grads[...] = jnp.zeros_like(r.grads)
    tokens_in.wait()
    upstream_in.start()
    take_rows(r.rows_in.at[0], r.x.at[0], r.mask)
    use_statistics(r, 0, sums[0].finish())

    forward_local(r, 0)
    forward_mixer(r, 0)
    forward_rest(r, 0)
    sums[1].start(statistics_partial(r))
    prepare_weights(r, 1)
    sums[1].step()
    upstream_in.wait()
    take_rows(r.rows_in.at[1], r.dy, r.mask)
    use_statistics(r, 1, sums[1].finish())

    forward_local(r, 1)
    forward_mixer(r, 1)
    turn_rest(r, 1)
    give_rows(r.out, r.rows_out)
    act_out.start()
    backward_mixer(r, 1)
    backward_local(r, 1)
    sums[2].start(statistics_grad_partial(r, 1))
    feed_forward_grads(r, 1)
    sums[2].step()
    mixer_grads(r, 1)
    local_grads(r, 1)
    vector_grads(r, 1)
    early.step(0)
    use_statistics_grad(r, 1, sums[2].finish())
    backward_input(r, 1)

    early.step(1)
    backward_rest(r, 0)
    early.step(2)
    backward_mixer(r, 0)
    early.step(3)
    feed_forward_grads(r, 0)
    mixer_grads(r, 0)
    late.step(0)
    backward_second(r, 0)
    late.step(1)
    backward_conv(r, 0)
    backward_first(r, 0)
    sums[3].start(statistics_grad_partial(r, 0))
    partial_input(r, 0)
    give_rows(r.dy, r.rows_back)
    grad_out.start()
    local_grads(r, 0)
    vector_grads(r, 0)
    last.step(0)
    late.step(2)
    sums[3].step()
    last.step(1)
    early.step(4)
    late.step(3)
    use_statistics_grad(r, 0, sums[3].finish())
    last.step(2)
    grad_out.wait()
    corrected_rows(r, r.own)
    copy = pltpu.make_async_copy(r.own, r.grad, r.out_sem.at[0])
    copy.start()
    late.step(4)
    last.step(3)
    early.step(5)
    late.step(5)
    last.step(4)
    act_out.wait()
    last.step(5)
    totals = pltpu.make_async_copy(r.totals, r.grad_sums, r.out_sem.at[1])
    totals.start()
    copy.wait()
    totals.wait()


def unpack_kernel(act_in, grad_in, totals, act, grad, *outs):
    refs, (act_sem, grad_sem) = outs[:-1], (outs[-1].at[0], outs[-1].at[1])
    copies = (pltpu.make_async_copy(act_in, act, act_sem), pltpu.make_async_copy(grad_in, grad, grad_sem))
    for copy in copies:
        copy.start()
    gains, biases, depth, spread, first, second, mixer, output, expand, ebias, reduce = refs
    for l in range(LAYERS):

        def rows(place, count, width=D):
            return totals[l, place : place + count, 0:width]

        gains[l] = rows(1216, 4)
        biases[:, l] = rows(1220, 12)
        depth[:, l] = rows(1232, 9)
        spread[l] = rows(1241, 4)
        first[l] = rows(1024, D)
        second[l] = rows(1120, D)
        output[l] = rows(576, D)
        for t in range(3):
            at = slice(t * LANES, (t + 1) * LANES)
            mixer[l, :, t * D : (t + 1) * D] = rows(672 + t * D, D)
            expand[l, :, at] = rows(t * D, D, LANES)
            reduce[l, :, at] = rows(288 + t * D, D, LANES)
            ebias[l : l + 1, at] = rows(1245 + t, 1, LANES)
    for copy in copies:
        copy.wait()


def turned(params):
    gains, biases, depth, spread, *maps, ebias, reduce = params
    return (gains, jnp.swapaxes(biases, 0, 1), jnp.swapaxes(depth, 0, 1), spread, *maps, ebias,
            jnp.swapaxes(reduce, 1, 2))


def shards(tokens, cotangent, image_size, slot_image, slot_batch, *params):
    params = turned(params)
    scratch = scratch_list() + comm_scratch()
    ins = ("tokens", "cotangent", "sizes", "slot_image", "slot_batch") + PARAMS
    outs = ("act", "grad", "grad_sums")
    names = ins + outs + tuple(name for name, _ in scratch)
    anywhere = pl.BlockSpec(memory_space=pl.ANY)
    vmem = pl.BlockSpec(memory_space=pltpu.VMEM)
    smem = pl.BlockSpec(memory_space=pltpu.SMEM)
    act, grad, totals = pl.pallas_call(
        functools.partial(layers_kernel, names),
        out_shape=[
            jax.ShapeDtypeStruct(tokens.shape, f32),
            jax.ShapeDtypeStruct(tokens.shape, f32),
            jax.ShapeDtypeStruct((LAYERS, GRAD_ROWS, LANES), f32),
        ],
        in_specs=[anywhere, anywhere, vmem, smem, smem] + [vmem] * len(params),
        out_specs=[anywhere] * 3,
        scratch_shapes=[shape for _, shape in scratch],
        compiler_params=pltpu.CompilerParams(
            collective_id=0, has_side_effects=True, vmem_limit_bytes=63 * 2**20
        ),
        name="layers",
    )(tokens, cotangent, image_size.T, slot_image, slot_batch, *params)
    act, grad, *grads = pl.pallas_call(
        unpack_kernel,
        out_shape=[jax.ShapeDtypeStruct(tokens.shape, f32)] * 2
        + [jax.ShapeDtypeStruct(p.shape, f32) for p in params],
        in_specs=[anywhere, anywhere, vmem],
        out_specs=[anywhere, anywhere] + [vmem] * len(params),
        scratch_shapes=[pltpu.SemaphoreType.DMA((2,))],
        compiler_params=pltpu.CompilerParams(vmem_limit_bytes=16 * 2**20),
        name="unpack",
    )(act, grad, totals)
    return (act, grad) + turned(grads)


def solution(mesh):
    rows = P("dp", "segment", None)
    return jax.shard_map(
        shards,
        mesh=mesh,
        in_specs=(rows, rows, P(), P("dp"), P("dp")) + (P(),) * len(PARAMS),
        out_specs=(rows, rows) + (P(),) * len(PARAMS),
        check_vma=False,
    )
```

```python
import functools
import math
from types import SimpleNamespace

import jax
import jax.numpy as jnp
from jax import lax
from jax.experimental import pallas as pl
from jax.experimental.pallas import tpu as pltpu
from jax.sharding import PartitionSpec as P

D = 96
FF = 384
LAYERS = 2
MICRO = 4
SIDE = 16
EPSILON = 1e-05
MASKED_SCORE = -1000000000.0
LANES = 128
TILE = 256
CELLS = SIDE * LANES
DELEGATES = 512
PARAM_ROWS = 32
GRAD_ROWS = 1280
HIGHEST = lax.Precision.HIGHEST
f32 = jnp.float32
bf16 = jnp.bfloat16

NN = (((1,), (0,)), ((), ()))
NT = (((1,), (1,)), ((), ()))
TN = (((0,), (0,)), ((), ()))


def dot(a, b, dims=NN):
    return lax.dot_general(a, b, dims, preferred_element_type=f32)


def exact_dot(a, b, dims=NN):
    return lax.dot_general(a, b, dims, preferred_element_type=f32, precision=HIGHEST)


def halves(v):
    high = v.astype(bf16)
    return high, (v - high.astype(f32)).astype(bf16)


def split(v):
    return jnp.concatenate(halves(v), axis=0)


def mapped(weight_pair, pair):
    both = dot(weight_pair, pair)
    count = both.shape[0] // 2
    return both[:count] + both[count:]


def joined(both):
    count = both.shape[0] // 2
    return both[:count] + both[count:]


def wide(v):
    return jnp.concatenate([v, v], axis=1)


def folded(v):
    return v[:, :LANES] + v[:, LANES:]


def normalized(v):
    centre = v - jnp.sum(v, axis=0, keepdims=True) * (1.0 / D)
    rate = lax.rsqrt(jnp.sum(centre * centre, axis=0, keepdims=True) * (1.0 / D) + EPSILON)
    return centre * rate, rate


def norm_pullback(dn, unit, rate):
    mean = jnp.sum(dn, axis=0, keepdims=True) * (1.0 / D)
    slope = jnp.sum(dn * unit, axis=0, keepdims=True) * (1.0 / D)
    return rate * (dn - mean - unit * slope)


def lane_iota(shape, dim):
    return lax.broadcasted_iota(jnp.int32, shape, dim)


def lane_slot(lane):
    return lane >> 4


def lane_row(lane):
    return lane & 15


def from_row_before(v, lane):
    return jnp.where(lane_row(lane) > 0, pltpu.roll(v, 1, 1), 0.0)


def from_row_after(v, lane):
    return jnp.where(lane_row(lane) < 15, pltpu.roll(v, LANES - 1, 1), 0.0)


def tile_at(j):
    return slice(j * TILE, (j + 1) * TILE)


def padded_tile_at(j):
    return slice(LANES + j * TILE, LANES + (j + 1) * TILE)


def lanes_at(j):
    return slice(j * LANES, (j + 1) * LANES)


def loop(count, body):
    for index in range(count):
        body(index)


def staggered(count, body, gap=1):
    running, index, step = [], 0, 0
    while index < count or running:
        if index < count and step % gap == 0:
            running.append(body(index))
            index += 1
        running = [part for part in running if next(part, "end") != "end"]
        step += 1


def prepare_weights(r, l):
    def left_pair(dst, w):
        n, k = w.shape
        high, low = halves(w)
        dst[0:n, 0:k] = high
        dst[0:n, k : 2 * k] = high
        dst[n : 2 * n, 0:k] = low
        dst[n : 2 * n, k : 2 * k] = low

    for name in ("first", "second", "mixer", "output", "expand"):
        w = getattr(r, name)[l]
        left_pair(getattr(r, name + "_t").at[l], jnp.transpose(w))
        left_pair(getattr(r, name + "_n").at[l], w)
    left_pair(r.reduce_t.at[l], r.reduce[l])
    left_pair(r.reduce_n.at[l], jnp.transpose(r.reduce[l]))
    r.rows[...] = jnp.zeros((PARAM_ROWS, LANES), f32)
    r.rows[0:4, 0:D] = r.gains[l]
    r.rows[4:16, 0:D] = r.biases[:, l]
    r.rows[16:25, 0:D] = r.depth[:, l]
    r.rows[25:29, 0:D] = r.spread[l]
    for t in range(3):
        r.rows[29 + t : 30 + t, :] = r.ebias[l : l + 1, t * LANES : (t + 1) * LANES]
    columns = jnp.transpose(r.rows[...])
    for k in range(29):
        r.par[l, k] = jnp.broadcast_to(columns[0:D, k : k + 1], (D, LANES))
    for t in range(3):
        r.epar[l, t * LANES : (t + 1) * LANES] = jnp.broadcast_to(
            columns[:, 29 + t : 30 + t], (LANES, LANES)
        )
    lane = lane_iota((D, LANES), 1)
    for b in range(2):
        r.taps[l, b] = jnp.where((lane & 1) == 0, r.par[l, 25 + b], r.par[l, 27 + b])
    r.acc[l] = jnp.zeros((27, D, LANES), f32)
    r.eacc[l] = jnp.zeros((FF, LANES), f32)


def prepare_masks(r, z):
    lane = lane_iota((8, LANES), 1)
    slot_ids = jnp.zeros((32, LANES), jnp.int32)
    slot_row = lane_iota((32, LANES), 0)
    batch = jnp.zeros((8, LANES), jnp.int32)
    row_batch = jnp.zeros((8, LANES), jnp.int32)
    for s in range(32):
        slot_ids = jnp.where(slot_row == s, r.slot_image[s], slot_ids)
        row_batch = jnp.where((lane >> 2) == s, r.slot_batch[s], row_batch)
    for s in range(8):
        batch = jnp.where(lane_slot(lane) == s, r.slot_batch[z * 8 + s], batch)
    slot_ids = jnp.concatenate([slot_ids] * 8, axis=1)
    chosen = (slot_ids == lane_iota((32, 1024), 1)).astype(f32).astype(bf16)
    sizes = jnp.concatenate([r.sizes[...].astype(f32), jnp.zeros((6, 1024), f32)], axis=0).astype(bf16)
    by_slot = dot(sizes, chosen, NT).astype(bf16)

    def placed(slots, count):
        found = (slots == lane_iota((32, count), 0)).astype(f32).astype(bf16)
        per_place = dot(by_slot, found)
        return (jnp.broadcast_to(per_place[k : k + 1], (8, count)) for k in range(2))

    height, width = placed(lane_slot(lane_iota((32, LANES), 1)) + z * 8, LANES)
    rows_in = lane_row(lane).astype(f32) < height
    for x in range(SIDE):
        r.mask[:, x * LANES : (x + 1) * LANES] = (rows_in & (width > float(x))).astype(f32)
    r.counts[...] = jnp.where(rows_in, width, 0.0)
    row_height, row_width = placed(lane_iota((32, LANES), 1) >> 2, LANES)
    row_count = jnp.where(((lane & 3) + z * 4).astype(f32) < row_height, row_width, 0.0)
    r.row_limit[...] = jnp.broadcast_to(jnp.transpose(row_count)[:, 0:1] * float(D), (LANES, LANES))
    micro = lane_iota((8, LANES), 0)
    r.onehot[0:8] = ((batch == micro) & (micro < MICRO)).astype(f32)
    r.onehot[8:16] = ((batch == micro - MICRO) & (micro >= MICRO)).astype(f32)
    upper = ((row_batch == micro) & (micro < MICRO)).astype(f32)
    lower = ((row_batch == micro - MICRO) & (micro >= MICRO)).astype(f32)
    r.row_onehot[0:8] = upper
    r.row_onehot[8:16] = lower
    r.row_counts[...] = jnp.broadcast_to(jnp.sum(upper * row_count, axis=1, keepdims=True), (8, LANES))
    for k, kind in enumerate((upper, lower)):
        r.row_columns[k] = jnp.transpose(jnp.concatenate([kind] * 4, axis=0)).astype(bf16)
    place = lane_iota((8, DELEGATES), 1)
    height, width = placed((lane_iota((32, DELEGATES), 1) >> 6) + z * 8, DELEGATES)
    inside = ((2 * (place & 7)).astype(f32) < height) & ((2 * ((place >> 3) & 7)).astype(f32) < width)
    inside = inside.astype(f32)
    key, query = lane_iota((LANES, LANES), 0), lane_iota((LANES, LANES), 1)
    for p in range(4):
        column = jnp.transpose(inside[:, p * LANES : (p + 1) * LANES])[:, 0:1]
        r.keep[p] = jnp.where((key >> 6) == (query >> 6), jnp.broadcast_to(column, (LANES, LANES)), 0.0)
    lane, place = lane_iota((LANES, DELEGATES), 0), lane_iota((LANES, DELEGATES), 1)
    same = ((place >> 6) == lane_slot(lane)) & ((place & 7) == (lane_row(lane) >> 1))
    for j in range(8):
        r.pool[j * LANES : (j + 1) * LANES] = (
            (same & (((place >> 3) & 7) == j)).astype(f32).astype(bf16)
        )


def take_rows(block, dst, mask):
    for k in range(12):
        at = slice(k * LANES, (k + 1) * LANES)
        rows = jnp.concatenate([block[z, s, :, at] for s in range(8) for z in range(4)], axis=0)
        turned = jnp.transpose(rows)
        for x in range(SIDE):
            lo, hi = max(k * LANES, x * D), min((k + 1) * LANES, (x + 1) * D)
            if lo < hi:
                part = turned[lo - k * LANES : hi - k * LANES]
                dst[lo - x * D : hi - x * D, x * LANES : (x + 1) * LANES] = (
                    part * mask[0:1, x * LANES : (x + 1) * LANES]
                )


def give_rows(src, block):
    for k in range(12):
        parts = []
        for x in range(SIDE):
            lo, hi = max(k * LANES, x * D), min((k + 1) * LANES, (x + 1) * D)
            if lo < hi:
                parts.append(src[lo - x * D : hi - x * D, x * LANES : (x + 1) * LANES])
        turned = jnp.transpose(jnp.concatenate(parts, axis=0))
        for s in range(8):
            for z in range(4):
                place = 4 * (4 * s + z)
                block[z, s, :, k * LANES : (k + 1) * LANES] = turned[place : place + 4]


def lane_sums(upper, lower, r):
    return exact_dot(r.onehot[0:8], upper, NT) + exact_dot(r.onehot[8:16], lower, NT)


def three_parts(v):
    high, low = halves(v)
    rest = (v - high.astype(f32)) - low.astype(f32)
    return jnp.concatenate([high, low, rest.astype(bf16)], axis=0)


def row_mask(r, at):
    lane = lane_iota((LANES, TILE), 1).astype(f32) + float(at)
    return lane < wide(r.row_limit[...])


def row_statistics(r):
    upper = jnp.concatenate([r.row_onehot[0:8]] * 3, axis=1).astype(bf16)
    lower = jnp.concatenate([r.row_onehot[8:16]] * 3, axis=1).astype(bf16)
    for k in range(6):
        at = slice(k * TILE, (k + 1) * TILE)
        v = jnp.where(row_mask(r, k * TILE), r.own[:, :, at].reshape(LANES, TILE), 0.0)
        r.row_sums[:, at] = dot(upper, three_parts(v)) + dot(lower, three_parts(v * v))
    total = r.row_sums[:, 0:D]
    for x in range(1, SIDE):
        total = total + r.row_sums[:, x * D : (x + 1) * D]
    return jnp.concatenate([total, r.row_counts[:, 0 : LANES - D]], axis=1)


def corrected_rows(r, out):
    for x in range(SIDE):
        r.row_sums[:, x * D : (x + 1) * D] = r.dstat_rows[:, 0:D]
    zero = jnp.zeros((8, TILE), bf16)
    for k in range(6):
        at = slice(k * TILE, (k + 1) * TILE)
        parts = jnp.concatenate([three_parts(r.row_sums[:, at]), zero], axis=0)
        dsums, dsquares = dot(r.row_columns[0], parts), dot(r.row_columns[1], parts)
        v = r.rows_in[0, :, :, :, at].reshape(LANES, TILE) + dsums + r.own[:, :, at].reshape(LANES, TILE) * dsquares
        out[:, :, at] = jnp.where(row_mask(r, k * TILE), v, 0.0).reshape(32, 4, TILE)


def statistics_partial(r):
    total = jnp.concatenate([r.sums[0], r.counts[...], jnp.zeros((24, LANES), f32)], axis=0)
    square = jnp.concatenate([r.sums[1], jnp.zeros((32, LANES), f32)], axis=0)
    return lane_sums(total, square, r)


def per_lane(upper, lower, r):
    turned = jnp.transpose(jnp.concatenate([upper, lower], axis=0))
    return exact_dot(turned, r.onehot[0:8])[0:D], exact_dot(turned, r.onehot[8:16])[0:D]


def use_statistics(r, l, totals):
    count = totals[0:4, D : D + 1]
    centre = totals[0:4] / count
    variance = totals[4:8] / count - centre * centre
    rate = lax.rsqrt(variance + EPSILON)
    r.stat_rows[l, 0:4] = centre
    r.stat_rows[l, 4:8] = rate
    r.count_rows[...] = jnp.broadcast_to(count, (4, LANES))
    centre_lanes, rate_lanes = per_lane(centre, rate, r)
    r.centre[l] = centre_lanes
    r.rate[l] = rate_lanes


def use_statistics_grad(r, l, totals):
    centre, rate = r.stat_rows[l, 0:4], r.stat_rows[l, 4:8]
    count = r.count_rows[...]
    gain = jnp.concatenate([r.gains[l, 0:1], jnp.zeros((1, LANES - D), f32)], axis=1)
    dcentre = -rate * gain * totals[0:4]
    dvariance = -0.5 * rate * rate * rate * gain * totals[4:8]
    dsums = (dcentre - 2.0 * centre * dvariance) / count
    dsquares = dvariance / count
    r.dstat_rows[0:4] = dsums
    r.dstat_rows[4:8] = 2.0 * dsquares
    if l > 0:
        r.dstat[0], r.dstat[1] = per_lane(dsums, 2.0 * dsquares, r)


def forward_local(r, l):
    r.fmap[l, :, 0:LANES] = jnp.zeros((D, LANES), f32)
    r.fmap[l, :, LANES + CELLS :] = jnp.zeros((D, LANES), f32)

    def body(j):
        v = r.x[l, :, tile_at(j)]
        pair = split((v - wide(r.centre[l])) * wide(r.rate[l] * r.par[l, 0]) + wide(r.par[l, 4]))
        r.n2[l, :, tile_at(j)] = pair
        yield
        out = mapped(r.first_t[l], pair) + wide(r.par[l, 5])
        r.fmap[l, :, padded_tile_at(j)] = out * r.mask[0:1, tile_at(j)]
        yield
        yield
        pair = split(convolved(r, l, j))
        r.d2[l, :, tile_at(j)] = pair
        yield
        out = mapped(r.second_t[l], pair) + wide(r.par[l, 7])
        local = r.x[l, :, tile_at(j)] + out * r.mask[0:1, tile_at(j)]
        r.local[:, tile_at(j)] = local
        unit, rate = normalized(local)
        r.unit1[l, :, tile_at(j)] = unit
        r.rates[l, 0:1, tile_at(j)] = rate
        r.pooled[:, lanes_at(j)] = split(
            0.25 * folded(unit * wide(r.par[l, 1]) + wide(r.par[l, 8]))
        )

    staggered(8, body)


def convolved(r, l, j):
    lane = lane_iota((8, LANES), 1)
    groups = []
    for g in range(12):
        rows = slice(g * 8, (g + 1) * 8)
        taps = [r.par[l, 16 + t, rows, :] for t in range(9)]
        cells = [r.fmap[l, rows, (2 * j + x) * LANES : (2 * j + x + 1) * LANES] for x in range(4)]
        columns = []
        for x in range(2):
            sums = [sum(taps[3 * q + c] * cells[x + c] for c in range(3)) for q in range(3)]
            columns.append(
                r.par[l, 6, rows, :] + sums[1] + from_row_before(sums[0], lane) + from_row_after(sums[2], lane)
            )
        groups.append(jnp.concatenate(columns, axis=1))
    return jnp.concatenate(groups, axis=0)


def forward_mixer(r, l):
    forward_queries(r, l)
    forward_attention(r, l)
    forward_spread(r, l)


def forward_queries(r, l):
    delegates = joined(dot(r.pooled[...], r.pool[...]))
    pair = split(delegates)
    r.g2[l] = pair
    qkv = mapped(r.mixer_t[l], pair)
    queries, keys, values = qkv[0:D], qkv[D : 2 * D], qkv[2 * D :]
    for t in range(4):
        at = slice(t * LANES, (t + 1) * LANES)
        r.qkv[l, 0:D, at] = (queries[:, at] + r.par[l, 9]) * SCALE
        r.qkv[l, D : 2 * D, at] = keys[:, at]
        r.qkv[l, 2 * D :, at] = values[:, at] + r.par[l, 10]


def by_head(v):
    zero = jnp.zeros((HEAD, LANES), f32)
    return jnp.concatenate(
        [jnp.concatenate([v[0:HEAD], zero], axis=1), jnp.concatenate([zero, v[HEAD:]], axis=1)], axis=0
    )


def own_head(v):
    return jnp.concatenate([v[0:HEAD, 0:LANES], v[HEAD:, LANES:]], axis=0)


def left_rows(v):
    turned = jnp.transpose(jnp.concatenate([v, v], axis=0))
    return jnp.concatenate(halves(turned), axis=0)


def left_columns(v):
    high, low = halves(v)
    return jnp.concatenate(
        [jnp.concatenate([high, high], axis=1), jnp.concatenate([low, low], axis=1)], axis=0
    )


def column_product(a_pair, b_pair):
    both = joined(dot(a_pair, b_pair, NT))
    return folded(both)


HEAD = D // 2
SCALE = 1.0 / math.sqrt(HEAD)


def forward_attention(r, l):
    def body(p):
        at = slice(p * LANES, (p + 1) * LANES)
        q, k, v = (r.qkv[l, part * D : (part + 1) * D, at] for part in range(3))
        left, right = left_rows(k), split(by_head(q))
        yield
        scores = joined(dot(left, right))
        scores = jnp.where(wide(r.keep[p]) > 0.0, scores, MASKED_SCORE)
        yield
        weights = jnp.exp(scores - jnp.max(scores, axis=0, keepdims=True))
        probs = weights / jnp.sum(weights, axis=0, keepdims=True)
        r.probs[l, p] = probs
        yield
        r.mixture[:, at] = own_head(mapped(left_columns(v), split(probs)))

    staggered(4, body)


def forward_spread(r, l):
    r.mix2[...] = split(r.mixture[...])

    def spread(t):
        r.up[l, :, tile_at(t)] = joined(dot(r.mix2[...], r.pool[tile_at(t), :], NT))

    loop(4, spread)


def rest_forward(r, l, j):
    mask = r.mask[0:1, tile_at(j)]
    up = r.up[l, :, lanes_at(j)]
    spread = jnp.concatenate([up * r.taps[l, 0], up * r.taps[l, 1]], axis=1) + wide(r.par[l, 11])
    unit2, rate2 = normalized(spread)
    pair = split(unit2 * wide(r.par[l, 2]) + wide(r.par[l, 12]))
    r.s2[l, :, tile_at(j)] = pair
    yield
    middle = r.local[:, tile_at(j)] + mask * (mapped(r.output_t[l], pair) + wide(r.par[l, 13]))
    unit3, rate3 = normalized(middle)
    pair = split(unit3 * wide(r.par[l, 3]) + wide(r.par[l, 14]))
    r.e2[l, :, tile_at(j)] = pair
    yield
    before = mapped(r.expand_t[l], pair) + wide(r.epar[l])
    yield
    normal = 0.5 + 0.5 * lax.erf(before * math.sqrt(0.5))
    slope = normal + before * (jnp.exp(-0.5 * before * before) * (1.0 / math.sqrt(2.0 * math.pi)))
    hidden = split(before * normal)
    r.h2[l, :, tile_at(j)] = hidden
    yield
    out = middle + mask * (mapped(r.reduce_t[l], hidden) + wide(r.par[l, 15]))
    return out, unit2, rate2, unit3, rate3, slope


def rest_backward(r, l, j, dy, unit2, rate2, unit3, rate3, slope):
    def add(k, v):
        r.acc[l, k] += folded(v)

    pair = split(dy)
    r.dy2[:, tile_at(j)] = pair
    add(15, dy)
    yield
    dbefore = mapped(r.reduce_n[l], pair) * slope
    r.eacc[l] += folded(dbefore)
    pair = split(dbefore)
    r.dp2[:, tile_at(j)] = pair
    yield
    de = mapped(r.expand_n[l], pair)
    add(14, de)
    add(3, de * unit3)
    dmiddle = dy + norm_pullback(de * wide(r.par[l, 3]), unit3, rate3)
    r.local[:, tile_at(j)] = dmiddle
    add(13, dmiddle)
    pair = split(dmiddle)
    r.dm2[:, tile_at(j)] = pair
    yield
    ds = mapped(r.output_n[l], pair)
    add(12, ds)
    add(2, ds * unit2)
    dspread = norm_pullback(ds * wide(r.par[l, 2]), unit2, rate2)
    add(11, dspread)
    up = r.up[l, :, lanes_at(j)]
    r.acc[l, 25] += dspread[:, :LANES] * up
    r.acc[l, 26] += dspread[:, LANES:] * up
    r.pooled[:, lanes_at(j)] = split(
        dspread[:, :LANES] * r.taps[l, 0] + dspread[:, LANES:] * r.taps[l, 1]
    )


def forward_rest(r, l):
    def body(j):
        out, unit2, rate2, unit3, rate3, slope = yield from rest_forward(r, l, j)
        r.unit2[:, tile_at(j)] = unit2
        r.unit3[:, tile_at(j)] = unit3
        r.rates2[0:1, tile_at(j)] = rate2
        r.rates2[1:2, tile_at(j)] = rate3
        r.slope[:, tile_at(j)] = slope
        r.x[l + 1, :, tile_at(j)] = out
        r.sums[0] += folded(out)
        r.sums[1] += folded(out * out)

    r.sums[...] = jnp.zeros_like(r.sums)
    staggered(8, body)


def backward_rest(r, l):
    def body(j):
        yield from rest_backward(
            r, l, j, r.dy[:, tile_at(j)], r.unit2[:, tile_at(j)], r.rates2[0:1, tile_at(j)],
            r.unit3[:, tile_at(j)], r.rates2[1:2, tile_at(j)], r.slope[:, tile_at(j)],
        )

    staggered(8, body)


def turn_rest(r, l):
    def body(j):
        out, *kept = yield from rest_forward(r, l, j)
        r.temp[:, tile_at(j)] = out
        yield from rest_backward(r, l, j, r.dy[:, tile_at(j)], *kept)

    staggered(8, body)


def backward_mixer(r, l):
    backward_gather(r, l)
    backward_attention(r, l)
    backward_queries(r, l)
    backward_spread(r, l)


def backward_gather(r, l):
    r.mixture[...] = joined(dot(r.pooled[...], r.pool[...]))


def backward_attention(r, l):
    def body(p):
        at = slice(p * LANES, (p + 1) * LANES)
        q, k, v = (r.qkv[l, part * D : (part + 1) * D, at] for part in range(3))
        probs = r.probs[l, p]
        dout = split(by_head(r.mixture[:, at]))
        left = left_rows(v)
        yield
        dprobs = joined(dot(left, dout))
        yield
        dscores = split(probs * (dprobs - jnp.sum(probs * dprobs, axis=0, keepdims=True)))
        r.dqkv[2 * D :, at] = column_product(dout, split(probs))
        yield
        r.dqkv[0:D, at] = own_head(mapped(left_columns(k), dscores)) * SCALE
        r.dqkv[D : 2 * D, at] = column_product(split(by_head(q)), dscores)

    staggered(4, body)


def backward_queries(r, l):
    dqkv = r.dqkv[...]
    for t in range(4):
        at = slice(t * LANES, (t + 1) * LANES)
        r.acc[l, 9] += dqkv[0:D, at]
        r.acc[l, 10] += dqkv[2 * D :, at]
    pair = split(dqkv)
    r.dq2[...] = pair
    r.mix2[...] = split(mapped(r.mixer_n[l], pair))


def backward_spread(r, l):
    def spread(t):
        r.dup[:, tile_at(t)] = 0.25 * joined(dot(r.mix2[...], r.pool[tile_at(t), :], NT))

    loop(4, spread)


def backward_local(r, l):
    lane = lane_iota((D, LANES), 1)
    for q in range(3):
        r.dmap[q, :, 0:LANES] = jnp.zeros((D, LANES), f32)
        r.dmap[q, :, LANES + CELLS :] = jnp.zeros((D, LANES), f32)

    def add(k, v):
        r.acc[l, k] += folded(v)

    def body(j):
        dup = wide(r.dup[:, lanes_at(j)])
        unit = r.unit1[l, :, tile_at(j)]
        add(8, dup)
        add(1, dup * unit)
        dlocal = r.local[:, tile_at(j)] + norm_pullback(
            dup * wide(r.par[l, 1]), unit, r.rates[l, 0:1, tile_at(j)]
        )
        r.local[:, tile_at(j)] = dlocal
        add(7, dlocal)
        pair = split(dlocal)
        r.dl2[:, tile_at(j)] = pair
        yield
        out = mapped(r.second_n[l], pair)
        add(6, out)
        r.dmap[1, :, padded_tile_at(j)] = out
        for x in range(2):
            column = out[:, x * LANES : (x + 1) * LANES]
            place = slice((2 * j + x + 1) * LANES, (2 * j + x + 2) * LANES)
            r.dmap[0, :, place] = from_row_after(column, lane)
            r.dmap[2, :, place] = from_row_before(column, lane)
        yield
        yield
        v = convolved_back(r, l, j) * r.mask[0:1, tile_at(j)]
        add(5, v)
        pair = split(v)
        r.df2[:, tile_at(j)] = pair
        yield
        dnormed = mapped(r.first_n[l], pair)
        r.temp[:, tile_at(j)] = dnormed
        r.acc[l, 4] += folded(dnormed)
        r.acc[l, 0] += folded(dnormed * (r.x[l, :, tile_at(j)] - wide(r.centre[l])))

    staggered(8, body)


def convolved_back(r, l, j):
    groups = []
    for g in range(12):
        rows = slice(g * 8, (g + 1) * 8)
        value = [r.fmap[l, rows, (2 * j + x + 1) * LANES : (2 * j + x + 2) * LANES] for x in range(2)]
        columns = [0.0, 0.0]
        for q in range(3):
            source = [r.dmap[q, rows, (2 * j + x) * LANES : (2 * j + x + 1) * LANES] for x in range(4)]
            for c in range(3):
                tap = r.par[l, 16 + 3 * q + c, rows, :]
                for x in range(2):
                    columns[x] = columns[x] + tap * source[x + 2 - c]
                r.acc[l, 16 + 3 * q + c, rows, :] += sum(source[x + 2 - c] * value[x] for x in range(2))
        groups.append(jnp.concatenate(columns, axis=1))
    return jnp.concatenate(groups, axis=0)


def statistics_grad_partial(r, l):
    pad = jnp.zeros((LANES - D, LANES), f32)
    return lane_sums(
        jnp.concatenate([r.acc[l, 4], pad], axis=0), jnp.concatenate([r.acc[l, 0], pad], axis=0), r
    )


def backward_input(r, l):
    def body(j):
        v = r.x[l, :, tile_at(j)]
        r.dy[:, tile_at(j)] = (
            r.temp[:, tile_at(j)] * wide(r.rate[l] * r.par[l, 0])
            + r.local[:, tile_at(j)]
            + r.mask[0:1, tile_at(j)] * (wide(r.dstat[0]) + v * wide(r.dstat[1]))
        )

    loop(8, body)


def partial_input(r, l):
    def body(j):
        r.dy[:, tile_at(j)] = (
            r.temp[:, tile_at(j)] * wide(r.rate[l] * r.par[l, 0]) + r.local[:, tile_at(j)]
        )

    loop(8, body)


def big_product(r, l, a, b, place):
    both = dot(a, b, NT)
    both = both[0:D] + both[D:]
    both = both[:, 0:FF] + both[:, FF:]
    for t in range(3):
        r.grads[l, place + t * D : place + (t + 1) * D] = both[:, t * LANES : (t + 1) * LANES]


def small_product(r, l, a, b, place):
    both = dot(a, b, NT)
    both = both[0:D] + both[D:]
    r.grads[l, place : place + D, 0:D] = both[:, 0:D] + both[:, D:]


def feed_forward_grads(r, l):
    big_product(r, l, r.e2[l], r.dp2[...], 0)
    big_product(r, l, r.dy2[...], r.h2[l], 288)


def mixer_grads(r, l):
    small_product(r, l, r.s2[l], r.dm2[...], 576)
    for t in range(3):
        part = jnp.concatenate(
            [r.dq2[t * D : (t + 1) * D], r.dq2[(3 + t) * D : (4 + t) * D]], axis=0
        )
        small_product(r, l, r.g2[l], part, 672 + t * D)


def local_grads(r, l):
    small_product(r, l, r.n2[l], r.df2[...], 1024)
    small_product(r, l, r.d2[l], r.dl2[...], 1120)


def vector_grads(r, l):
    r.acc[l, 0] = r.acc[l, 0] * r.rate[l]
    ones = jnp.ones((8, TILE), f32)
    even = ((lane_iota((8, TILE), 1) & 1) == 0).astype(f32)
    odd = (ones - even).astype(bf16)
    ones, even = ones.astype(bf16), even.astype(bf16)

    def row(kind, v, place, count):
        total = dot(kind, jnp.concatenate(halves(v), axis=1), NT)
        r.grads[l, 1216 + place : 1217 + place, 0:count] = total[0:1]

    for k in range(25):
        row(ones, r.acc[l, k], k, D)
    for b in range(2):
        row(even, r.acc[l, 25 + b], 25 + b, D)
        row(odd, r.acc[l, 25 + b], 27 + b, D)
    for t in range(3):
        row(ones, r.eacc[l, t * LANES : (t + 1) * LANES], 29 + t, LANES)


def weight_grads(r, l):
    feed_forward_grads(r, l)
    mixer_grads(r, l)
    local_grads(r, l)
    vector_grads(r, l)


def scratch_list():
    L = LAYERS
    v = pltpu.VMEM
    return [
        ("first_t", v((L, 192, 192), bf16)),
        ("first_n", v((L, 192, 192), bf16)),
        ("second_t", v((L, 192, 192), bf16)),
        ("second_n", v((L, 192, 192), bf16)),
        ("mixer_t", v((L, 576, 192), bf16)),
        ("mixer_n", v((L, 192, 576), bf16)),
        ("output_t", v((L, 192, 192), bf16)),
        ("output_n", v((L, 192, 192), bf16)),
        ("expand_t", v((L, 768, 192), bf16)),
        ("expand_n", v((L, 192, 768), bf16)),
        ("reduce_t", v((L, 192, 768), bf16)),
        ("reduce_n", v((L, 768, 192), bf16)),
        ("rows", v((PARAM_ROWS, LANES), f32)),
        ("par", v((L, 29, D, LANES), f32)),
        ("epar", v((L, FF, LANES), f32)),
        ("taps", v((L, 2, D, LANES), f32)),
        ("acc", v((L, 27, D, LANES), f32)),
        ("eacc", v((L, FF, LANES), f32)),
        ("mask", v((8, CELLS), f32)),
        ("counts", v((8, LANES), f32)),
        ("onehot", v((16, LANES), f32)),
        ("keep", v((4, LANES, LANES), f32)),
        ("pool", v((8 * LANES, DELEGATES), bf16)),
        ("sums", v((2, D, LANES), f32)),
        ("own", v((32, 4, SIDE * D), f32)),
        ("row_limit", v((LANES, LANES), f32)),
        ("row_onehot", v((16, LANES), f32)),
        ("row_counts", v((8, LANES), f32)),
        ("row_columns", v((2, LANES, 32), bf16)),
        ("row_sums", v((8, SIDE * D), f32)),
        ("dstat_rows", v((8, LANES), f32)),
        ("stat_rows", v((L, 8, LANES), f32)),
        ("count_rows", v((4, LANES), f32)),
        ("centre", v((L, D, LANES), f32)),
        ("rate", v((L, D, LANES), f32)),
        ("dstat", v((2, D, LANES), f32)),
        ("x", v((L, D, CELLS), f32)),
        ("n2", v((L, 2 * D, CELLS), bf16)),
        ("fmap", v((L, D, CELLS + 2 * LANES), f32)),
        ("temp", v((D, CELLS), f32)),
        ("d2", v((L, 2 * D, CELLS), bf16)),
        ("local", v((D, CELLS), f32)),
        ("unit1", v((L, D, CELLS), f32)),
        ("rates", v((L, 1, CELLS), f32)),
        ("pooled", v((2 * D, 8 * LANES), bf16)),
        ("g2", v((L, 2 * D, DELEGATES), bf16)),
        ("qkv", v((L, 3 * D, DELEGATES), f32)),
        ("probs", v((L, 4, LANES, TILE), f32)),
        ("mixture", v((D, DELEGATES), f32)),
        ("mix2", v((2 * D, DELEGATES), bf16)),
        ("up", v((L, D, 8 * LANES), f32)),
        ("unit2", v((D, CELLS), f32)),
        ("s2", v((L, 2 * D, CELLS), bf16)),
        ("unit3", v((D, CELLS), f32)),
        ("rates2", v((8, CELLS), f32)),
        ("e2", v((L, 2 * D, CELLS), bf16)),
        ("slope", v((FF, CELLS), f32)),
        ("h2", v((L, 2 * FF, CELLS), bf16)),
        ("dy", v((D, CELLS), f32)),
        ("dy2", v((2 * D, CELLS), bf16)),
        ("dp2", v((2 * FF, CELLS), bf16)),
        ("dm2", v((2 * D, CELLS), bf16)),
        ("dqkv", v((3 * D, DELEGATES), f32)),
        ("dq2", v((6 * D, DELEGATES), bf16)),
        ("dup", v((D, 8 * LANES), f32)),
        ("dl2", v((2 * D, CELLS), bf16)),
        ("dmap", v((3, D, CELLS + 2 * LANES), f32)),
        ("df2", v((2 * D, CELLS), bf16)),
        ("grads", v((L, GRAD_ROWS, LANES), f32)),
    ]


PARAMS = (
    "gains", "biases", "depth", "spread", "first", "second", "mixer", "output", "expand", "ebias", "reduce",
)

OTHERS = 15
GROUP = 7
STEPS = sorted(
    [(x, y) for x in range(4) for y in range(4) if x + y > 0],
    key=lambda step: -min(step[0], 4 - step[0]) - min(step[1], 4 - step[1]),
)
PARCELS = ((0, 0, 1024), (0, 1024, 256), (1, 0, 1280))


class Place:
    def __init__(self):
        dp = lax.axis_index("dp")
        self.z = lax.axis_index("segment")
        self.core = lax.rem(dp, 2)
        self.chip = lax.div(dp, 2)
        self.member = self.z * 2 + self.core

    def chip_at(self, d):
        x, y = STEPS[d - 1]
        return lax.rem(lax.div(self.chip, 4) + x, 4) * 4 + lax.rem(lax.rem(self.chip, 4) + y, 4)

    def chip_after(self, d):
        return (self.z, self.chip_at(d) * 2 + self.core)

    def member_after(self, d):
        member = lax.rem(self.member + d, 8)
        return (lax.div(member, 2), self.chip * 2 + lax.rem(member, 2))

    def z_after(self, d):
        return (lax.rem(self.z + d, 4), self.chip * 2 + self.core)

    def sibling(self):
        return (self.z, self.chip * 2 + 1 - self.core)


def remote(src, dst, sends, receives, index, device):
    return pltpu.make_async_remote_copy(
        src_ref=src,
        dst_ref=dst,
        send_sem=sends.at[index],
        recv_sem=receives.at[index],
        device_id=device,
        device_id_type=pl.DeviceIdType.MESH,
    )


def greet(me):
    barrier = pltpu.get_barrier_semaphore()
    for d in range(1, 16):
        pl.semaphore_signal(barrier, inc=1, device_id=me.chip_after(d), device_id_type=pl.DeviceIdType.MESH)
    for d in range(1, 8):
        pl.semaphore_signal(barrier, inc=1, device_id=me.member_after(d), device_id_type=pl.DeviceIdType.MESH)
    return barrier


class RowsIn:
    def __init__(self, r, me, src, dst, number):
        self.own = pltpu.make_async_copy(src.at[pl.ds(me.z * 8, 8)], dst.at[me.z], r.row_own.at[number])
        self.copies = [
            remote(
                src.at[pl.ds(lax.rem(me.z + d, 4) * 8, 8)], dst.at[me.z],
                r.row_send, r.row_recv, (number, d), me.z_after(d),
            )
            for d in range(1, 4)
        ]

    def start(self):
        for copy in self.copies:
            copy.start()
        self.own.start()

    def wait(self):
        self.own.wait()
        for copy in self.copies:
            copy.wait()


class RowsOut(RowsIn):
    def __init__(self, r, me, src, dst, number):
        self.own = pltpu.make_async_copy(src.at[me.z], dst, r.row_own.at[number])
        self.copies = [
            remote(
                src.at[lax.rem(me.z + d, 4)], dst,
                r.row_send, r.row_recv, (number, d), me.z_after(d),
            )
            for d in range(1, 4)
        ]


class SmallSum:
    def __init__(self, r, me, number):
        self.r, self.me, self.number = r, me, number
        mine = r.chip_parts.at[number, me.chip]
        self.first = [
            remote(mine, mine, r.chip_send, r.chip_recv, (number, d), me.chip_after(d)) for d in range(1, 16)
        ]
        mine = r.group_parts.at[number, me.member]
        self.second = [
            remote(mine, mine, r.group_send, r.group_recv, (number, d), me.member_after(d))
            for d in range(1, 8)
        ]

    def put(self, value):
        self.r.chip_parts[self.number, self.me.chip] = value

    def start(self):
        for copy in self.first:
            copy.start()

    def step(self):
        for copy in self.first:
            copy.wait()
        total = self.r.chip_parts[self.number, 0]
        for k in range(1, 16):
            total = total + self.r.chip_parts[self.number, k]
        self.r.group_parts[self.number, self.me.member] = total
        for copy in self.second:
            copy.start()

    def finish(self):
        for copy in self.second:
            copy.wait()
        total = self.r.group_parts[self.number, 0]
        for k in range(1, 8):
            total = total + self.r.group_parts[self.number, k]
        return total


class WeightSum:
    def __init__(self, r, me, number):
        self.r, self.me, self.number = r, me, number
        layer, start, rows = PARCELS[number]
        count, size = rows // 2, rows // 32
        grads, totals = r.grads.at[layer], r.totals.at[layer]
        self.half, self.parts, self.planes = (
            getattr(r, kind + str(number)) for kind in ("half", "parts", "planes")
        )

        def half_of(core):
            return pl.ds(pl.multiple_of(start + core * count, 8), count)

        def piece_of(chip):
            return pl.ds(pl.multiple_of(chip * size, 8), size)

        self.mine = grads.at[half_of(me.core)]
        self.own_piece = self.half.at[piece_of(me.chip)]
        self.halves = remote(
            grads.at[half_of(1 - me.core)], self.half, r.half_send, r.half_recv, (number, 0), me.sibling()
        )
        self.pieces = [
            remote(
                self.half.at[piece_of(me.chip_at(d))], self.parts.at[me.chip],
                r.piece_send, r.piece_recv, (number, 0, d), me.chip_after(d),
            )
            for d in range(1, 16)
        ]
        plane = self.planes.at[me.z]
        self.exchange = [
            remote(plane, plane, r.plane_send, r.plane_recv, (number, d), me.z_after(d)) for d in range(1, 4)
        ]
        self.total = totals.at[pl.ds(pl.multiple_of(start + me.core * count + me.chip * size, 8), size)]
        self.gathers = [
            remote(self.total, self.total, r.piece_send, r.piece_recv, (number, 1, d), me.chip_after(d))
            for d in range(1, 16)
        ]
        whole = totals.at[half_of(me.core)]
        self.last = remote(whole, whole, r.half_send, r.half_recv, (number, 1), me.sibling())

    def step(self, number):
        me = self.me
        if number == 0:
            self.halves.start()
        elif number == 1:
            self.halves.wait()
            self.half[...] = self.half[...] + self.mine[...]
            self.parts[me.chip] = self.own_piece[...]
            for copy in self.pieces:
                copy.start()
        elif number == 2:
            for copy in self.pieces:
                copy.wait()
            total = self.parts[0]
            for k in range(1, 16):
                total = total + self.parts[k]
            self.planes[me.z] = total
            for copy in self.exchange:
                copy.start()
        elif number == 3:
            for copy in self.exchange:
                copy.wait()
            self.total[...] = (self.planes[0] + self.planes[1]) + (self.planes[2] + self.planes[3])
            for copy in self.gathers:
                copy.start()
        elif number == 4:
            for copy in self.gathers:
                copy.wait()
            self.last.start()
        else:
            self.last.wait()


def comm_scratch():
    L = LAYERS
    v = pltpu.VMEM
    s = pltpu.SemaphoreType.DMA
    return [
        ("rows_in", v((2, 4, 8, 4, SIDE * D), f32)),
        ("rows_out", v((4, 8, 4, SIDE * D), f32)),
        ("chip_parts", v((4, 16, 8, LANES), f32)),
        ("group_parts", v((4, 8, 8, LANES), f32)),
        ("totals", v((L, GRAD_ROWS, LANES), f32)),
        ("row_own", s((5,))),
        ("row_send", s((4, 4))),
        ("row_recv", s((4, 4))),
        ("chip_send", s((4, 16))),
        ("chip_recv", s((4, 16))),
        ("group_send", s((4, 8))),
        ("group_recv", s((4, 8))),
        ("half_send", s((len(PARCELS), 2))),
        ("half_recv", s((len(PARCELS), 2))),
        ("piece_send", s((len(PARCELS), 2, 16))),
        ("piece_recv", s((len(PARCELS), 2, 16))),
        ("plane_send", s((len(PARCELS), 4))),
        ("plane_recv", s((len(PARCELS), 4))),
        ("out_sem", s((2,))),
    ] + [
        (kind + str(number), v(lead + (rows // share, LANES), f32))
        for number, (_, _, rows) in enumerate(PARCELS)
        for kind, lead, share in (("half", (), 2), ("parts", (16,), 32), ("planes", (4,), 32))
    ]


def layers_kernel(names, *refs):
    r = SimpleNamespace(**dict(zip(names, refs)))
    me = Place()
    barrier = greet(me)
    own_rows = pltpu.make_async_copy(r.tokens, r.own, r.row_own.at[4])
    own_rows.start()
    mine = pl.ds(me.z * 8, 8)
    tokens_in = RowsIn(r, me, r.tokens, r.rows_in.at[0], 0)
    upstream_in = RowsIn(r, me, r.cotangent, r.rows_in.at[1], 1)
    act_out = RowsOut(r, me, r.rows_out, r.act.at[mine], 2)
    grad_out = RowsOut(r, me, r.rows_in.at[1], r.rows_in.at[0, me.z], 3)
    sums = [SmallSum(r, me, number) for number in range(4)]
    late, last, early = (WeightSum(r, me, number) for number in range(3))

    def run(work):
        pl.when(me.z >= 0)(work)

    @run
    def masks():
        prepare_masks(r, me.z)

    own_rows.wait()
    pl.semaphore_wait(barrier, OTHERS + GROUP)
    tokens_in.start()

    @run
    def first_statistics():
        sums[0].put(row_statistics(r))

    sums[0].start()

    @run
    def first_weights():
        prepare_weights(r, 0)
        r.grads[...] = jnp.zeros_like(r.grads)

    sums[0].step()
    tokens_in.wait()
    upstream_in.start()

    @run
    def tokens():
        take_rows(r.rows_in.at[0], r.x.at[0], r.mask)

    use_statistics(r, 0, sums[0].finish())

    @run
    def first_layer():
        forward_local(r, 0)
        forward_mixer(r, 0)
        forward_rest(r, 0)
        sums[1].put(statistics_partial(r))

    sums[1].start()

    @run
    def second_weights():
        prepare_weights(r, 1)

    sums[1].step()
    upstream_in.wait()

    @run
    def upstream():
        take_rows(r.rows_in.at[1], r.dy, r.mask)

    use_statistics(r, 1, sums[1].finish())

    @run
    def second_layer():
        forward_local(r, 1)
        forward_mixer(r, 1)
        turn_rest(r, 1)
        give_rows(r.temp, r.rows_out)

    act_out.start()

    @run
    def second_backward():
        backward_mixer(r, 1)
        backward_local(r, 1)
        sums[2].put(statistics_grad_partial(r, 1))

    sums[2].start()

    @run
    def second_products():
        feed_forward_grads(r, 1)
        mixer_grads(r, 1)

    sums[2].step()

    @run
    def second_local_products():
        local_grads(r, 1)
        vector_grads(r, 1)

    early.step(0)
    use_statistics_grad(r, 1, sums[2].finish())

    @run
    def between():
        backward_input(r, 1)

    early.step(1)

    @run
    def first_backward():
        backward_rest(r, 0)
        backward_mixer(r, 0)
        feed_forward_grads(r, 0)
        mixer_grads(r, 0)

    late.step(0)
    early.step(2)

    @run
    def first_local_backward():
        backward_local(r, 0)
        sums[3].put(statistics_grad_partial(r, 0))

    sums[3].start()
    late.step(1)

    @run
    def first_local_products():
        local_grads(r, 0)
        vector_grads(r, 0)

    last.step(0)
    early.step(3)

    @run
    def input_grad():
        partial_input(r, 0)
        give_rows(r.dy, r.rows_in.at[1])

    grad_out.start()
    last.step(1)
    sums[3].step()
    late.step(2)
    last.step(2)
    early.step(4)
    use_statistics_grad(r, 0, sums[3].finish())
    late.step(3)
    last.step(3)
    grad_out.wait()

    @run
    def correction():
        corrected_rows(r, r.own)

    copy = pltpu.make_async_copy(r.own, r.grad, r.out_sem.at[0])
    copy.start()
    early.step(5)
    last.step(4)
    late.step(4)
    act_out.wait()
    last.step(5)
    late.step(5)
    totals = pltpu.make_async_copy(r.totals, r.grad_sums, r.out_sem.at[1])
    totals.start()
    copy.wait()
    totals.wait()


def unpack_kernel(act_in, grad_in, totals, act, grad, *outs):
    refs, (rows, sems) = outs[:-2], outs[-2:]
    loads = [
        pltpu.make_async_copy(src, rows.at[k], sems.at[0, k]) for k, src in enumerate((act_in, grad_in))
    ]
    stores = [pltpu.make_async_copy(rows.at[k], dst, sems.at[1, k]) for k, dst in enumerate((act, grad))]
    for copy in loads:
        copy.start()
    for load, store in zip(loads, stores):
        load.wait()
        store.start()
    gains, biases, depth, spread, first, second, mixer, output, expand, ebias, reduce = refs
    for l in range(LAYERS):

        def taken(place, count, width=D):
            return totals[l, place : place + count, 0:width]

        gains[l] = taken(1216, 4)
        biases[:, l] = taken(1220, 12)
        depth[:, l] = taken(1232, 9)
        spread[l] = taken(1241, 4)
        first[l] = taken(1024, D)
        second[l] = taken(1120, D)
        output[l] = taken(576, D)
        for t in range(3):
            at = slice(t * LANES, (t + 1) * LANES)
            mixer[l, :, t * D : (t + 1) * D] = taken(672 + t * D, D)
            expand[l, :, at] = taken(t * D, D, LANES)
            reduce[l, :, at] = taken(288 + t * D, D, LANES)
            ebias[l : l + 1, at] = taken(1245 + t, 1, LANES)
    for store in stores:
        store.wait()


def turned(params):
    gains, biases, depth, spread, *maps, ebias, reduce = params
    return (gains, jnp.swapaxes(biases, 0, 1), jnp.swapaxes(depth, 0, 1), spread, *maps, ebias,
            jnp.swapaxes(reduce, 1, 2))


def shards(tokens, cotangent, image_size, slot_image, slot_batch, *params):
    params = turned(params)
    scratch = scratch_list() + comm_scratch()
    ins = ("tokens", "cotangent", "sizes", "slot_image", "slot_batch") + PARAMS
    outs = ("act", "grad", "grad_sums")
    names = ins + outs + tuple(name for name, _ in scratch)
    anywhere = pl.BlockSpec(memory_space=pl.ANY)
    vmem = pl.BlockSpec(memory_space=pltpu.VMEM)
    smem = pl.BlockSpec(memory_space=pltpu.SMEM)
    act, grad, totals = pl.pallas_call(
        functools.partial(layers_kernel, names),
        out_shape=[
            jax.ShapeDtypeStruct(tokens.shape, f32),
            jax.ShapeDtypeStruct(tokens.shape, f32),
            jax.ShapeDtypeStruct((LAYERS, GRAD_ROWS, LANES), f32),
        ],
        in_specs=[anywhere, anywhere, vmem, smem, smem] + [vmem] * len(params),
        out_specs=[anywhere] * 3,
        scratch_shapes=[shape for _, shape in scratch],
        compiler_params=pltpu.CompilerParams(
            collective_id=0, has_side_effects=True, vmem_limit_bytes=63 * 2**20
        ),
        name="layers",
    )(tokens, cotangent, image_size.T, slot_image, slot_batch, *params)
    act, grad, *grads = pl.pallas_call(
        unpack_kernel,
        out_shape=[jax.ShapeDtypeStruct(tokens.shape, f32)] * 2
        + [jax.ShapeDtypeStruct(p.shape, f32) for p in params],
        in_specs=[anywhere, anywhere, vmem],
        out_specs=[anywhere, anywhere] + [vmem] * len(params),
        scratch_shapes=[pltpu.VMEM((2,) + tokens.shape, f32), pltpu.SemaphoreType.DMA((2, 2))],
        compiler_params=pltpu.CompilerParams(vmem_limit_bytes=60 * 2**20),
        name="unpack",
    )(act, grad, totals)
    return (act, grad) + turned(grads)


def solution(mesh):
    rows = P("dp", "segment", None)
    return jax.shard_map(
        shards,
        mesh=mesh,
        in_specs=(rows, rows, P(), P("dp"), P("dp")) + (P(),) * len(PARAMS),
        out_specs=(rows, rows) + (P(),) * len(PARAMS),
        check_vma=False,
    )
```

```python
import functools
import math
from types import SimpleNamespace

import jax
import jax.numpy as jnp
from jax import lax
from jax.experimental import pallas as pl
from jax.experimental.pallas import tpu as pltpu
from jax.sharding import PartitionSpec as P

D = 96
FF = 384
LAYERS = 2
MICRO = 4
SIDE = 16
EPSILON = 1e-05
MASKED_SCORE = -1000000000.0
LANES = 128
TILE = 256
CELLS = SIDE * LANES
DELEGATES = 512
PARAM_ROWS = 32
GRAD_ROWS = 1280
VALUE_PLACES = (768, 864, 1024)
f32 = jnp.float32
bf16 = jnp.bfloat16

NN = (((1,), (0,)), ((), ()))
NT = (((1,), (1,)), ((), ()))
TN = (((0,), (0,)), ((), ()))


def dot(a, b, dims=NN):
    return lax.dot_general(a, b, dims, preferred_element_type=f32)


def halves(v):
    high = v.astype(bf16)
    return high, (v - high.astype(f32)).astype(bf16)


def split(v):
    return jnp.concatenate(halves(v), axis=0)


def mapped(weight_pair, pair):
    both = dot(weight_pair, pair)
    count = both.shape[0] // 2
    return both[:count] + both[count:]


def joined(both):
    count = both.shape[0] // 2
    return both[:count] + both[count:]


def wide(v):
    return jnp.concatenate([v, v], axis=1)


def folded(v):
    return v[:, :LANES] + v[:, LANES:]


def normalized(v):
    centre = v - jnp.sum(v, axis=0, keepdims=True) * (1.0 / D)
    rate = lax.rsqrt(jnp.sum(centre * centre, axis=0, keepdims=True) * (1.0 / D) + EPSILON)
    return centre * rate, rate


def norm_pullback(dn, unit, rate):
    mean = jnp.sum(dn, axis=0, keepdims=True) * (1.0 / D)
    slope = jnp.sum(dn * unit, axis=0, keepdims=True) * (1.0 / D)
    return rate * (dn - mean - unit * slope)


def lane_iota(shape, dim):
    return lax.broadcasted_iota(jnp.int32, shape, dim)


def lane_slot(lane):
    return lane >> 4


def lane_row(lane):
    return lane & 15


def from_row_before(v, lane):
    return jnp.where(lane_row(lane) > 0, pltpu.roll(v, 1, 1), 0.0)


def from_row_after(v, lane):
    return jnp.where(lane_row(lane) < 15, pltpu.roll(v, LANES - 1, 1), 0.0)


def tile_at(j):
    return slice(j * TILE, (j + 1) * TILE)


def padded_tile_at(j):
    return slice(LANES + j * TILE, LANES + (j + 1) * TILE)


def lanes_at(j):
    return slice(j * LANES, (j + 1) * LANES)


def loop(count, body):
    for index in range(count):
        body(index)


def staggered(count, body, gap=1):
    running, index, step = [], 0, 0
    while index < count or running:
        if index < count and step % gap == 0:
            running.append(body(index))
            index += 1
        running = [part for part in running if next(part, "end") != "end"]
        step += 1


def prepare_weights(r, l):
    def left_pair(dst, w):
        n, k = w.shape
        high, low = halves(w)
        dst[0:n, 0:k] = high
        dst[0:n, k : 2 * k] = high
        dst[n : 2 * n, 0:k] = low
        dst[n : 2 * n, k : 2 * k] = low

    for name in ("first", "second", "mixer", "output", "expand"):
        w = getattr(r, name)[l]
        left_pair(getattr(r, name + "_t").at[l], jnp.transpose(w))
        left_pair(getattr(r, name + "_n").at[l], w)
    left_pair(r.reduce_t.at[l], r.reduce[l])
    left_pair(r.reduce_n.at[l], jnp.transpose(r.reduce[l]))
    r.rows[...] = jnp.zeros((PARAM_ROWS, LANES), f32)
    r.rows[0:4, 0:D] = r.gains[l]
    r.rows[4:16, 0:D] = r.biases[:, l]
    r.rows[16:25, 0:D] = r.depth[:, l]
    r.rows[25:29, 0:D] = r.spread[l]
    for t in range(3):
        r.rows[29 + t : 30 + t, :] = r.ebias[l : l + 1, t * LANES : (t + 1) * LANES]
    columns = jnp.transpose(r.rows[...])
    for k in range(29):
        r.par[l, k] = jnp.broadcast_to(columns[0:D, k : k + 1], (D, LANES))
    for t in range(3):
        r.epar[l, t * LANES : (t + 1) * LANES] = jnp.broadcast_to(
            columns[:, 29 + t : 30 + t], (LANES, LANES)
        )
    lane = lane_iota((D, LANES), 1)
    for b in range(2):
        r.taps[l, b] = jnp.where((lane & 1) == 0, r.par[l, 25 + b], r.par[l, 27 + b])
    r.acc[l] = jnp.zeros((27, D, LANES), f32)
    r.eacc[l] = jnp.zeros((FF, LANES), f32)


def prepare_masks(r, z):
    lane = lane_iota((8, LANES), 1)
    slot_ids = jnp.zeros((32, LANES), jnp.int32)
    slot_row = lane_iota((32, LANES), 0)
    batch = jnp.zeros((8, LANES), jnp.int32)
    row_batch = jnp.zeros((8, LANES), jnp.int32)
    for s in range(32):
        slot_ids = jnp.where(slot_row == s, r.slot_image[s], slot_ids)
        row_batch = jnp.where((lane >> 2) == s, r.slot_batch[s], row_batch)
    for s in range(8):
        batch = jnp.where(lane_slot(lane) == s, r.slot_batch[z * 8 + s], batch)
    slot_ids = jnp.concatenate([slot_ids] * 8, axis=1)
    chosen = (slot_ids == lane_iota((32, 1024), 1)).astype(f32).astype(bf16)
    sizes = jnp.concatenate([r.sizes[...].astype(f32), jnp.zeros((6, 1024), f32)], axis=0).astype(bf16)
    by_slot = dot(sizes, chosen, NT).astype(bf16)

    def placed(slots, count):
        found = (slots == lane_iota((32, count), 0)).astype(f32).astype(bf16)
        per_place = dot(by_slot, found)
        return (jnp.broadcast_to(per_place[k : k + 1], (8, count)) for k in range(2))

    height, width = placed(lane_slot(lane_iota((32, LANES), 1)) + z * 8, LANES)
    rows_in = lane_row(lane).astype(f32) < height
    for x in range(SIDE):
        r.mask[:, x * LANES : (x + 1) * LANES] = (rows_in & (width > float(x))).astype(f32)
    r.counts[...] = jnp.where(rows_in, width, 0.0)
    row_height, row_width = placed(lane_iota((32, LANES), 1) >> 2, LANES)
    row_count = jnp.where(((lane & 3) + z * 4).astype(f32) < row_height, row_width, 0.0)
    r.row_limit[...] = jnp.broadcast_to(jnp.transpose(row_count)[:, 0:1] * float(D), (LANES, LANES))
    micro = lane_iota((8, LANES), 0)
    upper = ((batch == micro) & (micro < MICRO)).astype(f32)
    lower = ((batch == micro - MICRO) & (micro >= MICRO)).astype(f32)
    zero = jnp.zeros((8, 6 * LANES), f32)
    both = jnp.concatenate([upper, lower], axis=1)
    summing = jnp.concatenate([upper] * 3 + [lower] * 3, axis=1)
    r.summing[...] = jnp.concatenate([summing, zero], axis=0).astype(bf16)
    r.placing[...] = jnp.concatenate([both] * 3 + [zero[:, 0:TILE]], axis=0).astype(bf16)
    upper = ((row_batch == micro) & (micro < MICRO)).astype(f32)
    lower = ((row_batch == micro - MICRO) & (micro >= MICRO)).astype(f32)
    r.row_onehot[0:8] = upper
    r.row_onehot[8:16] = lower
    r.row_counts[...] = jnp.broadcast_to(jnp.sum(upper * row_count, axis=1, keepdims=True), (8, LANES))
    for k, kind in enumerate((upper, lower)):
        r.row_columns[k] = jnp.transpose(jnp.concatenate([kind] * 4, axis=0)).astype(bf16)
    place = lane_iota((8, DELEGATES), 1)
    height, width = placed((lane_iota((32, DELEGATES), 1) >> 6) + z * 8, DELEGATES)
    inside = ((2 * (place & 7)).astype(f32) < height) & ((2 * ((place >> 3) & 7)).astype(f32) < width)
    inside = inside.astype(f32)
    key, query = lane_iota((LANES, LANES), 0), lane_iota((LANES, LANES), 1)
    for p in range(4):
        column = jnp.transpose(inside[:, p * LANES : (p + 1) * LANES])[:, 0:1]
        r.keep[p] = jnp.where((key >> 6) == (query >> 6), jnp.broadcast_to(column, (LANES, LANES)), 0.0)
    lane, place = lane_iota((LANES, DELEGATES), 0), lane_iota((LANES, DELEGATES), 1)
    same = ((place >> 6) == lane_slot(lane)) & ((place & 7) == (lane_row(lane) >> 1))
    for j in range(8):
        r.pool[j * LANES : (j + 1) * LANES] = (
            (same & (((place >> 3) & 7) == j)).astype(f32).astype(bf16)
        )


def take_rows(block, dst, mask):
    for k in range(12):
        at = slice(k * LANES, (k + 1) * LANES)
        rows = jnp.concatenate([block[z, s, :, at] for s in range(8) for z in range(4)], axis=0)
        turned = jnp.transpose(rows)
        for x in range(SIDE):
            lo, hi = max(k * LANES, x * D), min((k + 1) * LANES, (x + 1) * D)
            if lo < hi:
                part = turned[lo - k * LANES : hi - k * LANES]
                dst[lo - x * D : hi - x * D, x * LANES : (x + 1) * LANES] = (
                    part * mask[0:1, x * LANES : (x + 1) * LANES]
                )


def give_rows(src, block):
    for k in range(12):
        parts = []
        for x in range(SIDE):
            lo, hi = max(k * LANES, x * D), min((k + 1) * LANES, (x + 1) * D)
            if lo < hi:
                parts.append(src[lo - x * D : hi - x * D, x * LANES : (x + 1) * LANES])
        turned = jnp.transpose(jnp.concatenate(parts, axis=0))
        for s in range(8):
            for z in range(4):
                place = 4 * (4 * s + z)
                block[z, s, :, k * LANES : (k + 1) * LANES] = turned[place : place + 4]


def three_parts(v, axis=0):
    high, low = halves(v)
    rest = (v - high.astype(f32)) - low.astype(f32)
    return jnp.concatenate([high, low, rest.astype(bf16)], axis=axis)


def lane_sums(upper, lower, r):
    parts = jnp.concatenate([three_parts(upper, 1), three_parts(lower, 1)], axis=1)
    return dot(r.summing[...], parts, NT)[0:8]


def row_mask(r, at):
    lane = lane_iota((LANES, TILE), 1).astype(f32) + float(at)
    return lane < wide(r.row_limit[...])


def row_statistics(r):
    upper = jnp.concatenate([r.row_onehot[0:8]] * 3, axis=1).astype(bf16)
    lower = jnp.concatenate([r.row_onehot[8:16]] * 3, axis=1).astype(bf16)
    for k in range(6):
        at = slice(k * TILE, (k + 1) * TILE)
        v = jnp.where(row_mask(r, k * TILE), r.own[:, :, at].reshape(LANES, TILE), 0.0)
        r.row_sums[:, at] = dot(upper, three_parts(v)) + dot(lower, three_parts(v * v))
    total = r.row_sums[:, 0:D]
    for x in range(1, SIDE):
        total = total + r.row_sums[:, x * D : (x + 1) * D]
    return jnp.concatenate([total, r.row_counts[:, 0 : LANES - D]], axis=1)


def corrected_rows(r, out):
    for x in range(SIDE):
        r.row_sums[:, x * D : (x + 1) * D] = r.dstat_rows[:, 0:D]
    zero = jnp.zeros((8, TILE), bf16)
    for k in range(6):
        at = slice(k * TILE, (k + 1) * TILE)
        parts = jnp.concatenate([three_parts(r.row_sums[:, at]), zero], axis=0)
        dsums, dsquares = dot(r.row_columns[0], parts), dot(r.row_columns[1], parts)
        v = r.rows_in[0, :, :, :, at].reshape(LANES, TILE) + dsums + r.own[:, :, at].reshape(LANES, TILE) * dsquares
        out[:, :, at] = jnp.where(row_mask(r, k * TILE), v, 0.0).reshape(32, 4, TILE)


def statistics_partial(r):
    total = jnp.concatenate([r.sums[0], r.counts[...], jnp.zeros((24, LANES), f32)], axis=0)
    square = jnp.concatenate([r.sums[1], jnp.zeros((32, LANES), f32)], axis=0)
    return lane_sums(total, square, r)


def per_lane(upper, lower, r):
    parts = three_parts(jnp.concatenate([upper, lower], axis=0)).astype(f32)
    turned = jnp.transpose(jnp.concatenate([parts, jnp.zeros((8, LANES), f32)], axis=0)).astype(bf16)
    both = dot(turned, r.placing[...])
    return both[0:D, 0:LANES], both[0:D, LANES:]


def use_statistics(r, l, totals):
    count = totals[0:4, D : D + 1]
    centre = totals[0:4] / count
    variance = totals[4:8] / count - centre * centre
    rate = lax.rsqrt(variance + EPSILON)
    r.stat_rows[l, 0:4] = centre
    r.stat_rows[l, 4:8] = rate
    r.count_rows[...] = jnp.broadcast_to(count, (4, LANES))
    centre_lanes, rate_lanes = per_lane(centre, rate, r)
    r.centre[l] = centre_lanes
    r.rate[l] = rate_lanes


def use_statistics_grad(r, l, totals):
    centre, rate = r.stat_rows[l, 0:4], r.stat_rows[l, 4:8]
    count = r.count_rows[...]
    gain = jnp.concatenate([r.gains[l, 0:1], jnp.zeros((1, LANES - D), f32)], axis=1)
    dcentre = -rate * gain * totals[0:4]
    dvariance = -0.5 * rate * rate * rate * gain * totals[4:8]
    dsums = (dcentre - 2.0 * centre * dvariance) / count
    dsquares = dvariance / count
    r.dstat_rows[0:4] = dsums
    r.dstat_rows[4:8] = 2.0 * dsquares
    if l > 0:
        r.dstat[0], r.dstat[1] = per_lane(dsums, 2.0 * dsquares, r)


def forward_local(r, l):
    r.fmap[l, :, 0:LANES] = jnp.zeros((D, LANES), f32)
    r.fmap[l, :, LANES + CELLS :] = jnp.zeros((D, LANES), f32)

    def body(j):
        v = r.x[l, :, tile_at(j)]
        pair = split((v - wide(r.centre[l])) * wide(r.rate[l] * r.par[l, 0]) + wide(r.par[l, 4]))
        r.n2[l, :, tile_at(j)] = pair
        yield
        out = mapped(r.first_t[l], pair) + wide(r.par[l, 5])
        r.fmap[l, :, padded_tile_at(j)] = out * r.mask[0:1, tile_at(j)]
        yield
        yield
        pair = split(convolved(r, l, j))
        r.d2[l, :, tile_at(j)] = pair
        yield
        out = mapped(r.second_t[l], pair) + wide(r.par[l, 7])
        local = r.x[l, :, tile_at(j)] + out * r.mask[0:1, tile_at(j)]
        r.local[:, tile_at(j)] = local
        unit, rate = normalized(local)
        r.unit1[l, :, tile_at(j)] = unit
        r.rates[l, 0:1, tile_at(j)] = rate
        r.pooled[:, lanes_at(j)] = split(
            0.25 * folded(unit * wide(r.par[l, 1]) + wide(r.par[l, 8]))
        )

    staggered(8, body)


def convolved(r, l, j):
    lane = lane_iota((8, LANES), 1)
    groups = []
    for g in range(12):
        rows = slice(g * 8, (g + 1) * 8)
        taps = [r.par[l, 16 + t, rows, :] for t in range(9)]
        cells = [r.fmap[l, rows, (2 * j + x) * LANES : (2 * j + x + 1) * LANES] for x in range(4)]
        columns = []
        for x in range(2):
            sums = [sum(taps[3 * q + c] * cells[x + c] for c in range(3)) for q in range(3)]
            columns.append(
                r.par[l, 6, rows, :] + sums[1] + from_row_before(sums[0], lane) + from_row_after(sums[2], lane)
            )
        groups.append(jnp.concatenate(columns, axis=1))
    return jnp.concatenate(groups, axis=0)


def forward_mixer(r, l):
    forward_queries(r, l)
    forward_attention(r, l)
    forward_spread(r, l)


def forward_queries(r, l):
    delegates = joined(dot(r.pooled[...], r.pool[...]))
    pair = split(delegates)
    r.g2[l] = pair
    qkv = mapped(r.mixer_t[l], pair)
    queries, keys, values = qkv[0:D], qkv[D : 2 * D], qkv[2 * D :]
    for t in range(4):
        at = slice(t * LANES, (t + 1) * LANES)
        r.qkv[l, 0:D, at] = (queries[:, at] + r.par[l, 9]) * SCALE
        r.qkv[l, D : 2 * D, at] = keys[:, at]
        r.qkv[l, 2 * D :, at] = values[:, at] + r.par[l, 10]


def by_head(v):
    zero = jnp.zeros((HEAD, LANES), f32)
    return jnp.concatenate(
        [jnp.concatenate([v[0:HEAD], zero], axis=1), jnp.concatenate([zero, v[HEAD:]], axis=1)], axis=0
    )


def own_head(v):
    return jnp.concatenate([v[0:HEAD, 0:LANES], v[HEAD:, LANES:]], axis=0)


def left_rows(v):
    turned = jnp.transpose(jnp.concatenate([v, v], axis=0))
    return jnp.concatenate(halves(turned), axis=0)


def left_columns(v):
    high, low = halves(v)
    return jnp.concatenate(
        [jnp.concatenate([high, high], axis=1), jnp.concatenate([low, low], axis=1)], axis=0
    )


def column_product(a_pair, b_pair):
    both = joined(dot(a_pair, b_pair, NT))
    return folded(both)


HEAD = D // 2
SCALE = 1.0 / math.sqrt(HEAD)


def forward_attention(r, l):
    def body(p):
        at = slice(p * LANES, (p + 1) * LANES)
        q, k, v = (r.qkv[l, part * D : (part + 1) * D, at] for part in range(3))
        left, right = left_rows(k), split(by_head(q))
        yield
        scores = joined(dot(left, right))
        scores = jnp.where(wide(r.keep[p]) > 0.0, scores, MASKED_SCORE)
        yield
        weights = jnp.exp(scores - jnp.max(scores, axis=0, keepdims=True))
        probs = weights / jnp.sum(weights, axis=0, keepdims=True)
        r.probs[l, p] = probs
        yield
        r.mixture[:, at] = own_head(mapped(left_columns(v), split(probs)))

    staggered(4, body)


def forward_spread(r, l):
    r.mix2[...] = split(r.mixture[...])

    def spread(t):
        r.up[l, :, tile_at(t)] = joined(dot(r.mix2[...], r.pool[tile_at(t), :], NT))

    loop(4, spread)


def rest_forward(r, l, j):
    mask = r.mask[0:1, tile_at(j)]
    up = r.up[l, :, lanes_at(j)]
    spread = jnp.concatenate([up * r.taps[l, 0], up * r.taps[l, 1]], axis=1) + wide(r.par[l, 11])
    unit2, rate2 = normalized(spread)
    pair = split(unit2 * wide(r.par[l, 2]) + wide(r.par[l, 12]))
    r.s2[l, :, tile_at(j)] = pair
    yield
    middle = r.local[:, tile_at(j)] + mask * (mapped(r.output_t[l], pair) + wide(r.par[l, 13]))
    unit3, rate3 = normalized(middle)
    pair = split(unit3 * wide(r.par[l, 3]) + wide(r.par[l, 14]))
    r.e2[l, :, tile_at(j)] = pair
    yield
    before = mapped(r.expand_t[l], pair) + wide(r.epar[l])
    yield
    normal = 0.5 + 0.5 * lax.erf(before * math.sqrt(0.5))
    slope = normal + before * (jnp.exp(-0.5 * before * before) * (1.0 / math.sqrt(2.0 * math.pi)))
    hidden = split(before * normal)
    r.h2[l, :, tile_at(j)] = hidden
    yield
    out = middle + mask * (mapped(r.reduce_t[l], hidden) + wide(r.par[l, 15]))
    return out, unit2, rate2, unit3, rate3, slope


def rest_backward(r, l, j, dy, unit2, rate2, unit3, rate3, slope):
    def add(k, v):
        r.acc[l, k] += folded(v)

    pair = split(dy)
    r.dy2[:, tile_at(j)] = pair
    add(15, dy)
    yield
    dbefore = mapped(r.reduce_n[l], pair) * slope
    r.eacc[l] += folded(dbefore)
    pair = split(dbefore)
    r.dp2[:, tile_at(j)] = pair
    yield
    de = mapped(r.expand_n[l], pair)
    add(14, de)
    add(3, de * unit3)
    dmiddle = dy + norm_pullback(de * wide(r.par[l, 3]), unit3, rate3)
    r.local[:, tile_at(j)] = dmiddle
    add(13, dmiddle)
    pair = split(dmiddle)
    r.dm2[:, tile_at(j)] = pair
    yield
    ds = mapped(r.output_n[l], pair)
    add(12, ds)
    add(2, ds * unit2)
    dspread = norm_pullback(ds * wide(r.par[l, 2]), unit2, rate2)
    add(11, dspread)
    up = r.up[l, :, lanes_at(j)]
    r.acc[l, 25] += dspread[:, :LANES] * up
    r.acc[l, 26] += dspread[:, LANES:] * up
    r.pooled[:, lanes_at(j)] = split(
        dspread[:, :LANES] * r.taps[l, 0] + dspread[:, LANES:] * r.taps[l, 1]
    )


def forward_rest(r, l):
    def body(j):
        out, unit2, rate2, unit3, rate3, slope = yield from rest_forward(r, l, j)
        r.unit2[:, tile_at(j)] = unit2
        r.unit3[:, tile_at(j)] = unit3
        r.rates2[0:1, tile_at(j)] = rate2
        r.rates2[1:2, tile_at(j)] = rate3
        r.slope[:, tile_at(j)] = slope
        r.x[l + 1, :, tile_at(j)] = out
        r.sums[0] += folded(out)
        r.sums[1] += folded(out * out)

    r.sums[...] = jnp.zeros_like(r.sums)
    staggered(8, body)


def backward_rest(r, l):
    def body(j):
        yield from rest_backward(
            r, l, j, r.dy[:, tile_at(j)], r.unit2[:, tile_at(j)], r.rates2[0:1, tile_at(j)],
            r.unit3[:, tile_at(j)], r.rates2[1:2, tile_at(j)], r.slope[:, tile_at(j)],
        )

    staggered(8, body)


def turn_rest(r, l):
    def body(j):
        out, *kept = yield from rest_forward(r, l, j)
        r.temp[:, tile_at(j)] = out
        yield from rest_backward(r, l, j, r.dy[:, tile_at(j)], *kept)

    staggered(8, body)


def backward_mixer(r, l):
    backward_gather(r, l)
    backward_attention(r, l)
    backward_queries(r, l)
    backward_spread(r, l)


def backward_gather(r, l):
    r.mixture[...] = joined(dot(r.pooled[...], r.pool[...]))


def backward_attention(r, l):
    def body(p):
        at = slice(p * LANES, (p + 1) * LANES)
        q, k, v = (r.qkv[l, part * D : (part + 1) * D, at] for part in range(3))
        probs = r.probs[l, p]
        dout = split(by_head(r.mixture[:, at]))
        left = left_rows(v)
        yield
        dprobs = joined(dot(left, dout))
        yield
        dscores = split(probs * (dprobs - jnp.sum(probs * dprobs, axis=0, keepdims=True)))
        r.dqkv[2 * D :, at] = column_product(dout, split(probs))
        yield
        r.dqkv[0:D, at] = own_head(mapped(left_columns(k), dscores)) * SCALE
        r.dqkv[D : 2 * D, at] = column_product(split(by_head(q)), dscores)

    staggered(4, body)


def backward_queries(r, l):
    dqkv = r.dqkv[...]
    for t in range(4):
        at = slice(t * LANES, (t + 1) * LANES)
        r.acc[l, 9] += dqkv[0:D, at]
        r.acc[l, 10] += dqkv[2 * D :, at]
    pair = split(dqkv)
    r.dq2[...] = pair
    r.mix2[...] = split(mapped(r.mixer_n[l], pair))


def backward_spread(r, l):
    def spread(t):
        r.dup[:, tile_at(t)] = 0.25 * joined(dot(r.mix2[...], r.pool[tile_at(t), :], NT))

    loop(4, spread)


def shifted_maps(r):
    return r.dy, r.dmap.at[0], r.dmap.at[1]


def backward_local(r, l):
    lane = lane_iota((D, LANES), 1)
    for shifted in shifted_maps(r):
        shifted[:, 0:LANES] = jnp.zeros((D, LANES), f32)
        shifted[:, LANES + CELLS :] = jnp.zeros((D, LANES), f32)

    def add(k, v):
        r.acc[l, k] += folded(v)

    def body(j):
        dup = wide(r.dup[:, lanes_at(j)])
        unit = r.unit1[l, :, tile_at(j)]
        add(8, dup)
        add(1, dup * unit)
        dlocal = r.local[:, tile_at(j)] + norm_pullback(
            dup * wide(r.par[l, 1]), unit, r.rates[l, 0:1, tile_at(j)]
        )
        r.local[:, tile_at(j)] = dlocal
        add(7, dlocal)
        pair = split(dlocal)
        r.dl2[:, tile_at(j)] = pair
        yield
        out = mapped(r.second_n[l], pair)
        add(6, out)
        after, same, before = shifted_maps(r)
        same[:, padded_tile_at(j)] = out
        for x in range(2):
            column = out[:, x * LANES : (x + 1) * LANES]
            place = slice((2 * j + x + 1) * LANES, (2 * j + x + 2) * LANES)
            after[:, place] = from_row_after(column, lane)
            before[:, place] = from_row_before(column, lane)
        yield
        yield
        v = convolved_back(r, l, j) * r.mask[0:1, tile_at(j)]
        add(5, v)
        pair = split(v)
        r.df2[:, tile_at(j)] = pair
        yield
        dnormed = mapped(r.first_n[l], pair)
        r.temp[:, tile_at(j)] = dnormed
        r.acc[l, 4] += folded(dnormed)
        r.acc[l, 0] += folded(dnormed * (r.x[l, :, tile_at(j)] - wide(r.centre[l])))

    staggered(8, body)


def convolved_back(r, l, j):
    groups = []
    for g in range(12):
        rows = slice(g * 8, (g + 1) * 8)
        value = [r.fmap[l, rows, (2 * j + x + 1) * LANES : (2 * j + x + 2) * LANES] for x in range(2)]
        columns = [0.0, 0.0]
        for q, shifted in enumerate(shifted_maps(r)):
            source = [shifted[rows, (2 * j + x) * LANES : (2 * j + x + 1) * LANES] for x in range(4)]
            for c in range(3):
                tap = r.par[l, 16 + 3 * q + c, rows, :]
                for x in range(2):
                    columns[x] = columns[x] + tap * source[x + 2 - c]
                r.acc[l, 16 + 3 * q + c, rows, :] += sum(source[x + 2 - c] * value[x] for x in range(2))
        groups.append(jnp.concatenate(columns, axis=1))
    return jnp.concatenate(groups, axis=0)


def statistics_grad_partial(r, l):
    pad = jnp.zeros((LANES - D, LANES), f32)
    return lane_sums(
        jnp.concatenate([r.acc[l, 4], pad], axis=0), jnp.concatenate([r.acc[l, 0], pad], axis=0), r
    )


def backward_input(r, l):
    def body(j):
        v = r.x[l, :, tile_at(j)]
        r.dy[:, tile_at(j)] = (
            r.temp[:, tile_at(j)] * wide(r.rate[l] * r.par[l, 0])
            + r.local[:, tile_at(j)]
            + r.mask[0:1, tile_at(j)] * (wide(r.dstat[0]) + v * wide(r.dstat[1]))
        )

    loop(8, body)


def partial_input(r, l):
    def body(j):
        r.dy[:, tile_at(j)] = (
            r.temp[:, tile_at(j)] * wide(r.rate[l] * r.par[l, 0]) + r.local[:, tile_at(j)]
        )

    loop(8, body)


def big_product(r, l, a, b, place):
    both = joined(dot(a, b, NT))
    both = both[:, 0:D] + both[:, D:]
    for t in range(3):
        r.grads[l, place + t * D : place + (t + 1) * D] = jnp.transpose(both[t * LANES : (t + 1) * LANES])


def small_product(a, b):
    both = joined(dot(a, b, NT))
    return both[:, 0:D] + both[:, D:]


def feed_forward_grads(r, l):
    big_product(r, l, r.dp2[...], r.e2[l], 0)
    big_product(r, l, r.h2[l], r.dy2[...], 288)
    r.grads[l, 576:672, 0:D] = small_product(r.s2[l], r.dm2[...])


def mixer_grads(r, l):
    queries, keys, values = (
        small_product(
            r.g2[l], jnp.concatenate([r.dq2[t * D : (t + 1) * D], r.dq2[(3 + t) * D : (4 + t) * D]], axis=0)
        )
        for t in range(3)
    )
    r.grads[l, 768:864, 0:D] = queries
    r.grads[l, 864:960, 0:D] = keys
    for t, place in enumerate(VALUE_PLACES):
        r.grads[l, place : place + D, D:] = values[:, t * 32 : (t + 1) * 32]


def local_grads(r, l):
    r.grads[l, 1024:1120, 0:D] = small_product(r.n2[l], r.df2[...])
    r.grads[l, 1120:1216, 0:D] = small_product(r.d2[l], r.dl2[...])


def vector_grads(r, l):
    r.acc[l, 0] = r.acc[l, 0] * r.rate[l]
    ones = jnp.ones((8, TILE), f32)
    even = ((lane_iota((8, TILE), 1) & 1) == 0).astype(f32)
    odd = (ones - even).astype(bf16)
    ones, even = ones.astype(bf16), even.astype(bf16)

    def row(kind, v, place, count):
        total = dot(kind, jnp.concatenate(halves(v), axis=1), NT)
        r.grads[l, 1216 + place : 1217 + place, 0:count] = total[0:1]

    for k in range(25):
        row(ones, r.acc[l, k], k, D)
    for b in range(2):
        row(even, r.acc[l, 25 + b], 25 + b, D)
        row(odd, r.acc[l, 25 + b], 27 + b, D)
    for t in range(3):
        row(ones, r.eacc[l, t * LANES : (t + 1) * LANES], 29 + t, LANES)


def weight_grads(r, l):
    feed_forward_grads(r, l)
    mixer_grads(r, l)
    local_grads(r, l)
    vector_grads(r, l)


def scratch_list():
    L = LAYERS
    v = pltpu.VMEM
    return [
        ("first_t", v((L, 192, 192), bf16)),
        ("first_n", v((L, 192, 192), bf16)),
        ("second_t", v((L, 192, 192), bf16)),
        ("second_n", v((L, 192, 192), bf16)),
        ("mixer_t", v((L, 576, 192), bf16)),
        ("mixer_n", v((L, 192, 576), bf16)),
        ("output_t", v((L, 192, 192), bf16)),
        ("output_n", v((L, 192, 192), bf16)),
        ("expand_t", v((L, 768, 192), bf16)),
        ("expand_n", v((L, 192, 768), bf16)),
        ("reduce_t", v((L, 192, 768), bf16)),
        ("reduce_n", v((L, 768, 192), bf16)),
        ("rows", v((PARAM_ROWS, LANES), f32)),
        ("par", v((L, 29, D, LANES), f32)),
        ("epar", v((L, FF, LANES), f32)),
        ("taps", v((L, 2, D, LANES), f32)),
        ("acc", v((L, 27, D, LANES), f32)),
        ("eacc", v((L, FF, LANES), f32)),
        ("mask", v((8, CELLS), f32)),
        ("counts", v((8, LANES), f32)),
        ("summing", v((16, 6 * LANES), bf16)),
        ("placing", v((32, TILE), bf16)),
        ("keep", v((4, LANES, LANES), f32)),
        ("pool", v((8 * LANES, DELEGATES), bf16)),
        ("sums", v((2, D, LANES), f32)),
        ("own", v((32, 4, SIDE * D), f32)),
        ("row_limit", v((LANES, LANES), f32)),
        ("row_onehot", v((16, LANES), f32)),
        ("row_counts", v((8, LANES), f32)),
        ("row_columns", v((2, LANES, 32), bf16)),
        ("row_sums", v((8, SIDE * D), f32)),
        ("dstat_rows", v((8, LANES), f32)),
        ("stat_rows", v((L, 8, LANES), f32)),
        ("count_rows", v((4, LANES), f32)),
        ("centre", v((L, D, LANES), f32)),
        ("rate", v((L, D, LANES), f32)),
        ("dstat", v((2, D, LANES), f32)),
        ("x", v((L, D, CELLS), f32)),
        ("n2", v((L, 2 * D, CELLS), bf16)),
        ("fmap", v((L, D, CELLS + 2 * LANES), f32)),
        ("temp", v((D, CELLS), f32)),
        ("d2", v((L, 2 * D, CELLS), bf16)),
        ("local", v((D, CELLS), f32)),
        ("unit1", v((L, D, CELLS), f32)),
        ("rates", v((L, 1, CELLS), f32)),
        ("pooled", v((2 * D, 8 * LANES), bf16)),
        ("g2", v((L, 2 * D, DELEGATES), bf16)),
        ("qkv", v((L, 3 * D, DELEGATES), f32)),
        ("probs", v((L, 4, LANES, TILE), f32)),
        ("mixture", v((D, DELEGATES), f32)),
        ("mix2", v((2 * D, DELEGATES), bf16)),
        ("up", v((L, D, 8 * LANES), f32)),
        ("unit2", v((D, CELLS), f32)),
        ("s2", v((L, 2 * D, CELLS), bf16)),
        ("unit3", v((D, CELLS), f32)),
        ("rates2", v((8, CELLS), f32)),
        ("e2", v((L, 2 * D, CELLS), bf16)),
        ("slope", v((FF, CELLS), f32)),
        ("h2", v((L, 2 * FF, CELLS), bf16)),
        ("dy", v((D, CELLS + 2 * LANES), f32)),
        ("dy2", v((2 * D, CELLS), bf16)),
        ("dp2", v((2 * FF, CELLS), bf16)),
        ("dm2", v((2 * D, CELLS), bf16)),
        ("dqkv", v((3 * D, DELEGATES), f32)),
        ("dq2", v((6 * D, DELEGATES), bf16)),
        ("dup", v((D, 8 * LANES), f32)),
        ("dl2", v((2 * D, CELLS), bf16)),
        ("dmap", v((2, D, CELLS + 2 * LANES), f32)),
        ("df2", v((2 * D, CELLS), bf16)),
        ("grads", v((L, GRAD_ROWS, LANES), f32)),
    ]


PARAMS = (
    "gains", "biases", "depth", "spread", "first", "second", "mixer", "output", "expand", "ebias", "reduce",
)

OTHERS = 15
GROUP = 7
STEPS = sorted(
    [(x, y) for x in range(4) for y in range(4) if x + y > 0],
    key=lambda step: -min(step[0], 4 - step[0]) - min(step[1], 4 - step[1]),
)
PARCELS = ((0, 0, 768), (1, 0, 1280), (0, 768, 256), (0, 1024, 256))


class Place:
    def __init__(self):
        dp = lax.axis_index("dp")
        self.z = lax.axis_index("segment")
        self.core = lax.rem(dp, 2)
        self.chip = lax.div(dp, 2)
        self.member = self.z * 2 + self.core

    def chip_at(self, d):
        x, y = STEPS[d - 1]
        return lax.rem(lax.div(self.chip, 4) + x, 4) * 4 + lax.rem(lax.rem(self.chip, 4) + y, 4)

    def chip_after(self, d):
        return (self.z, self.chip_at(d) * 2 + self.core)

    def member_after(self, d):
        member = lax.rem(self.member + d, 8)
        return (lax.div(member, 2), self.chip * 2 + lax.rem(member, 2))

    def z_after(self, d):
        return (lax.rem(self.z + d, 4), self.chip * 2 + self.core)

    def sibling(self):
        return (self.z, self.chip * 2 + 1 - self.core)


def remote(src, dst, sends, receives, index, device):
    return pltpu.make_async_remote_copy(
        src_ref=src,
        dst_ref=dst,
        send_sem=sends.at[index],
        recv_sem=receives.at[index],
        device_id=device,
        device_id_type=pl.DeviceIdType.MESH,
    )


def greet(me):
    barrier = pltpu.get_barrier_semaphore()
    for d in range(1, 16):
        pl.semaphore_signal(barrier, inc=1, device_id=me.chip_after(d), device_id_type=pl.DeviceIdType.MESH)
    for d in range(1, 8):
        pl.semaphore_signal(barrier, inc=1, device_id=me.member_after(d), device_id_type=pl.DeviceIdType.MESH)
    return barrier


class RowsIn:
    def __init__(self, r, me, src, dst, number):
        self.own = pltpu.make_async_copy(src.at[pl.ds(me.z * 8, 8)], dst.at[me.z], r.row_own.at[number])
        self.copies = [
            remote(
                src.at[pl.ds(lax.rem(me.z + d, 4) * 8, 8)], dst.at[me.z],
                r.row_send, r.row_recv, (number, d), me.z_after(d),
            )
            for d in range(1, 4)
        ]

    def start(self):
        for copy in self.copies:
            copy.start()
        self.own.start()

    def wait(self):
        self.own.wait()
        for copy in self.copies:
            copy.wait()


class RowsOut(RowsIn):
    def __init__(self, r, me, src, dst, number):
        self.own = pltpu.make_async_copy(src.at[me.z], dst, r.row_own.at[number])
        self.copies = [
            remote(
                src.at[lax.rem(me.z + d, 4)], dst,
                r.row_send, r.row_recv, (number, d), me.z_after(d),
            )
            for d in range(1, 4)
        ]


class SmallSum:
    def __init__(self, r, me, number):
        self.r, self.me, self.number = r, me, number
        mine = r.chip_parts.at[number, me.chip]
        self.first = [
            remote(mine, mine, r.chip_send, r.chip_recv, (number, d), me.chip_after(d)) for d in range(1, 16)
        ]
        mine = r.group_parts.at[number, me.member]
        self.second = [
            remote(mine, mine, r.group_send, r.group_recv, (number, d), me.member_after(d))
            for d in range(1, 8)
        ]

    def put(self, value):
        self.r.chip_parts[self.number, self.me.chip] = value

    def start(self):
        for copy in self.first:
            copy.start()

    def step(self):
        for copy in self.first:
            copy.wait()
        total = self.r.chip_parts[self.number, 0]
        for k in range(1, 16):
            total = total + self.r.chip_parts[self.number, k]
        self.r.group_parts[self.number, self.me.member] = total
        for copy in self.second:
            copy.start()

    def finish(self):
        for copy in self.second:
            copy.wait()
        total = self.r.group_parts[self.number, 0]
        for k in range(1, 8):
            total = total + self.r.group_parts[self.number, k]
        return total


class WeightSum:
    def __init__(self, r, me, number):
        self.r, self.me, self.number = r, me, number
        layer, start, rows = PARCELS[number]
        count, size = rows // 2, rows // 32
        grads, totals = r.grads.at[layer], r.totals.at[layer]
        self.half, self.parts, self.planes = (
            getattr(r, kind + str(number)) for kind in ("half", "parts", "planes")
        )

        def half_of(core):
            return pl.ds(pl.multiple_of(start + core * count, 8), count)

        def piece_of(chip):
            return pl.ds(pl.multiple_of(chip * size, 8), size)

        self.mine = grads.at[half_of(me.core)]
        self.own_piece = self.half.at[piece_of(me.chip)]
        self.halves = remote(
            grads.at[half_of(1 - me.core)], self.half, r.half_send, r.half_recv, (number, 0), me.sibling()
        )
        self.pieces = [
            remote(
                self.half.at[piece_of(me.chip_at(d))], self.parts.at[me.chip],
                r.piece_send, r.piece_recv, (number, 0, d), me.chip_after(d),
            )
            for d in range(1, 16)
        ]
        plane = self.planes.at[me.z]
        self.exchange = [
            remote(plane, plane, r.plane_send, r.plane_recv, (number, d), me.z_after(d)) for d in range(1, 4)
        ]
        self.total = totals.at[pl.ds(pl.multiple_of(start + me.core * count + me.chip * size, 8), size)]
        self.gathers = [
            remote(self.total, self.total, r.piece_send, r.piece_recv, (number, 1, d), me.chip_after(d))
            for d in range(1, 16)
        ]
        whole = totals.at[half_of(me.core)]
        self.last = remote(whole, whole, r.half_send, r.half_recv, (number, 1), me.sibling())

    def step(self, number):
        me = self.me
        if number == 0:
            self.halves.start()
        elif number == 1:
            self.halves.wait()
            self.half[...] = self.half[...] + self.mine[...]
            self.parts[me.chip] = self.own_piece[...]
            for copy in self.pieces:
                copy.start()
        elif number == 2:
            for copy in self.pieces:
                copy.wait()
            total = self.parts[0]
            for k in range(1, 16):
                total = total + self.parts[k]
            self.planes[me.z] = total
            for copy in self.exchange:
                copy.start()
        elif number == 3:
            for copy in self.exchange:
                copy.wait()
            self.total[...] = (self.planes[0] + self.planes[1]) + (self.planes[2] + self.planes[3])
            for copy in self.gathers:
                copy.start()
        elif number == 4:
            for copy in self.gathers:
                copy.wait()
            self.last.start()
        else:
            self.last.wait()


class DirectSum:
    def __init__(self, r, me, number):
        self.me = me
        layer, start, rows = PARCELS[number]
        size = rows // 16
        self.parts, self.groups = (getattr(r, kind + str(number)) for kind in ("parts", "groups"))

        def piece_of(chip):
            return pl.ds(pl.multiple_of(start + chip * size, 8), size)

        self.mine = r.grads.at[layer, piece_of(me.chip)]
        self.pieces = [
            remote(
                r.grads.at[layer, piece_of(me.chip_at(d))], self.parts.at[me.chip],
                r.piece_send, r.piece_recv, (number, 0, d), me.chip_after(d),
            )
            for d in range(1, 16)
        ]
        group = self.groups.at[me.member]
        self.exchange = [
            remote(group, group, r.member_send, r.member_recv, (number, d), me.member_after(d))
            for d in range(1, 8)
        ]
        self.total = r.totals.at[layer, piece_of(me.chip)]
        self.gathers = [
            remote(self.total, self.total, r.piece_send, r.piece_recv, (number, 1, d), me.chip_after(d))
            for d in range(1, 16)
        ]

    def step(self, number):
        if number == 0:
            for copy in self.pieces:
                copy.start()
            self.parts[self.me.chip] = self.mine[...]
        elif number == 1:
            for copy in self.pieces:
                copy.wait()
            total = self.parts[0]
            for k in range(1, 16):
                total = total + self.parts[k]
            self.groups[self.me.member] = total
            for copy in self.exchange:
                copy.start()
        elif number == 2:
            for copy in self.exchange:
                copy.wait()
            total = self.groups[0]
            for k in range(1, 8):
                total = total + self.groups[k]
            self.total[...] = total
            for copy in self.gathers:
                copy.start()
        else:
            for copy in self.gathers:
                copy.wait()


def comm_scratch():
    L = LAYERS
    v = pltpu.VMEM
    s = pltpu.SemaphoreType.DMA
    return [
        ("rows_in", v((2, 4, 8, 4, SIDE * D), f32)),
        ("chip_parts", v((4, 16, 8, LANES), f32)),
        ("group_parts", v((4, 8, 8, LANES), f32)),
        ("totals", v((L, GRAD_ROWS, LANES), f32)),
        ("row_own", s((5,))),
        ("row_send", s((4, 4))),
        ("row_recv", s((4, 4))),
        ("chip_send", s((4, 16))),
        ("chip_recv", s((4, 16))),
        ("group_send", s((4, 8))),
        ("group_recv", s((4, 8))),
        ("half_send", s((len(PARCELS), 2))),
        ("half_recv", s((len(PARCELS), 2))),
        ("piece_send", s((len(PARCELS), 2, 16))),
        ("piece_recv", s((len(PARCELS), 2, 16))),
        ("plane_send", s((len(PARCELS), 4))),
        ("plane_recv", s((len(PARCELS), 4))),
        ("member_send", s((len(PARCELS), 8))),
        ("member_recv", s((len(PARCELS), 8))),
        ("out_sem", s((2,))),
        ("param_sem", s((12,))),
    ] + [
        (kind + str(number), v(lead + (PARCELS[number][2] // share, LANES), f32))
        for number in range(2)
        for kind, lead, share in (("half", (), 2), ("parts", (16,), 32), ("planes", (4,), 32))
    ] + [
        (kind + str(number), v((count, PARCELS[number][2] // 16, LANES), f32))
        for number in range(2, 4)
        for kind, count in (("parts", 16), ("groups", 8))
    ]


def layers_kernel(names, *refs):
    r = SimpleNamespace(**dict(zip(names, refs)))
    me = Place()
    barrier = greet(me)
    own_rows = pltpu.make_async_copy(r.tokens, r.own, r.row_own.at[4])
    loads = [
        pltpu.make_async_copy(getattr(r, name + "_in"), getattr(r, name), r.param_sem.at[k])
        for k, name in enumerate(("sizes",) + PARAMS)
    ]
    loads[0].start()
    own_rows.start()
    for load in loads[1:]:
        load.start()
    mine = pl.ds(me.z * 8, 8)
    tokens_in = RowsIn(r, me, r.tokens, r.rows_in.at[0], 0)
    upstream_in = RowsIn(r, me, r.cotangent, r.rows_in.at[1], 1)
    act_out = RowsOut(r, me, r.rows_in.at[0], r.act.at[mine], 2)
    grad_out = RowsOut(r, me, r.rows_in.at[1], r.rows_in.at[0, me.z], 3)
    sums = [SmallSum(r, me, number) for number in range(4)]
    outer, early = (WeightSum(r, me, number) for number in range(2))
    inner, last = (DirectSum(r, me, number) for number in range(2, 4))

    def run(work):
        pl.when(me.z >= 0)(work)

    loads[0].wait()

    @run
    def masks():
        prepare_masks(r, me.z)

    own_rows.wait()

    @run
    def first_statistics():
        sums[0].put(row_statistics(r))

    pl.semaphore_wait(barrier, OTHERS + GROUP)
    tokens_in.start()
    sums[0].start()
    for load in loads[1:]:
        load.wait()

    @run
    def first_weights():
        prepare_weights(r, 0)
        r.grads[...] = jnp.zeros_like(r.grads)

    sums[0].step()
    tokens_in.wait()
    upstream_in.start()

    @run
    def tokens():
        take_rows(r.rows_in.at[0], r.x.at[0], r.mask)

    use_statistics(r, 0, sums[0].finish())

    @run
    def first_layer():
        forward_local(r, 0)
        forward_mixer(r, 0)
        forward_rest(r, 0)
        sums[1].put(statistics_partial(r))

    sums[1].start()

    @run
    def second_weights():
        prepare_weights(r, 1)

    sums[1].step()
    upstream_in.wait()

    @run
    def upstream():
        take_rows(r.rows_in.at[1], r.dy, r.mask)

    use_statistics(r, 1, sums[1].finish())

    @run
    def second_layer():
        forward_local(r, 1)
        forward_mixer(r, 1)
        turn_rest(r, 1)
        give_rows(r.temp, r.rows_in.at[0])

    act_out.start()

    @run
    def second_backward():
        backward_mixer(r, 1)
        backward_local(r, 1)
        sums[2].put(statistics_grad_partial(r, 1))

    sums[2].start()

    @run
    def second_products():
        feed_forward_grads(r, 1)
        mixer_grads(r, 1)

    act_out.wait()
    sums[2].step()

    @run
    def second_local_products():
        local_grads(r, 1)
        vector_grads(r, 1)

    early.step(0)
    use_statistics_grad(r, 1, sums[2].finish())

    @run
    def between():
        backward_input(r, 1)

    early.step(1)

    @run
    def first_backward():
        backward_rest(r, 0)
        feed_forward_grads(r, 0)

    outer.step(0)

    @run
    def first_attention():
        backward_gather(r, 0)
        backward_attention(r, 0)

    outer.step(1)
    early.step(2)

    @run
    def first_mixer():
        backward_queries(r, 0)
        backward_spread(r, 0)
        mixer_grads(r, 0)

    inner.step(0)

    @run
    def first_local_backward():
        backward_local(r, 0)
        sums[3].put(statistics_grad_partial(r, 0))

    sums[3].start()

    @run
    def first_local_products():
        local_grads(r, 0)
        vector_grads(r, 0)

    last.step(0)

    @run
    def input_grad():
        partial_input(r, 0)
        give_rows(r.dy, r.rows_in.at[1])

    grad_out.start()
    early.step(3)
    inner.step(1)
    outer.step(2)
    sums[3].step()
    last.step(1)
    inner.step(2)
    outer.step(3)
    use_statistics_grad(r, 0, sums[3].finish())
    last.step(2)
    early.step(4)
    grad_out.wait()

    @run
    def correction():
        corrected_rows(r, r.own)

    copy = pltpu.make_async_copy(r.own, r.grad, r.out_sem.at[0])
    copy.start()
    inner.step(3)
    early.step(5)
    outer.step(4)
    last.step(3)
    outer.step(5)
    totals = pltpu.make_async_copy(r.totals, r.grad_sums, r.out_sem.at[1])
    totals.start()
    copy.wait()
    totals.wait()


def unpack_kernel(act_in, grad_in, totals_in, act, grad, *refs):
    count = len(PARAMS)
    outs, parts, (rows, totals, sems) = refs[:count], refs[count : 2 * count], refs[2 * count :]
    loads = [
        pltpu.make_async_copy(src, dst, sems.at[0, k])
        for k, (src, dst) in enumerate(
            ((totals_in.at[0], totals.at[0]), (totals_in.at[1], totals.at[1]), (act_in, rows.at[0]),
             (grad_in, rows.at[1]))
        )
    ]
    stores = [
        pltpu.make_async_copy(src, dst, sems.at[1, k])
        for k, (src, dst) in enumerate(
            ((rows.at[0], act), (rows.at[1], grad)) + tuple(zip(parts, outs))
        )
    ]
    for load in loads:
        load.start()
    gains, biases, depth, spread, first, second, mixer, output, expand, ebias, reduce = parts
    for l in range(LAYERS):
        loads[l].wait()

        def taken(place, count, width=D, start=0):
            return totals[l, place : place + count, start : start + width]

        gains[l] = taken(1216, 4)
        biases[:, l] = taken(1220, 12)
        depth[:, l] = taken(1232, 9)
        spread[l] = taken(1241, 4)
        first[l] = taken(1024, D)
        second[l] = taken(1120, D)
        output[l] = taken(576, D)
        mixer[l, :, 0:D] = taken(768, D)
        mixer[l, :, D : 2 * D] = taken(864, D)
        for t, place in enumerate(VALUE_PLACES):
            mixer[l, :, 2 * D + t * 32 : 2 * D + (t + 1) * 32] = taken(place, D, 32, D)
        for t in range(3):
            at = slice(t * LANES, (t + 1) * LANES)
            expand[l, :, at] = taken(t * D, D, LANES)
            reduce[l, :, at] = taken(288 + t * D, D, LANES)
            ebias[l : l + 1, at] = taken(1245 + t, 1, LANES)
    for store in stores[2:]:
        store.start()
    for load, store in zip(loads[2:], stores[:2]):
        load.wait()
        store.start()
    for store in stores:
        store.wait()


def turned(params):
    gains, biases, depth, spread, *maps, ebias, reduce = params
    return (gains, jnp.swapaxes(biases, 0, 1), jnp.swapaxes(depth, 0, 1), spread, *maps, ebias,
            jnp.swapaxes(reduce, 1, 2))


def shards(tokens, cotangent, image_size, slot_image, slot_batch, *params):
    params = turned(params)
    sizes = image_size.T
    scratch = scratch_list() + comm_scratch()
    scratch += [
        (name, pltpu.VMEM(p.shape, p.dtype)) for name, p in zip(("sizes",) + PARAMS, (sizes,) + params)
    ]
    ins = ("tokens", "cotangent", "slot_image", "slot_batch", "sizes_in")
    ins += tuple(name + "_in" for name in PARAMS)
    outs = ("act", "grad", "grad_sums")
    names = ins + outs + tuple(name for name, _ in scratch)
    anywhere = pl.BlockSpec(memory_space=pl.ANY)
    smem = pl.BlockSpec(memory_space=pltpu.SMEM)
    rows = jax.ShapeDtypeStruct(tokens.shape, f32)
    act, grad, totals = pl.pallas_call(
        functools.partial(layers_kernel, names),
        out_shape=[rows, rows, jax.ShapeDtypeStruct((LAYERS, GRAD_ROWS, LANES), f32)],
        in_specs=[anywhere, anywhere, smem, smem, anywhere] + [anywhere] * len(params),
        out_specs=[anywhere] * 3,
        scratch_shapes=[shape for _, shape in scratch],
        compiler_params=pltpu.CompilerParams(
            collective_id=0, has_side_effects=True, vmem_limit_bytes=63 * 2**20
        ),
        name="layers",
    )(tokens, cotangent, slot_image, slot_batch, sizes, *params)
    act, grad, *grads = pl.pallas_call(
        unpack_kernel,
        out_shape=[rows, rows] + [jax.ShapeDtypeStruct(p.shape, f32) for p in params],
        in_specs=[anywhere] * 3,
        out_specs=[anywhere] * (2 + len(params)),
        scratch_shapes=[pltpu.VMEM(p.shape, f32) for p in params]
        + [
            pltpu.VMEM((2,) + tokens.shape, f32),
            pltpu.VMEM(totals.shape, f32),
            pltpu.SemaphoreType.DMA((2, 2 + len(params))),
        ],
        compiler_params=pltpu.CompilerParams(vmem_limit_bytes=60 * 2**20),
        name="unpack",
    )(act, grad, totals)
    return (act, grad) + turned(grads)


def solution(mesh):
    rows = P("dp", "segment", None)
    return jax.shard_map(
        shards,
        mesh=mesh,
        in_specs=(rows, rows, P(), P("dp"), P("dp")) + (P(),) * len(PARAMS),
        out_specs=(rows, rows) + (P(),) * len(PARAMS),
        check_vma=False,
    )
```

```python
import functools
import math
from types import SimpleNamespace

import jax
import jax.numpy as jnp
from jax import lax
from jax.experimental import pallas as pl
from jax.experimental.pallas import tpu as pltpu
from jax.sharding import PartitionSpec as P

D = 96
FF = 384
LAYERS = 2
MICRO = 4
SIDE = 16
EPSILON = 1e-05
MASKED_SCORE = -1000000000.0
LANES = 128
TILE = 256
CELLS = SIDE * LANES
DELEGATES = 512
PARAM_ROWS = 32
GRAD_ROWS = 1280
VALUE_PLACES = (768, 864, 1024)
f32 = jnp.float32
bf16 = jnp.bfloat16

NN = (((1,), (0,)), ((), ()))
NT = (((1,), (1,)), ((), ()))
TN = (((0,), (0,)), ((), ()))


def dot(a, b, dims=NN):
    return lax.dot_general(a, b, dims, preferred_element_type=f32)


def halves(v):
    high = v.astype(bf16)
    return high, (v - high.astype(f32)).astype(bf16)


def split(v):
    return jnp.concatenate(halves(v), axis=0)


def mapped(weight_pair, pair):
    both = dot(weight_pair, pair)
    count = both.shape[0] // 2
    return both[:count] + both[count:]


def joined(both):
    count = both.shape[0] // 2
    return both[:count] + both[count:]


def wide(v):
    return jnp.concatenate([v, v], axis=1)


def folded(v):
    return v[:, :LANES] + v[:, LANES:]


def normalized(v):
    centre = v - jnp.sum(v, axis=0, keepdims=True) * (1.0 / D)
    rate = lax.rsqrt(jnp.sum(centre * centre, axis=0, keepdims=True) * (1.0 / D) + EPSILON)
    return centre * rate, rate


def norm_pullback(dn, unit, rate):
    mean = jnp.sum(dn, axis=0, keepdims=True) * (1.0 / D)
    slope = jnp.sum(dn * unit, axis=0, keepdims=True) * (1.0 / D)
    return rate * (dn - mean - unit * slope)


def lane_iota(shape, dim):
    return lax.broadcasted_iota(jnp.int32, shape, dim)


def lane_slot(lane):
    return lane >> 4


def lane_row(lane):
    return lane & 15


def from_row_before(v, lane):
    return jnp.where(lane_row(lane) > 0, pltpu.roll(v, 1, 1), 0.0)


def from_row_after(v, lane):
    return jnp.where(lane_row(lane) < 15, pltpu.roll(v, LANES - 1, 1), 0.0)


def tile_at(j):
    return slice(j * TILE, (j + 1) * TILE)


def padded_tile_at(j):
    return slice(LANES + j * TILE, LANES + (j + 1) * TILE)


def lanes_at(j):
    return slice(j * LANES, (j + 1) * LANES)


def loop(count, body):
    for index in range(count):
        body(index)


def counted(start, stop, body):
    def step(index, carry):
        body(index)
        return carry

    lax.fori_loop(start, stop, step, 0)


def staggered(count, body, gap=1):
    running, index, step = [], 0, 0
    while index < count or running:
        if index < count and step % gap == 0:
            running.append(body(index))
            index += 1
        running = [part for part in running if next(part, "end") != "end"]
        step += 1


def prepare_weights(r, l):
    def left_pair(dst, w):
        n, k = w.shape
        high, low = halves(w)
        dst[0:n, 0:k] = high
        dst[0:n, k : 2 * k] = high
        dst[n : 2 * n, 0:k] = low
        dst[n : 2 * n, k : 2 * k] = low

    for name in ("first", "second", "mixer", "output", "expand"):
        w = getattr(r, name)[l]
        left_pair(getattr(r, name + "_t").at[l], jnp.transpose(w))
        left_pair(getattr(r, name + "_n").at[l], w)
    left_pair(r.reduce_t.at[l], r.reduce[l])
    left_pair(r.reduce_n.at[l], jnp.transpose(r.reduce[l]))
    r.rows[...] = jnp.zeros((PARAM_ROWS, LANES), f32)
    r.rows[0:4, 0:D] = r.gains[l]
    r.rows[4:16, 0:D] = jnp.where(l == 0, r.biases[:, 0], r.biases[:, 1])
    r.rows[16:25, 0:D] = jnp.where(l == 0, r.depth[:, 0], r.depth[:, 1])
    r.rows[25:29, 0:D] = r.spread[l]
    for t in range(3):
        at = slice(t * LANES, (t + 1) * LANES)
        r.rows[29 + t : 30 + t, :] = jnp.where(l == 0, r.ebias[0:1, at], r.ebias[1:2, at])
    columns = jnp.transpose(r.rows[...])
    for k in range(29):
        r.par[l, k] = jnp.broadcast_to(columns[0:D, k : k + 1], (D, LANES))
    for t in range(3):
        r.epar[l, t * LANES : (t + 1) * LANES] = jnp.broadcast_to(
            columns[:, 29 + t : 30 + t], (LANES, LANES)
        )
    lane = lane_iota((D, LANES), 1)
    for b in range(2):
        r.taps[l, b] = jnp.where((lane & 1) == 0, r.par[l, 25 + b], r.par[l, 27 + b])
    r.acc[l] = jnp.zeros((27, D, LANES), f32)
    r.eacc[l] = jnp.zeros((FF, LANES), f32)


def placed(r, slots):
    found = (slots == lane_iota(slots.shape, 0)).astype(f32).astype(bf16)
    per_place = dot(r.by_slot[...].astype(bf16), found)
    return (jnp.broadcast_to(per_place[k : k + 1], (8, slots.shape[1])) for k in range(2))


def one_hots(batch):
    micro = lane_iota((8, LANES), 0)
    upper = ((batch == micro) & (micro < MICRO)).astype(f32)
    lower = ((batch == micro - MICRO) & (micro >= MICRO)).astype(f32)
    return upper, lower


def prepare_rows(r, z):
    lane = lane_iota((8, LANES), 1)
    slot_ids = jnp.zeros((32, LANES), jnp.int32)
    slot_row = lane_iota((32, LANES), 0)
    batch = jnp.zeros((8, LANES), jnp.int32)
    for s in range(32):
        slot_ids = jnp.where(slot_row == s, r.slot_image[s], slot_ids)
        batch = jnp.where((lane >> 2) == s, r.slot_batch[s], batch)
    slot_ids = jnp.concatenate([slot_ids] * 8, axis=1)
    chosen = (slot_ids == lane_iota((32, 1024), 1)).astype(f32).astype(bf16)
    sizes = jnp.concatenate([r.sizes[...].astype(f32), jnp.zeros((6, 1024), f32)], axis=0).astype(bf16)
    r.by_slot[...] = dot(sizes, chosen, NT)
    height, width = placed(r, lane_iota((32, LANES), 1) >> 2)
    count = jnp.where(((lane & 3) + z * 4).astype(f32) < height, width, 0.0)
    r.row_limit[...] = jnp.broadcast_to(jnp.transpose(count)[:, 0:1] * float(D), (LANES, LANES))
    upper, lower = one_hots(batch)
    r.row_onehot[0:8] = upper
    r.row_onehot[8:16] = lower
    r.row_counts[...] = jnp.broadcast_to(jnp.sum(upper * count, axis=1, keepdims=True), (8, LANES))
    for k, kind in enumerate((upper, lower)):
        r.row_columns[k] = jnp.transpose(jnp.concatenate([kind] * 4, axis=0)).astype(bf16)


def prepare_masks(r, z):
    lane = lane_iota((8, LANES), 1)
    batch = jnp.zeros((8, LANES), jnp.int32)
    for s in range(8):
        batch = jnp.where(lane_slot(lane) == s, r.slot_batch[z * 8 + s], batch)
    height, width = placed(r, lane_slot(lane_iota((32, LANES), 1)) + z * 8)
    rows_in = lane_row(lane).astype(f32) < height
    for x in range(SIDE):
        r.mask[:, x * LANES : (x + 1) * LANES] = (rows_in & (width > float(x))).astype(f32)
    r.counts[...] = jnp.where(rows_in, width, 0.0)
    upper, lower = one_hots(batch)
    zero = jnp.zeros((8, 6 * LANES), f32)
    both = jnp.concatenate([upper, lower], axis=1)
    summing = jnp.concatenate([upper] * 3 + [lower] * 3, axis=1)
    r.summing[...] = jnp.concatenate([summing, zero], axis=0).astype(bf16)
    r.placing[...] = jnp.concatenate([both] * 3 + [zero[:, 0:TILE]], axis=0).astype(bf16)
    place = lane_iota((8, DELEGATES), 1)
    height, width = placed(r, (lane_iota((32, DELEGATES), 1) >> 6) + z * 8)
    inside = ((2 * (place & 7)).astype(f32) < height) & ((2 * ((place >> 3) & 7)).astype(f32) < width)
    inside = inside.astype(f32)
    key, query = lane_iota((LANES, LANES), 0), lane_iota((LANES, LANES), 1)
    for p in range(4):
        column = jnp.transpose(inside[:, p * LANES : (p + 1) * LANES])[:, 0:1]
        r.keep[p] = jnp.where((key >> 6) == (query >> 6), jnp.broadcast_to(column, (LANES, LANES)), 0.0)
    lane, place = lane_iota((LANES, DELEGATES), 0), lane_iota((LANES, DELEGATES), 1)
    same = ((place >> 6) == lane_slot(lane)) & ((place & 7) == (lane_row(lane) >> 1))
    for j in range(8):
        r.pool[j * LANES : (j + 1) * LANES] = (
            (same & (((place >> 3) & 7) == j)).astype(f32).astype(bf16)
        )


def take_rows(block, dst, mask):
    for k in range(12):
        at = slice(k * LANES, (k + 1) * LANES)
        rows = jnp.concatenate([block[z, s, :, at] for s in range(8) for z in range(4)], axis=0)
        turned = jnp.transpose(rows)
        for x in range(SIDE):
            lo, hi = max(k * LANES, x * D), min((k + 1) * LANES, (x + 1) * D)
            if lo < hi:
                part = turned[lo - k * LANES : hi - k * LANES]
                dst[lo - x * D : hi - x * D, x * LANES : (x + 1) * LANES] = (
                    part * mask[0:1, x * LANES : (x + 1) * LANES]
                )


def give_rows(src, block):
    for k in range(12):
        parts = []
        for x in range(SIDE):
            lo, hi = max(k * LANES, x * D), min((k + 1) * LANES, (x + 1) * D)
            if lo < hi:
                parts.append(src[lo - x * D : hi - x * D, x * LANES : (x + 1) * LANES])
        turned = jnp.transpose(jnp.concatenate(parts, axis=0))
        for s in range(8):
            for z in range(4):
                place = 4 * (4 * s + z)
                block[z, s, :, k * LANES : (k + 1) * LANES] = turned[place : place + 4]


def three_parts(v, axis=0):
    high, low = halves(v)
    rest = (v - high.astype(f32)) - low.astype(f32)
    return jnp.concatenate([high, low, rest.astype(bf16)], axis=axis)


def lane_sums(upper, lower, r):
    parts = jnp.concatenate([three_parts(upper, 1), three_parts(lower, 1)], axis=1)
    return dot(r.summing[...], parts, NT)[0:8]


def row_mask(r, at):
    lane = (lane_iota((LANES, TILE), 1) + at).astype(f32)
    return lane < wide(r.row_limit[...])


def row_statistics(r):
    upper = jnp.concatenate([r.row_onehot[0:8]] * 3, axis=1).astype(bf16)
    lower = jnp.concatenate([r.row_onehot[8:16]] * 3, axis=1).astype(bf16)

    def body(k):
        at = tile_at(k)
        v = jnp.where(row_mask(r, k * TILE), r.own[:, :, at].reshape(LANES, TILE), 0.0)
        r.row_sums[:, at] = dot(upper, three_parts(v)) + dot(lower, three_parts(v * v))

    loop(6, body)
    total = r.row_sums[:, 0:D]
    for x in range(1, SIDE):
        total = total + r.row_sums[:, x * D : (x + 1) * D]
    return jnp.concatenate([total, r.row_counts[:, 0 : LANES - D]], axis=1)


def corrected_rows(r, out):
    for x in range(SIDE):
        r.row_sums[:, x * D : (x + 1) * D] = r.dstat_rows[:, 0:D]
    zero = jnp.zeros((8, TILE), bf16)

    def body(k):
        at = pl.ds(pl.multiple_of(k * TILE, TILE), TILE)
        parts = jnp.concatenate([three_parts(r.row_sums[:, at]), zero], axis=0)
        dsums, dsquares = dot(r.row_columns[0], parts), dot(r.row_columns[1], parts)
        v = r.rows_in[0, :, :, :, at].reshape(LANES, TILE) + dsums + r.own[:, :, at].reshape(LANES, TILE) * dsquares
        out[:, :, at] = jnp.where(row_mask(r, k * TILE), v, 0.0).reshape(32, 4, TILE)

    counted(0, 6, body)


def statistics_partial(r):
    total = jnp.concatenate([r.sums[0], r.counts[...], jnp.zeros((24, LANES), f32)], axis=0)
    square = jnp.concatenate([r.sums[1], jnp.zeros((32, LANES), f32)], axis=0)
    return lane_sums(total, square, r)


def per_lane(upper, lower, r):
    parts = three_parts(jnp.concatenate([upper, lower], axis=0)).astype(f32)
    turned = jnp.transpose(jnp.concatenate([parts, jnp.zeros((8, LANES), f32)], axis=0)).astype(bf16)
    both = dot(turned, r.placing[...])
    return both[0:D, 0:LANES], both[0:D, LANES:]


def use_statistics(r, l, totals):
    count = totals[0:4, D : D + 1]
    centre = totals[0:4] / count
    variance = totals[4:8] / count - centre * centre
    rate = lax.rsqrt(variance + EPSILON)
    r.stat_rows[l, 0:4] = centre
    r.stat_rows[l, 4:8] = rate
    r.count_rows[...] = jnp.broadcast_to(count, (4, LANES))
    centre_lanes, rate_lanes = per_lane(centre, rate, r)
    r.centre[l] = centre_lanes
    r.rate[l] = rate_lanes


def use_statistics_grad(r, l, totals):
    centre, rate = r.stat_rows[l, 0:4], r.stat_rows[l, 4:8]
    count = r.count_rows[...]
    gain = jnp.concatenate([r.gains[l, 0:1], jnp.zeros((1, LANES - D), f32)], axis=1)
    dcentre = -rate * gain * totals[0:4]
    dvariance = -0.5 * rate * rate * rate * gain * totals[4:8]
    dsums = (dcentre - 2.0 * centre * dvariance) / count
    dsquares = dvariance / count
    r.dstat_rows[0:4] = dsums
    r.dstat_rows[4:8] = 2.0 * dsquares
    if l > 0:
        r.dstat[0], r.dstat[1] = per_lane(dsums, 2.0 * dsquares, r)


def forward_local(r, l):
    r.fmap[l, :, 0:LANES] = jnp.zeros((D, LANES), f32)
    r.fmap[l, :, LANES + CELLS :] = jnp.zeros((D, LANES), f32)

    def body(j):
        v = r.x[l, :, tile_at(j)]
        pair = split((v - wide(r.centre[l])) * wide(r.rate[l] * r.par[l, 0]) + wide(r.par[l, 4]))
        r.n2[l, :, tile_at(j)] = pair
        yield
        out = mapped(r.first_t[l], pair) + wide(r.par[l, 5])
        r.fmap[l, :, padded_tile_at(j)] = out * r.mask[0:1, tile_at(j)]
        yield
        yield
        pair = split(convolved(r, l, j))
        r.d2[l, :, tile_at(j)] = pair
        yield
        out = mapped(r.second_t[l], pair) + wide(r.par[l, 7])
        local = r.x[l, :, tile_at(j)] + out * r.mask[0:1, tile_at(j)]
        r.local[:, tile_at(j)] = local
        unit, rate = normalized(local)
        r.unit1[l, :, tile_at(j)] = unit
        r.rates[l, 0:1, tile_at(j)] = rate
        r.pooled[:, lanes_at(j)] = split(
            0.25 * folded(unit * wide(r.par[l, 1]) + wide(r.par[l, 8]))
        )

    staggered(8, body)


def convolved(r, l, j):
    lane = lane_iota((8, LANES), 1)
    groups = []
    for g in range(12):
        rows = slice(g * 8, (g + 1) * 8)
        taps = [r.par[l, 16 + t, rows, :] for t in range(9)]
        cells = [r.fmap[l, rows, (2 * j + x) * LANES : (2 * j + x + 1) * LANES] for x in range(4)]
        columns = []
        for x in range(2):
            sums = [sum(taps[3 * q + c] * cells[x + c] for c in range(3)) for q in range(3)]
            columns.append(
                r.par[l, 6, rows, :] + sums[1] + from_row_before(sums[0], lane) + from_row_after(sums[2], lane)
            )
        groups.append(jnp.concatenate(columns, axis=1))
    return jnp.concatenate(groups, axis=0)


def forward_mixer(r, l):
    forward_queries(r, l)
    forward_attention(r, l)
    forward_spread(r, l)


def forward_queries(r, l):
    delegates = joined(dot(r.pooled[...], r.pool[...]))
    pair = split(delegates)
    r.g2[l] = pair
    qkv = mapped(r.mixer_t[l], pair)
    queries, keys, values = qkv[0:D], qkv[D : 2 * D], qkv[2 * D :]
    for t in range(4):
        at = slice(t * LANES, (t + 1) * LANES)
        r.qkv[l, 0:D, at] = (queries[:, at] + r.par[l, 9]) * SCALE
        r.qkv[l, D : 2 * D, at] = keys[:, at]
        r.qkv[l, 2 * D :, at] = values[:, at] + r.par[l, 10]


def by_head(v):
    zero = jnp.zeros((HEAD, LANES), f32)
    return jnp.concatenate(
        [jnp.concatenate([v[0:HEAD], zero], axis=1), jnp.concatenate([zero, v[HEAD:]], axis=1)], axis=0
    )


def own_head(v):
    return jnp.concatenate([v[0:HEAD, 0:LANES], v[HEAD:, LANES:]], axis=0)


def left_rows(v):
    turned = jnp.transpose(jnp.concatenate([v, v], axis=0))
    return jnp.concatenate(halves(turned), axis=0)


def left_columns(v):
    high, low = halves(v)
    return jnp.concatenate(
        [jnp.concatenate([high, high], axis=1), jnp.concatenate([low, low], axis=1)], axis=0
    )


def column_product(a_pair, b_pair):
    both = joined(dot(a_pair, b_pair, NT))
    return folded(both)


HEAD = D // 2
SCALE = 1.0 / math.sqrt(HEAD)


def forward_attention(r, l):
    def body(p):
        at = slice(p * LANES, (p + 1) * LANES)
        q, k, v = (r.qkv[l, part * D : (part + 1) * D, at] for part in range(3))
        left, right = left_rows(k), split(by_head(q))
        yield
        scores = joined(dot(left, right))
        scores = jnp.where(wide(r.keep[p]) > 0.0, scores, MASKED_SCORE)
        yield
        weights = jnp.exp(scores - jnp.max(scores, axis=0, keepdims=True))
        probs = weights / jnp.sum(weights, axis=0, keepdims=True)
        r.probs[l, p] = probs
        yield
        r.mixture[:, at] = own_head(mapped(left_columns(v), split(probs)))

    staggered(4, body)


def forward_spread(r, l):
    r.mix2[...] = split(r.mixture[...])

    def spread(t):
        r.up[l, :, tile_at(t)] = joined(dot(r.mix2[...], r.pool[tile_at(t), :], NT))

    loop(4, spread)


def rest_forward(r, l, j):
    mask = r.mask[0:1, tile_at(j)]
    up = r.up[l, :, lanes_at(j)]
    spread = jnp.concatenate([up * r.taps[l, 0], up * r.taps[l, 1]], axis=1) + wide(r.par[l, 11])
    unit2, rate2 = normalized(spread)
    pair = split(unit2 * wide(r.par[l, 2]) + wide(r.par[l, 12]))
    r.s2[l, :, tile_at(j)] = pair
    yield
    middle = r.local[:, tile_at(j)] + mask * (mapped(r.output_t[l], pair) + wide(r.par[l, 13]))
    unit3, rate3 = normalized(middle)
    pair = split(unit3 * wide(r.par[l, 3]) + wide(r.par[l, 14]))
    r.e2[l, :, tile_at(j)] = pair
    yield
    before = mapped(r.expand_t[l], pair) + wide(r.epar[l])
    yield
    normal = 0.5 + 0.5 * lax.erf(before * math.sqrt(0.5))
    slope = normal + before * (jnp.exp(-0.5 * before * before) * (1.0 / math.sqrt(2.0 * math.pi)))
    hidden = split(before * normal)
    r.h2[l, :, tile_at(j)] = hidden
    yield
    out = middle + mask * (mapped(r.reduce_t[l], hidden) + wide(r.par[l, 15]))
    return out, unit2, rate2, unit3, rate3, slope


def rest_backward(r, l, j, dy, unit2, rate2, unit3, rate3, slope):
    def add(k, v):
        r.acc[l, k] += folded(v)

    pair = split(dy)
    r.dy2[:, tile_at(j)] = pair
    add(15, dy)
    yield
    dbefore = mapped(r.reduce_n[l], pair) * slope
    r.eacc[l] += folded(dbefore)
    pair = split(dbefore)
    r.dp2[:, tile_at(j)] = pair
    yield
    de = mapped(r.expand_n[l], pair)
    add(14, de)
    add(3, de * unit3)
    dmiddle = dy + norm_pullback(de * wide(r.par[l, 3]), unit3, rate3)
    r.local[:, tile_at(j)] = dmiddle
    add(13, dmiddle)
    pair = split(dmiddle)
    r.dm2[:, tile_at(j)] = pair
    yield
    ds = mapped(r.output_n[l], pair)
    add(12, ds)
    add(2, ds * unit2)
    dspread = norm_pullback(ds * wide(r.par[l, 2]), unit2, rate2)
    add(11, dspread)
    up = r.up[l, :, lanes_at(j)]
    r.acc[l, 25] += dspread[:, :LANES] * up
    r.acc[l, 26] += dspread[:, LANES:] * up
    r.pooled[:, lanes_at(j)] = split(
        dspread[:, :LANES] * r.taps[l, 0] + dspread[:, LANES:] * r.taps[l, 1]
    )


def forward_rest(r, l):
    def body(j):
        out, unit2, rate2, unit3, rate3, slope = yield from rest_forward(r, l, j)
        r.unit2[:, tile_at(j)] = unit2
        r.unit3[:, tile_at(j)] = unit3
        r.rates2[0:1, tile_at(j)] = rate2
        r.rates2[1:2, tile_at(j)] = rate3
        r.slope[:, tile_at(j)] = slope
        r.x[l + 1, :, tile_at(j)] = out
        r.sums[0] += folded(out)
        r.sums[1] += folded(out * out)

    r.sums[...] = jnp.zeros_like(r.sums)
    staggered(8, body)


def backward_rest(r, l):
    def body(j):
        yield from rest_backward(
            r, l, j, r.dy[:, tile_at(j)], r.unit2[:, tile_at(j)], r.rates2[0:1, tile_at(j)],
            r.unit3[:, tile_at(j)], r.rates2[1:2, tile_at(j)], r.slope[:, tile_at(j)],
        )

    staggered(8, body)


def turn_rest(r, l):
    def body(j):
        out, *kept = yield from rest_forward(r, l, j)
        r.temp[:, tile_at(j)] = out
        yield from rest_backward(r, l, j, r.dy[:, tile_at(j)], *kept)

    staggered(8, body)


def backward_mixer(r, l):
    backward_gather(r, l)
    backward_attention(r, l)
    backward_queries(r, l)
    backward_spread(r, l)


def backward_gather(r, l):
    r.mixture[...] = joined(dot(r.pooled[...], r.pool[...]))


def backward_attention(r, l):
    def body(p):
        at = slice(p * LANES, (p + 1) * LANES)
        q, k, v = (r.qkv[l, part * D : (part + 1) * D, at] for part in range(3))
        probs = r.probs[l, p]
        dout = split(by_head(r.mixture[:, at]))
        left = left_rows(v)
        yield
        dprobs = joined(dot(left, dout))
        yield
        dscores = split(probs * (dprobs - jnp.sum(probs * dprobs, axis=0, keepdims=True)))
        r.dqkv[2 * D :, at] = column_product(dout, split(probs))
        yield
        r.dqkv[0:D, at] = own_head(mapped(left_columns(k), dscores)) * SCALE
        r.dqkv[D : 2 * D, at] = column_product(split(by_head(q)), dscores)

    staggered(4, body)


def backward_queries(r, l):
    dqkv = r.dqkv[...]
    for t in range(4):
        at = slice(t * LANES, (t + 1) * LANES)
        r.acc[l, 9] += dqkv[0:D, at]
        r.acc[l, 10] += dqkv[2 * D :, at]
    pair = split(dqkv)
    r.dq2[...] = pair
    r.mix2[...] = split(mapped(r.mixer_n[l], pair))


def backward_spread(r, l):
    def spread(t):
        r.dup[:, tile_at(t)] = 0.25 * joined(dot(r.mix2[...], r.pool[tile_at(t), :], NT))

    loop(4, spread)


def shifted_maps(r):
    return r.dy, r.dmap.at[0], r.dmap.at[1]


def backward_local(r, l):
    lane = lane_iota((D, LANES), 1)
    for shifted in shifted_maps(r):
        shifted[:, 0:LANES] = jnp.zeros((D, LANES), f32)
        shifted[:, LANES + CELLS :] = jnp.zeros((D, LANES), f32)

    def add(k, v):
        r.acc[l, k] += folded(v)

    def body(j):
        dup = wide(r.dup[:, lanes_at(j)])
        unit = r.unit1[l, :, tile_at(j)]
        add(8, dup)
        add(1, dup * unit)
        dlocal = r.local[:, tile_at(j)] + norm_pullback(
            dup * wide(r.par[l, 1]), unit, r.rates[l, 0:1, tile_at(j)]
        )
        r.local[:, tile_at(j)] = dlocal
        add(7, dlocal)
        pair = split(dlocal)
        r.dl2[:, tile_at(j)] = pair
        yield
        out = mapped(r.second_n[l], pair)
        add(6, out)
        after, same, before = shifted_maps(r)
        same[:, padded_tile_at(j)] = out
        for x in range(2):
            column = out[:, x * LANES : (x + 1) * LANES]
            place = slice((2 * j + x + 1) * LANES, (2 * j + x + 2) * LANES)
            after[:, place] = from_row_after(column, lane)
            before[:, place] = from_row_before(column, lane)
        yield
        yield
        v = convolved_back(r, l, j) * r.mask[0:1, tile_at(j)]
        add(5, v)
        pair = split(v)
        r.df2[:, tile_at(j)] = pair
        yield
        dnormed = mapped(r.first_n[l], pair)
        r.temp[:, tile_at(j)] = dnormed
        r.acc[l, 4] += folded(dnormed)
        r.acc[l, 0] += folded(dnormed * (r.x[l, :, tile_at(j)] - wide(r.centre[l])))

    staggered(8, body)


def convolved_back(r, l, j):
    groups = []
    for g in range(12):
        rows = slice(g * 8, (g + 1) * 8)
        value = [r.fmap[l, rows, (2 * j + x + 1) * LANES : (2 * j + x + 2) * LANES] for x in range(2)]
        columns = [0.0, 0.0]
        for q, shifted in enumerate(shifted_maps(r)):
            source = [shifted[rows, (2 * j + x) * LANES : (2 * j + x + 1) * LANES] for x in range(4)]
            for c in range(3):
                tap = r.par[l, 16 + 3 * q + c, rows, :]
                for x in range(2):
                    columns[x] = columns[x] + tap * source[x + 2 - c]
                r.acc[l, 16 + 3 * q + c, rows, :] += sum(source[x + 2 - c] * value[x] for x in range(2))
        groups.append(jnp.concatenate(columns, axis=1))
    return jnp.concatenate(groups, axis=0)


def statistics_grad_partial(r, l):
    pad = jnp.zeros((LANES - D, LANES), f32)
    return lane_sums(
        jnp.concatenate([r.acc[l, 4], pad], axis=0), jnp.concatenate([r.acc[l, 0], pad], axis=0), r
    )


def backward_input(r, l):
    def body(j):
        v = r.x[l, :, tile_at(j)]
        r.dy[:, tile_at(j)] = (
            r.temp[:, tile_at(j)] * wide(r.rate[l] * r.par[l, 0])
            + r.local[:, tile_at(j)]
            + r.mask[0:1, tile_at(j)] * (wide(r.dstat[0]) + v * wide(r.dstat[1]))
        )

    loop(8, body)


def partial_input(r, l):
    def body(j):
        r.dy[:, tile_at(j)] = (
            r.temp[:, tile_at(j)] * wide(r.rate[l] * r.par[l, 0]) + r.local[:, tile_at(j)]
        )

    loop(8, body)


def big_product(r, l, a, b, place):
    both = joined(dot(a, b, NT))
    both = both[:, 0:D] + both[:, D:]
    for t in range(3):
        r.grads[l, place + t * D : place + (t + 1) * D] = jnp.transpose(both[t * LANES : (t + 1) * LANES])


def small_product(a, b):
    both = joined(dot(a, b, NT))
    return both[:, 0:D] + both[:, D:]


def feed_forward_grads(r, l):
    big_product(r, l, r.dp2[...], r.e2[l], 0)
    big_product(r, l, r.h2[l], r.dy2[...], 288)
    r.grads[l, 576:672, 0:D] = small_product(r.s2[l], r.dm2[...])


def mixer_grads(r, l):
    queries, keys, values = (
        small_product(
            r.g2[l], jnp.concatenate([r.dq2[t * D : (t + 1) * D], r.dq2[(3 + t) * D : (4 + t) * D]], axis=0)
        )
        for t in range(3)
    )
    r.grads[l, 768:864, 0:D] = queries
    r.grads[l, 864:960, 0:D] = keys
    for t, place in enumerate(VALUE_PLACES):
        r.grads[l, place : place + D, D:] = values[:, t * 32 : (t + 1) * 32]


def local_grads(r, l):
    r.grads[l, 1024:1120, 0:D] = small_product(r.n2[l], r.df2[...])
    r.grads[l, 1120:1216, 0:D] = small_product(r.d2[l], r.dl2[...])


def vector_grads(r, l):
    r.acc[l, 0] = r.acc[l, 0] * r.rate[l]
    ones = jnp.ones((8, TILE), f32)
    even = ((lane_iota((8, TILE), 1) & 1) == 0).astype(f32)
    odd = (ones - even).astype(bf16)
    ones, even = ones.astype(bf16), even.astype(bf16)

    def row(kind, v, place, count):
        total = dot(kind, jnp.concatenate(halves(v), axis=1), NT)
        r.grads[l, 1216 + place : 1217 + place, 0:count] = total[0:1]

    for k in range(25):
        row(ones, r.acc[l, k], k, D)
    for b in range(2):
        row(even, r.acc[l, 25 + b], 25 + b, D)
        row(odd, r.acc[l, 25 + b], 27 + b, D)
    for t in range(3):
        row(ones, r.eacc[l, t * LANES : (t + 1) * LANES], 29 + t, LANES)


def weight_grads(r, l):
    feed_forward_grads(r, l)
    mixer_grads(r, l)
    local_grads(r, l)
    vector_grads(r, l)


def scratch_list():
    L = LAYERS
    v = pltpu.VMEM
    return [
        ("first_t", v((L, 192, 192), bf16)),
        ("first_n", v((L, 192, 192), bf16)),
        ("second_t", v((L, 192, 192), bf16)),
        ("second_n", v((L, 192, 192), bf16)),
        ("mixer_t", v((L, 576, 192), bf16)),
        ("mixer_n", v((L, 192, 576), bf16)),
        ("output_t", v((L, 192, 192), bf16)),
        ("output_n", v((L, 192, 192), bf16)),
        ("expand_t", v((L, 768, 192), bf16)),
        ("expand_n", v((L, 192, 768), bf16)),
        ("reduce_t", v((L, 192, 768), bf16)),
        ("reduce_n", v((L, 768, 192), bf16)),
        ("rows", v((PARAM_ROWS, LANES), f32)),
        ("par", v((L, 29, D, LANES), f32)),
        ("epar", v((L, FF, LANES), f32)),
        ("taps", v((L, 2, D, LANES), f32)),
        ("acc", v((L, 27, D, LANES), f32)),
        ("eacc", v((L, FF, LANES), f32)),
        ("mask", v((8, CELLS), f32)),
        ("counts", v((8, LANES), f32)),
        ("summing", v((16, 6 * LANES), bf16)),
        ("placing", v((32, TILE), bf16)),
        ("keep", v((4, LANES, LANES), f32)),
        ("pool", v((8 * LANES, DELEGATES), bf16)),
        ("sums", v((2, D, LANES), f32)),
        ("own", v((32, 4, SIDE * D), f32)),
        ("by_slot", v((8, 32), f32)),
        ("row_limit", v((LANES, LANES), f32)),
        ("row_onehot", v((16, LANES), f32)),
        ("row_counts", v((8, LANES), f32)),
        ("row_columns", v((2, LANES, 32), bf16)),
        ("row_sums", v((8, SIDE * D), f32)),
        ("dstat_rows", v((8, LANES), f32)),
        ("stat_rows", v((L, 8, LANES), f32)),
        ("count_rows", v((4, LANES), f32)),
        ("centre", v((L, D, LANES), f32)),
        ("rate", v((L, D, LANES), f32)),
        ("dstat", v((2, D, LANES), f32)),
        ("x", v((L, D, CELLS), f32)),
        ("n2", v((L, 2 * D, CELLS), bf16)),
        ("fmap", v((L, D, CELLS + 2 * LANES), f32)),
        ("temp", v((D, CELLS), f32)),
        ("d2", v((L, 2 * D, CELLS), bf16)),
        ("local", v((D, CELLS), f32)),
        ("unit1", v((L, D, CELLS), f32)),
        ("rates", v((L, 1, CELLS), f32)),
        ("pooled", v((2 * D, 8 * LANES), bf16)),
        ("g2", v((L, 2 * D, DELEGATES), bf16)),
        ("qkv", v((L, 3 * D, DELEGATES), f32)),
        ("probs", v((L, 4, LANES, TILE), f32)),
        ("mixture", v((D, DELEGATES), f32)),
        ("mix2", v((2 * D, DELEGATES), bf16)),
        ("up", v((L, D, 8 * LANES), f32)),
        ("unit2", v((D, CELLS), f32)),
        ("s2", v((L, 2 * D, CELLS), bf16)),
        ("unit3", v((D, CELLS), f32)),
        ("rates2", v((8, CELLS), f32)),
        ("e2", v((L, 2 * D, CELLS), bf16)),
        ("slope", v((FF, CELLS), f32)),
        ("h2", v((L, 2 * FF, CELLS), bf16)),
        ("dy", v((D, CELLS + 2 * LANES), f32)),
        ("dy2", v((2 * D, CELLS), bf16)),
        ("dp2", v((2 * FF, CELLS), bf16)),
        ("dm2", v((2 * D, CELLS), bf16)),
        ("dqkv", v((3 * D, DELEGATES), f32)),
        ("dq2", v((6 * D, DELEGATES), bf16)),
        ("dup", v((D, 8 * LANES), f32)),
        ("dl2", v((2 * D, CELLS), bf16)),
        ("dmap", v((2, D, CELLS + 2 * LANES), f32)),
        ("df2", v((2 * D, CELLS), bf16)),
        ("grads", v((L, GRAD_ROWS, LANES), f32)),
    ]


PARAMS = (
    "gains", "biases", "depth", "spread", "first", "second", "mixer", "output", "expand", "ebias", "reduce",
)

OTHERS = 15
GROUP = 7
PARCELS = ((0, 0, 1024), (1, 0, 1280), (0, 1024, 256))


class Place:
    def __init__(self):
        dp = lax.axis_index("dp")
        self.z = lax.axis_index("segment")
        self.core = lax.rem(dp, 2)
        self.chip = lax.div(dp, 2)
        self.member = self.z * 2 + self.core

    def chip_at(self, d):
        step = lax.rem(d + 8, 15) + 1
        x, y = lax.div(self.chip, 4) + lax.div(step, 4), lax.rem(self.chip, 4) + lax.rem(step, 4)
        return lax.rem(x, 4) * 4 + lax.rem(y, 4)

    def chip_after(self, d):
        return (self.z, self.chip_at(d) * 2 + self.core)

    def member_after(self, d):
        member = lax.rem(self.member + d, 8)
        return (lax.div(member, 2), self.chip * 2 + lax.rem(member, 2))

    def z_after(self, d):
        return (lax.rem(self.z + d, 4), self.chip * 2 + self.core)

    def sibling(self):
        return (self.z, self.chip * 2 + 1 - self.core)


def remote(src, dst, sends, receives, index, device):
    return pltpu.make_async_remote_copy(
        src_ref=src,
        dst_ref=dst,
        send_sem=sends.at[index],
        recv_sem=receives.at[index],
        device_id=device,
        device_id_type=pl.DeviceIdType.MESH,
    )


def greet(me):
    barrier = pltpu.get_barrier_semaphore()


    def signal(device):
        pl.semaphore_signal(barrier, inc=1, device_id=device, device_id_type=pl.DeviceIdType.MESH)

    counted(1, 16, lambda d: signal(me.chip_after(d)))
    counted(1, 8, lambda d: signal(me.member_after(d)))
    return barrier


class Exchange:
    def __init__(self, count, make, urgent=False):
        self.count, self.make, self.urgent = count, make, urgent

    def each(self, act):
        if self.urgent:
            for d in range(1, self.count + 1):
                act(self.make(d))
        else:
            counted(1, self.count + 1, lambda d: act(self.make(d)))

    def start(self):
        self.each(lambda copy: copy.start())

    def wait(self):
        self.each(lambda copy: copy.wait())


class RowsIn:
    def __init__(self, r, me, src, dst, number):
        self.own = pltpu.make_async_copy(src.at[pl.ds(me.z * 8, 8)], dst.at[me.z], r.row_own.at[number])
        self.copies = [
            remote(
                src.at[pl.ds(lax.rem(me.z + d, 4) * 8, 8)], dst.at[me.z],
                r.row_send, r.row_recv, (number, d), me.z_after(d),
            )
            for d in range(1, 4)
        ]

    def start(self):
        for copy in self.copies:
            copy.start()
        self.own.start()

    def wait(self):
        self.own.wait()
        for copy in self.copies:
            copy.wait()


class RowsOut(RowsIn):
    def __init__(self, r, me, src, dst, number):
        self.own = pltpu.make_async_copy(src.at[me.z], dst, r.row_own.at[number])
        self.copies = [
            remote(
                src.at[lax.rem(me.z + d, 4)], dst,
                r.row_send, r.row_recv, (number, d), me.z_after(d),
            )
            for d in range(1, 4)
        ]


class SmallSum:
    def __init__(self, r, me, number):
        self.r, self.me, self.number = r, me, number
        mine = r.chip_parts.at[number, me.chip]
        self.first = Exchange(
            OTHERS,
            lambda d: remote(mine, mine, r.chip_send, r.chip_recv, (number, d), me.chip_after(d)),
            number in (1, 2),
        )
        group = r.group_parts.at[number, me.member]
        self.second = Exchange(
            GROUP,
            lambda d: remote(group, group, r.group_send, r.group_recv, (number, d), me.member_after(d)),
            number in (1, 2),
        )

    def put(self, value):
        self.r.chip_parts[self.number, self.me.chip] = value

    def start(self):
        self.first.start()

    def step(self):
        self.first.wait()
        total = self.r.chip_parts[self.number, 0]
        for k in range(1, 16):
            total = total + self.r.chip_parts[self.number, k]
        self.r.group_parts[self.number, self.me.member] = total
        self.second.start()

    def finish(self):
        self.second.wait()
        total = self.r.group_parts[self.number, 0]
        for k in range(1, 8):
            total = total + self.r.group_parts[self.number, k]
        return total


class WeightSum:
    def __init__(self, r, me, number):
        self.r, self.me, self.number = r, me, number
        layer, start, rows = PARCELS[number]
        count, size = rows // 2, rows // 32
        grads, totals = r.grads.at[layer], r.totals.at[layer]
        self.half, self.parts, self.planes = (
            getattr(r, kind + str(number)) for kind in ("half", "parts", "planes")
        )

        def half_of(core):
            return pl.ds(pl.multiple_of(start + core * count, 8), count)

        def piece_of(chip):
            return pl.ds(pl.multiple_of(chip * size, 8), size)

        self.mine = grads.at[half_of(me.core)]
        self.own_piece = self.half.at[piece_of(me.chip)]
        self.halves = remote(
            grads.at[half_of(1 - me.core)], self.half, r.half_send, r.half_recv, (number, 0), me.sibling()
        )
        self.pieces = Exchange(
            OTHERS,
            lambda d: remote(
                self.half.at[piece_of(me.chip_at(d))], self.parts.at[me.chip],
                r.piece_send, r.piece_recv, (number, 0, d), me.chip_after(d),
            ),
        )
        plane = self.planes.at[me.z]
        self.exchange = Exchange(
            3, lambda d: remote(plane, plane, r.plane_send, r.plane_recv, (number, d), me.z_after(d))
        )
        self.total = totals.at[pl.ds(pl.multiple_of(start + me.core * count + me.chip * size, 8), size)]
        self.gathers = Exchange(
            OTHERS,
            lambda d: remote(
                self.total, self.total, r.piece_send, r.piece_recv, (number, 1, d), me.chip_after(d)
            ),
        )
        whole = totals.at[half_of(me.core)]
        self.last = remote(whole, whole, r.half_send, r.half_recv, (number, 1), me.sibling())

    def step(self, number):
        me = self.me
        if number == 0:
            self.halves.start()
        elif number == 1:
            self.halves.wait()
            self.half[...] = self.half[...] + self.mine[...]
            self.parts[me.chip] = self.own_piece[...]
            self.pieces.start()
        elif number == 2:
            self.pieces.wait()
            total = self.parts[0]
            for k in range(1, 16):
                total = total + self.parts[k]
            self.planes[me.z] = total
            self.exchange.start()
        elif number == 3:
            self.exchange.wait()
            self.total[...] = (self.planes[0] + self.planes[1]) + (self.planes[2] + self.planes[3])
            self.gathers.start()
        elif number == 4:
            self.gathers.wait()
            self.last.start()
        else:
            self.last.wait()


def comm_scratch():
    L = LAYERS
    v = pltpu.VMEM
    s = pltpu.SemaphoreType.DMA
    return [
        ("rows_in", v((2, 4, 8, 4, SIDE * D), f32)),
        ("chip_parts", v((4, 16, 8, LANES), f32)),
        ("group_parts", v((4, 8, 8, LANES), f32)),
        ("totals", v((L, GRAD_ROWS, LANES), f32)),
        ("row_own", s((5,))),
        ("row_send", s((4, 4))),
        ("row_recv", s((4, 4))),
        ("chip_send", s((4, 16))),
        ("chip_recv", s((4, 16))),
        ("group_send", s((4, 8))),
        ("group_recv", s((4, 8))),
        ("half_send", s((len(PARCELS), 2))),
        ("half_recv", s((len(PARCELS), 2))),
        ("piece_send", s((len(PARCELS), 2, 16))),
        ("piece_recv", s((len(PARCELS), 2, 16))),
        ("plane_send", s((len(PARCELS), 4))),
        ("plane_recv", s((len(PARCELS), 4))),
        ("member_send", s((len(PARCELS), 8))),
        ("member_recv", s((len(PARCELS), 8))),
        ("out_sem", s((2,))),
        ("param_sem", s((12,))),
    ] + [
        (kind + str(number), v(lead + (PARCELS[number][2] // share, LANES), f32))
        for number in range(len(PARCELS))
        for kind, lead, share in (("half", (), 2), ("parts", (16,), 32), ("planes", (4,), 32))
    ]


def layers_kernel(names, *refs):
    r = SimpleNamespace(**dict(zip(names, refs)))
    me = Place()
    barrier = greet(me)
    own_rows = pltpu.make_async_copy(r.tokens, r.own, r.row_own.at[4])
    loads = [
        pltpu.make_async_copy(getattr(r, name + "_in"), getattr(r, name), r.param_sem.at[k])
        for k, name in enumerate(("sizes",) + PARAMS)
    ]
    loads[0].start()
    own_rows.start()
    for load in loads[1:]:
        load.start()
    mine = pl.ds(me.z * 8, 8)
    tokens_in = RowsIn(r, me, r.tokens, r.rows_in.at[0], 0)
    upstream_in = RowsIn(r, me, r.cotangent, r.rows_in.at[1], 1)
    act_out = RowsOut(r, me, r.rows_in.at[1], r.act.at[mine], 2)
    grad_out = RowsOut(r, me, r.rows_in.at[1], r.rows_in.at[0, me.z], 3)
    sums = [SmallSum(r, me, number) for number in range(4)]
    outer, early, last = (WeightSum(r, me, number) for number in range(3))

    def run(work):
        pl.when(me.z >= 0)(work)

    pl.semaphore_wait(barrier, OTHERS + GROUP)
    tokens_in.start()
    loads[0].wait()
    own_rows.wait()

    @run
    def first_statistics():
        prepare_rows(r, me.z)
        sums[0].put(row_statistics(r))

    sums[0].start()

    @run
    def masks():
        prepare_masks(r, me.z)

    for load in loads[1:]:
        load.wait()

    @run
    def first_weights():
        counted(0, LAYERS, functools.partial(prepare_weights, r))
        r.grads[...] = jnp.zeros_like(r.grads)

    sums[0].step()
    tokens_in.wait()
    upstream_in.start()

    @run
    def tokens():
        take_rows(r.rows_in.at[0], r.x.at[0], r.mask)

    use_statistics(r, 0, sums[0].finish())

    @run
    def first_layer():
        forward_local(r, 0)
        forward_mixer(r, 0)
        forward_rest(r, 0)
        sums[1].put(statistics_partial(r))

    sums[1].start()

    sums[1].step()
    upstream_in.wait()

    @run
    def upstream():
        take_rows(r.rows_in.at[1], r.dy, r.mask)

    use_statistics(r, 1, sums[1].finish())

    @run
    def second_layer():
        forward_local(r, 1)
        forward_mixer(r, 1)
        turn_rest(r, 1)
        give_rows(r.temp, r.rows_in.at[1])

    act_out.start()

    @run
    def second_backward():
        backward_mixer(r, 1)
        backward_local(r, 1)
        sums[2].put(statistics_grad_partial(r, 1))

    sums[2].start()

    @run
    def second_products():
        feed_forward_grads(r, 1)
        mixer_grads(r, 1)

    sums[2].step()

    @run
    def second_local_products():
        local_grads(r, 1)
        vector_grads(r, 1)

    early.step(0)
    use_statistics_grad(r, 1, sums[2].finish())

    @run
    def between():
        backward_input(r, 1)

    early.step(1)

    @run
    def first_backward():
        backward_rest(r, 0)
        backward_mixer(r, 0)
        feed_forward_grads(r, 0)
        mixer_grads(r, 0)

    outer.step(0)
    early.step(2)

    @run
    def first_local_backward():
        backward_local(r, 0)
        sums[3].put(statistics_grad_partial(r, 0))

    sums[3].start()
    outer.step(1)

    @run
    def first_local_products():
        local_grads(r, 0)
        vector_grads(r, 0)

    last.step(0)
    early.step(3)
    act_out.wait()

    @run
    def input_grad():
        partial_input(r, 0)
        give_rows(r.dy, r.rows_in.at[1])

    grad_out.start()
    last.step(1)
    sums[3].step()
    outer.step(2)
    last.step(2)
    early.step(4)
    use_statistics_grad(r, 0, sums[3].finish())
    outer.step(3)
    last.step(3)
    grad_out.wait()

    @run
    def correction():
        corrected_rows(r, r.own)

    copy = pltpu.make_async_copy(r.own, r.grad, r.out_sem.at[0])
    copy.start()
    early.step(5)
    last.step(4)
    outer.step(4)
    last.step(5)
    outer.step(5)
    totals = pltpu.make_async_copy(r.totals, r.grad_sums, r.out_sem.at[1])
    totals.start()
    copy.wait()
    totals.wait()


def unpack_kernel(act_in, grad_in, totals_in, act, grad, *refs):
    count = len(PARAMS)
    outs, parts, (rows, totals, sems) = refs[:count], refs[count : 2 * count], refs[2 * count :]
    loads = [
        pltpu.make_async_copy(src, dst, sems.at[0, k])
        for k, (src, dst) in enumerate(
            ((totals_in.at[0], totals.at[0]), (totals_in.at[1], totals.at[1]), (act_in, rows.at[0]),
             (grad_in, rows.at[1]))
        )
    ]
    stores = [
        pltpu.make_async_copy(src, dst, sems.at[1, k])
        for k, (src, dst) in enumerate(
            ((rows.at[0], act), (rows.at[1], grad)) + tuple(zip(parts, outs))
        )
    ]
    for load in loads:
        load.start()
    gains, biases, depth, spread, first, second, mixer, output, expand, ebias, reduce = parts
    for l in range(LAYERS):
        loads[l].wait()

        def taken(place, count, width=D, start=0):
            return totals[l, place : place + count, start : start + width]

        gains[l] = taken(1216, 4)
        biases[:, l] = taken(1220, 12)
        depth[:, l] = taken(1232, 9)
        spread[l] = taken(1241, 4)
        first[l] = taken(1024, D)
        second[l] = taken(1120, D)
        output[l] = taken(576, D)
        mixer[l, :, 0:D] = taken(768, D)
        mixer[l, :, D : 2 * D] = taken(864, D)
        for t, place in enumerate(VALUE_PLACES):
            mixer[l, :, 2 * D + t * 32 : 2 * D + (t + 1) * 32] = taken(place, D, 32, D)
        for t in range(3):
            at = slice(t * LANES, (t + 1) * LANES)
            expand[l, :, at] = taken(t * D, D, LANES)
            reduce[l, :, at] = taken(288 + t * D, D, LANES)
            ebias[l : l + 1, at] = taken(1245 + t, 1, LANES)
    for store in stores[2:]:
        store.start()
    for load, store in zip(loads[2:], stores[:2]):
        load.wait()
        store.start()
    for store in stores:
        store.wait()


def turned(params):
    gains, biases, depth, spread, *maps, ebias, reduce = params
    return (gains, jnp.swapaxes(biases, 0, 1), jnp.swapaxes(depth, 0, 1), spread, *maps, ebias,
            jnp.swapaxes(reduce, 1, 2))


def shards(tokens, cotangent, image_size, slot_image, slot_batch, *params):
    params = turned(params)
    sizes = image_size.T
    scratch = scratch_list() + comm_scratch()
    scratch += [
        (name, pltpu.VMEM(p.shape, p.dtype)) for name, p in zip(("sizes",) + PARAMS, (sizes,) + params)
    ]
    ins = ("tokens", "cotangent", "slot_image", "slot_batch", "sizes_in")
    ins += tuple(name + "_in" for name in PARAMS)
    outs = ("act", "grad", "grad_sums")
    names = ins + outs + tuple(name for name, _ in scratch)
    anywhere = pl.BlockSpec(memory_space=pl.ANY)
    smem = pl.BlockSpec(memory_space=pltpu.SMEM)
    rows = jax.ShapeDtypeStruct(tokens.shape, f32)
    act, grad, totals = pl.pallas_call(
        functools.partial(layers_kernel, names),
        out_shape=[rows, rows, jax.ShapeDtypeStruct((LAYERS, GRAD_ROWS, LANES), f32)],
        in_specs=[anywhere, anywhere, smem, smem, anywhere] + [anywhere] * len(params),
        out_specs=[anywhere] * 3,
        scratch_shapes=[shape for _, shape in scratch],
        compiler_params=pltpu.CompilerParams(
            collective_id=0, has_side_effects=True, vmem_limit_bytes=63 * 2**20
        ),
        name="layers",
    )(tokens, cotangent, slot_image, slot_batch, sizes, *params)
    act, grad, *grads = pl.pallas_call(
        unpack_kernel,
        out_shape=[rows, rows] + [jax.ShapeDtypeStruct(p.shape, f32) for p in params],
        in_specs=[anywhere] * 3,
        out_specs=[anywhere] * (2 + len(params)),
        scratch_shapes=[pltpu.VMEM(p.shape, f32) for p in params]
        + [
            pltpu.VMEM((2,) + tokens.shape, f32),
            pltpu.VMEM(totals.shape, f32),
            pltpu.SemaphoreType.DMA((2, 2 + len(params))),
        ],
        compiler_params=pltpu.CompilerParams(vmem_limit_bytes=60 * 2**20),
        name="unpack",
    )(act, grad, totals)
    return (act, grad) + turned(grads)


def solution(mesh):
    rows = P("dp", "segment", None)
    return jax.shard_map(
        shards,
        mesh=mesh,
        in_specs=(rows, rows, P(), P("dp"), P("dp")) + (P(),) * len(PARAMS),
        out_specs=(rows, rows) + (P(),) * len(PARAMS),
        check_vma=False,
    )
```

```python
import functools
import math
from types import SimpleNamespace

import jax
import jax.numpy as jnp
from jax import lax
from jax.experimental import pallas as pl
from jax.experimental.pallas import tpu as pltpu
from jax.sharding import PartitionSpec as P

D = 96
FF = 384
LAYERS = 2
MICRO = 4
SIDE = 16
EPSILON = 1e-05
MASKED_SCORE = -1000000000.0
LANES = 128
TILE = 256
CELLS = SIDE * LANES
DELEGATES = 512
PARAM_ROWS = 32
GRAD_ROWS = 1280
VALUE_PLACES = (768, 864, 1024)
f32 = jnp.float32
bf16 = jnp.bfloat16

NN = (((1,), (0,)), ((), ()))
NT = (((1,), (1,)), ((), ()))
TN = (((0,), (0,)), ((), ()))


def dot(a, b, dims=NN):
    return lax.dot_general(a, b, dims, preferred_element_type=f32)


def halves(v):
    high = v.astype(bf16)
    return high, (v - high.astype(f32)).astype(bf16)


def split(v):
    return jnp.concatenate(halves(v), axis=0)


def mapped(weight_pair, pair):
    both = dot(weight_pair, pair)
    count = both.shape[0] // 2
    return both[:count] + both[count:]


def joined(both):
    count = both.shape[0] // 2
    return both[:count] + both[count:]


def wide(v):
    return jnp.concatenate([v, v], axis=1)


def folded(v):
    return v[:, :LANES] + v[:, LANES:]


def normalized(v):
    centre = v - jnp.sum(v, axis=0, keepdims=True) * (1.0 / D)
    rate = lax.rsqrt(jnp.sum(centre * centre, axis=0, keepdims=True) * (1.0 / D) + EPSILON)
    return centre * rate, rate


def norm_pullback(dn, unit, rate):
    mean = jnp.sum(dn, axis=0, keepdims=True) * (1.0 / D)
    slope = jnp.sum(dn * unit, axis=0, keepdims=True) * (1.0 / D)
    return rate * (dn - mean - unit * slope)


def lane_iota(shape, dim):
    return lax.broadcasted_iota(jnp.int32, shape, dim)


def lane_slot(lane):
    return lane >> 4


def lane_row(lane):
    return lane & 15


def from_row_before(v, lane):
    return jnp.where(lane_row(lane) > 0, pltpu.roll(v, 1, 1), 0.0)


def from_row_after(v, lane):
    return jnp.where(lane_row(lane) < 15, pltpu.roll(v, LANES - 1, 1), 0.0)


def tile_at(j):
    return slice(j * TILE, (j + 1) * TILE)


def padded_tile_at(j):
    return slice(LANES + j * TILE, LANES + (j + 1) * TILE)


def lanes_at(j):
    return slice(j * LANES, (j + 1) * LANES)


def loop(count, body):
    for index in range(count):
        body(index)


def counted(start, stop, body):
    def step(index, carry):
        body(index)
        return carry

    lax.fori_loop(start, stop, step, 0)


def staggered(count, body, gap=1):
    running, index, step = [], 0, 0
    while index < count or running:
        if index < count and step % gap == 0:
            running.append(body(index))
            index += 1
        running = [part for part in running if next(part, "end") != "end"]
        step += 1


def prepare_weights(r, l):
    def left_pair(dst, w):
        n, k = w.shape
        high, low = halves(w)
        dst[0:n, 0:k] = high
        dst[0:n, k : 2 * k] = high
        dst[n : 2 * n, 0:k] = low
        dst[n : 2 * n, k : 2 * k] = low

    for name in ("first", "second", "mixer", "output", "expand"):
        w = getattr(r, name)[l]
        left_pair(getattr(r, name + "_t").at[l], jnp.transpose(w))
        left_pair(getattr(r, name + "_n").at[l], w)
    left_pair(r.reduce_t.at[l], r.reduce[l])
    left_pair(r.reduce_n.at[l], jnp.transpose(r.reduce[l]))
    r.rows[...] = jnp.zeros((PARAM_ROWS, LANES), f32)
    r.rows[0:4, 0:D] = r.gains[l]
    r.rows[4:16, 0:D] = jnp.where(l == 0, r.biases[:, 0], r.biases[:, 1])
    r.rows[16:25, 0:D] = jnp.where(l == 0, r.depth[:, 0], r.depth[:, 1])
    r.rows[25:29, 0:D] = r.spread[l]
    for t in range(3):
        at = slice(t * LANES, (t + 1) * LANES)
        r.rows[29 + t : 30 + t, :] = jnp.where(l == 0, r.ebias[0:1, at], r.ebias[1:2, at])
    columns = jnp.transpose(r.rows[...])
    for k in range(29):
        r.par[l, k] = jnp.broadcast_to(columns[0:D, k : k + 1], (D, LANES))
    for t in range(3):
        r.epar[l, t * LANES : (t + 1) * LANES] = jnp.broadcast_to(
            columns[:, 29 + t : 30 + t], (LANES, LANES)
        )
    lane = lane_iota((D, LANES), 1)
    for b in range(2):
        r.taps[l, b] = jnp.where((lane & 1) == 0, r.par[l, 25 + b], r.par[l, 27 + b])
    r.acc[l] = jnp.zeros((27, D, LANES), f32)
    r.eacc[l] = jnp.zeros((FF, LANES), f32)


def placed(r, slots):
    found = (slots == lane_iota(slots.shape, 0)).astype(f32).astype(bf16)
    per_place = dot(r.by_slot[...].astype(bf16), found)
    return (jnp.broadcast_to(per_place[k : k + 1], (8, slots.shape[1])) for k in range(2))


def one_hots(batch):
    micro = lane_iota((8, LANES), 0)
    upper = ((batch == micro) & (micro < MICRO)).astype(f32)
    lower = ((batch == micro - MICRO) & (micro >= MICRO)).astype(f32)
    return upper, lower


def prepare_rows(r, z):
    lane = lane_iota((8, LANES), 1)
    slot_ids = jnp.zeros((32, LANES), jnp.int32)
    slot_row = lane_iota((32, LANES), 0)
    batch = jnp.zeros((8, LANES), jnp.int32)
    for s in range(32):
        slot_ids = jnp.where(slot_row == s, r.slot_image[s], slot_ids)
        batch = jnp.where((lane >> 2) == s, r.slot_batch[s], batch)
    slot_ids = jnp.concatenate([slot_ids] * 8, axis=1)
    chosen = (slot_ids == lane_iota((32, 1024), 1)).astype(f32).astype(bf16)
    sizes = jnp.concatenate([r.sizes[...].astype(f32), jnp.zeros((6, 1024), f32)], axis=0).astype(bf16)
    r.by_slot[...] = dot(sizes, chosen, NT)
    height, width = placed(r, lane_iota((32, LANES), 1) >> 2)
    count = jnp.where(((lane & 3) + z * 4).astype(f32) < height, width, 0.0)
    r.row_limit[...] = jnp.broadcast_to(jnp.transpose(count)[:, 0:1] * float(D), (LANES, LANES))
    upper, lower = one_hots(batch)
    r.row_onehot[0:8] = upper
    r.row_onehot[8:16] = lower
    r.row_counts[...] = jnp.broadcast_to(jnp.sum(upper * count, axis=1, keepdims=True), (8, LANES))
    for k, kind in enumerate((upper, lower)):
        r.row_columns[k] = jnp.transpose(jnp.concatenate([kind] * 4, axis=0)).astype(bf16)


def prepare_masks(r, z):
    lane = lane_iota((8, LANES), 1)
    batch = jnp.zeros((8, LANES), jnp.int32)
    for s in range(8):
        batch = jnp.where(lane_slot(lane) == s, r.slot_batch[z * 8 + s], batch)
    height, width = placed(r, lane_slot(lane_iota((32, LANES), 1)) + z * 8)
    rows_in = lane_row(lane).astype(f32) < height
    for x in range(SIDE):
        r.mask[:, x * LANES : (x + 1) * LANES] = (rows_in & (width > float(x))).astype(f32)
    r.counts[...] = jnp.where(rows_in, width, 0.0)
    upper, lower = one_hots(batch)
    zero = jnp.zeros((8, 6 * LANES), f32)
    both = jnp.concatenate([upper, lower], axis=1)
    summing = jnp.concatenate([upper] * 3 + [lower] * 3, axis=1)
    r.summing[...] = jnp.concatenate([summing, zero], axis=0).astype(bf16)
    r.placing[...] = jnp.concatenate([both] * 3 + [zero[:, 0:TILE]], axis=0).astype(bf16)
    place = lane_iota((8, DELEGATES), 1)
    height, width = placed(r, (lane_iota((32, DELEGATES), 1) >> 6) + z * 8)
    inside = ((2 * (place & 7)).astype(f32) < height) & ((2 * ((place >> 3) & 7)).astype(f32) < width)
    inside = inside.astype(f32)
    key, query = lane_iota((LANES, LANES), 0), lane_iota((LANES, LANES), 1)
    for p in range(4):
        column = jnp.transpose(inside[:, p * LANES : (p + 1) * LANES])[:, 0:1]
        r.keep[p] = jnp.where((key >> 6) == (query >> 6), jnp.broadcast_to(column, (LANES, LANES)), 0.0)
    lane, place = lane_iota((LANES, DELEGATES), 0), lane_iota((LANES, DELEGATES), 1)
    same = ((place >> 6) == lane_slot(lane)) & ((place & 7) == (lane_row(lane) >> 1))
    for j in range(8):
        r.pool[j * LANES : (j + 1) * LANES] = (
            (same & (((place >> 3) & 7) == j)).astype(f32).astype(bf16)
        )


def take_rows(block, dst, mask):
    for k in range(12):
        at = slice(k * LANES, (k + 1) * LANES)
        rows = jnp.concatenate([block[z, s, :, at] for s in range(8) for z in range(4)], axis=0)
        turned = jnp.transpose(rows)
        for x in range(SIDE):
            lo, hi = max(k * LANES, x * D), min((k + 1) * LANES, (x + 1) * D)
            if lo < hi:
                part = turned[lo - k * LANES : hi - k * LANES]
                dst[lo - x * D : hi - x * D, x * LANES : (x + 1) * LANES] = (
                    part * mask[0:1, x * LANES : (x + 1) * LANES]
                )


def give_rows(src, block):
    for k in range(12):
        parts = []
        for x in range(SIDE):
            lo, hi = max(k * LANES, x * D), min((k + 1) * LANES, (x + 1) * D)
            if lo < hi:
                parts.append(src[lo - x * D : hi - x * D, x * LANES : (x + 1) * LANES])
        turned = jnp.transpose(jnp.concatenate(parts, axis=0))
        for s in range(8):
            for z in range(4):
                place = 4 * (4 * s + z)
                block[z, s, :, k * LANES : (k + 1) * LANES] = turned[place : place + 4]


def three_parts(v, axis=0):
    high, low = halves(v)
    rest = (v - high.astype(f32)) - low.astype(f32)
    return jnp.concatenate([high, low, rest.astype(bf16)], axis=axis)


def lane_sums(upper, lower, r):
    parts = jnp.concatenate([three_parts(upper, 1), three_parts(lower, 1)], axis=1)
    return dot(r.summing[...], parts, NT)[0:8]


def row_mask(r, at):
    lane = (lane_iota((LANES, TILE), 1) + at).astype(f32)
    return lane < wide(r.row_limit[...])


def row_statistics(r):
    upper = jnp.concatenate([r.row_onehot[0:8]] * 3, axis=1).astype(bf16)
    lower = jnp.concatenate([r.row_onehot[8:16]] * 3, axis=1).astype(bf16)

    def body(k):
        at = tile_at(k)
        v = jnp.where(row_mask(r, k * TILE), r.own[:, :, at].reshape(LANES, TILE), 0.0)
        r.row_sums[:, at] = dot(upper, three_parts(v)) + dot(lower, three_parts(v * v))

    loop(6, body)
    total = r.row_sums[:, 0:D]
    for x in range(1, SIDE):
        total = total + r.row_sums[:, x * D : (x + 1) * D]
    return jnp.concatenate([total, r.row_counts[:, 0 : LANES - D]], axis=1)


def corrected_rows(r, out):
    for x in range(SIDE):
        r.row_sums[:, x * D : (x + 1) * D] = r.dstat_rows[:, 0:D]
    zero = jnp.zeros((8, TILE), bf16)

    def body(k):
        at = pl.ds(pl.multiple_of(k * TILE, TILE), TILE)
        parts = jnp.concatenate([three_parts(r.row_sums[:, at]), zero], axis=0)
        dsums, dsquares = dot(r.row_columns[0], parts), dot(r.row_columns[1], parts)
        v = r.rows_in[0, :, :, :, at].reshape(LANES, TILE) + dsums + r.own[:, :, at].reshape(LANES, TILE) * dsquares
        out[:, :, at] = jnp.where(row_mask(r, k * TILE), v, 0.0).reshape(32, 4, TILE)

    counted(0, 6, body)


def statistics_partial(r):
    total = jnp.concatenate([r.sums[0], r.counts[...], jnp.zeros((24, LANES), f32)], axis=0)
    square = jnp.concatenate([r.sums[1], jnp.zeros((32, LANES), f32)], axis=0)
    return lane_sums(total, square, r)


def per_lane(upper, lower, r):
    parts = three_parts(jnp.concatenate([upper, lower], axis=0)).astype(f32)
    turned = jnp.transpose(jnp.concatenate([parts, jnp.zeros((8, LANES), f32)], axis=0)).astype(bf16)
    both = dot(turned, r.placing[...])
    return both[0:D, 0:LANES], both[0:D, LANES:]


def use_statistics(r, l, totals):
    count = totals[0:4, D : D + 1]
    centre = totals[0:4] / count
    variance = totals[4:8] / count - centre * centre
    rate = lax.rsqrt(variance + EPSILON)
    r.stat_rows[l, 0:4] = centre
    r.stat_rows[l, 4:8] = rate
    r.count_rows[...] = jnp.broadcast_to(count, (4, LANES))
    centre_lanes, rate_lanes = per_lane(centre, rate, r)
    r.centre[l] = centre_lanes
    r.rate[l] = rate_lanes


def use_statistics_grad(r, l, totals):
    centre, rate = r.stat_rows[l, 0:4], r.stat_rows[l, 4:8]
    count = r.count_rows[...]
    gain = jnp.concatenate([r.gains[l, 0:1], jnp.zeros((1, LANES - D), f32)], axis=1)
    dcentre = -rate * gain * totals[0:4]
    dvariance = -0.5 * rate * rate * rate * gain * totals[4:8]
    dsums = (dcentre - 2.0 * centre * dvariance) / count
    dsquares = dvariance / count
    r.dstat_rows[0:4] = dsums
    r.dstat_rows[4:8] = 2.0 * dsquares
    if l > 0:
        r.dstat[0], r.dstat[1] = per_lane(dsums, 2.0 * dsquares, r)


def forward_local(r, l):
    r.fmap[l, :, 0:LANES] = jnp.zeros((D, LANES), f32)
    r.fmap[l, :, LANES + CELLS :] = jnp.zeros((D, LANES), f32)

    def body(j):
        v = r.x[l, :, tile_at(j)]
        pair = split((v - wide(r.centre[l])) * wide(r.rate[l] * r.par[l, 0]) + wide(r.par[l, 4]))
        r.n2[l, :, tile_at(j)] = pair
        yield
        out = mapped(r.first_t[l], pair) + wide(r.par[l, 5])
        r.fmap[l, :, padded_tile_at(j)] = out * r.mask[0:1, tile_at(j)]
        yield
        yield
        pair = split(convolved(r, l, j))
        r.d2[l, :, tile_at(j)] = pair
        yield
        out = mapped(r.second_t[l], pair) + wide(r.par[l, 7])
        local = r.x[l, :, tile_at(j)] + out * r.mask[0:1, tile_at(j)]
        r.local[:, tile_at(j)] = local
        unit, rate = normalized(local)
        r.unit1[l, :, tile_at(j)] = unit
        r.rates[l, 0:1, tile_at(j)] = rate
        r.pooled[:, lanes_at(j)] = split(
            0.25 * folded(unit * wide(r.par[l, 1]) + wide(r.par[l, 8]))
        )

    staggered(8, body)


def convolved(r, l, j):
    lane = lane_iota((8, LANES), 1)
    groups = []
    for g in range(12):
        rows = slice(g * 8, (g + 1) * 8)
        taps = [r.par[l, 16 + t, rows, :] for t in range(9)]
        cells = [r.fmap[l, rows, (2 * j + x) * LANES : (2 * j + x + 1) * LANES] for x in range(4)]
        columns = []
        for x in range(2):
            sums = [sum(taps[3 * q + c] * cells[x + c] for c in range(3)) for q in range(3)]
            columns.append(
                r.par[l, 6, rows, :] + sums[1] + from_row_before(sums[0], lane) + from_row_after(sums[2], lane)
            )
        groups.append(jnp.concatenate(columns, axis=1))
    return jnp.concatenate(groups, axis=0)


def forward_mixer(r, l):
    forward_queries(r, l)
    forward_attention(r, l)
    forward_spread(r, l)


def forward_queries(r, l):
    delegates = joined(dot(r.pooled[...], r.pool[...]))
    pair = split(delegates)
    r.g2[l] = pair
    qkv = mapped(r.mixer_t[l], pair)
    queries, keys, values = qkv[0:D], qkv[D : 2 * D], qkv[2 * D :]
    for t in range(4):
        at = slice(t * LANES, (t + 1) * LANES)
        r.qkv[l, 0:D, at] = (queries[:, at] + r.par[l, 9]) * SCALE
        r.qkv[l, D : 2 * D, at] = keys[:, at]
        r.qkv[l, 2 * D :, at] = values[:, at] + r.par[l, 10]


def by_head(v):
    zero = jnp.zeros((HEAD, LANES), f32)
    return jnp.concatenate(
        [jnp.concatenate([v[0:HEAD], zero], axis=1), jnp.concatenate([zero, v[HEAD:]], axis=1)], axis=0
    )


def own_head(v):
    return jnp.concatenate([v[0:HEAD, 0:LANES], v[HEAD:, LANES:]], axis=0)


def left_rows(v):
    turned = jnp.transpose(jnp.concatenate([v, v], axis=0))
    return jnp.concatenate(halves(turned), axis=0)


def left_columns(v):
    high, low = halves(v)
    return jnp.concatenate(
        [jnp.concatenate([high, high], axis=1), jnp.concatenate([low, low], axis=1)], axis=0
    )


def column_product(a_pair, b_pair):
    both = joined(dot(a_pair, b_pair, NT))
    return folded(both)


HEAD = D // 2
SCALE = 1.0 / math.sqrt(HEAD)


def forward_attention(r, l):
    def body(p):
        at = slice(p * LANES, (p + 1) * LANES)
        q, k, v = (r.qkv[l, part * D : (part + 1) * D, at] for part in range(3))
        left, right = left_rows(k), split(by_head(q))
        yield
        scores = joined(dot(left, right))
        scores = jnp.where(wide(r.keep[p]) > 0.0, scores, MASKED_SCORE)
        yield
        weights = jnp.exp(scores - jnp.max(scores, axis=0, keepdims=True))
        probs = weights / jnp.sum(weights, axis=0, keepdims=True)
        r.probs[l, p] = probs
        yield
        r.mixture[:, at] = own_head(mapped(left_columns(v), split(probs)))

    staggered(4, body)


def forward_spread(r, l):
    r.mix2[...] = split(r.mixture[...])

    def spread(t):
        r.up[l, :, tile_at(t)] = joined(dot(r.mix2[...], r.pool[tile_at(t), :], NT))

    loop(4, spread)


def rest_forward(r, l, j):
    mask = r.mask[0:1, tile_at(j)]
    up = r.up[l, :, lanes_at(j)]
    spread = jnp.concatenate([up * r.taps[l, 0], up * r.taps[l, 1]], axis=1) + wide(r.par[l, 11])
    unit2, rate2 = normalized(spread)
    pair = split(unit2 * wide(r.par[l, 2]) + wide(r.par[l, 12]))
    r.s2[l, :, tile_at(j)] = pair
    yield
    middle = r.local[:, tile_at(j)] + mask * (mapped(r.output_t[l], pair) + wide(r.par[l, 13]))
    unit3, rate3 = normalized(middle)
    pair = split(unit3 * wide(r.par[l, 3]) + wide(r.par[l, 14]))
    r.e2[l, :, tile_at(j)] = pair
    yield
    before = mapped(r.expand_t[l], pair) + wide(r.epar[l])
    yield
    normal = 0.5 + 0.5 * lax.erf(before * math.sqrt(0.5))
    slope = normal + before * (jnp.exp(-0.5 * before * before) * (1.0 / math.sqrt(2.0 * math.pi)))
    hidden = split(before * normal)
    r.h2[l, :, tile_at(j)] = hidden
    yield
    out = middle + mask * (mapped(r.reduce_t[l], hidden) + wide(r.par[l, 15]))
    return out, unit2, rate2, unit3, rate3, slope


def rest_backward(r, l, j, dy, unit2, rate2, unit3, rate3, slope):
    def add(k, v):
        r.acc[l, k] += folded(v)

    pair = split(dy)
    r.dy2[:, tile_at(j)] = pair
    add(15, dy)
    yield
    dbefore = mapped(r.reduce_n[l], pair) * slope
    r.eacc[l] += folded(dbefore)
    pair = split(dbefore)
    r.dp2[:, tile_at(j)] = pair
    yield
    de = mapped(r.expand_n[l], pair)
    add(14, de)
    add(3, de * unit3)
    dmiddle = dy + norm_pullback(de * wide(r.par[l, 3]), unit3, rate3)
    r.local[:, tile_at(j)] = dmiddle
    add(13, dmiddle)
    pair = split(dmiddle)
    r.dm2[:, tile_at(j)] = pair
    yield
    ds = mapped(r.output_n[l], pair)
    add(12, ds)
    add(2, ds * unit2)
    dspread = norm_pullback(ds * wide(r.par[l, 2]), unit2, rate2)
    add(11, dspread)
    up = r.up[l, :, lanes_at(j)]
    r.acc[l, 25] += dspread[:, :LANES] * up
    r.acc[l, 26] += dspread[:, LANES:] * up
    r.pooled[:, lanes_at(j)] = split(
        dspread[:, :LANES] * r.taps[l, 0] + dspread[:, LANES:] * r.taps[l, 1]
    )


def forward_rest(r, l):
    def body(j):
        out, unit2, rate2, unit3, rate3, slope = yield from rest_forward(r, l, j)
        r.unit2[:, tile_at(j)] = unit2
        r.unit3[:, tile_at(j)] = unit3
        r.rates2[0:1, tile_at(j)] = rate2
        r.rates2[1:2, tile_at(j)] = rate3
        r.slope[:, tile_at(j)] = slope
        r.x[l + 1, :, tile_at(j)] = out
        r.sums[0] += folded(out)
        r.sums[1] += folded(out * out)

    r.sums[...] = jnp.zeros_like(r.sums)
    staggered(8, body)


def backward_rest(r, l):
    def body(j):
        yield from rest_backward(
            r, l, j, r.dy[:, tile_at(j)], r.unit2[:, tile_at(j)], r.rates2[0:1, tile_at(j)],
            r.unit3[:, tile_at(j)], r.rates2[1:2, tile_at(j)], r.slope[:, tile_at(j)],
        )

    staggered(8, body)


def turn_rest(r, l):
    def body(j):
        out, *kept = yield from rest_forward(r, l, j)
        r.temp[:, tile_at(j)] = out
        yield from rest_backward(r, l, j, r.dy[:, tile_at(j)], *kept)

    staggered(8, body)


def backward_mixer(r, l):
    backward_gather(r, l)
    backward_attention(r, l)
    backward_queries(r, l)
    backward_spread(r, l)


def backward_gather(r, l):
    r.mixture[...] = joined(dot(r.pooled[...], r.pool[...]))


def backward_attention(r, l):
    def body(p):
        at = slice(p * LANES, (p + 1) * LANES)
        q, k, v = (r.qkv[l, part * D : (part + 1) * D, at] for part in range(3))
        probs = r.probs[l, p]
        dout = split(by_head(r.mixture[:, at]))
        left = left_rows(v)
        yield
        dprobs = joined(dot(left, dout))
        yield
        dscores = split(probs * (dprobs - jnp.sum(probs * dprobs, axis=0, keepdims=True)))
        r.dqkv[2 * D :, at] = column_product(dout, split(probs))
        yield
        r.dqkv[0:D, at] = own_head(mapped(left_columns(k), dscores)) * SCALE
        r.dqkv[D : 2 * D, at] = column_product(split(by_head(q)), dscores)

    staggered(4, body)


def backward_queries(r, l):
    dqkv = r.dqkv[...]
    for t in range(4):
        at = slice(t * LANES, (t + 1) * LANES)
        r.acc[l, 9] += dqkv[0:D, at]
        r.acc[l, 10] += dqkv[2 * D :, at]
    pair = split(dqkv)
    r.dq2[...] = pair
    r.mix2[...] = split(mapped(r.mixer_n[l], pair))


def backward_spread(r, l):
    def spread(t):
        r.dup[:, tile_at(t)] = 0.25 * joined(dot(r.mix2[...], r.pool[tile_at(t), :], NT))

    loop(4, spread)


def shifted_maps(r):
    return r.dy, r.dmap.at[0], r.dmap.at[1]


def backward_local(r, l):
    lane = lane_iota((D, LANES), 1)
    for shifted in shifted_maps(r):
        shifted[:, 0:LANES] = jnp.zeros((D, LANES), f32)
        shifted[:, LANES + CELLS :] = jnp.zeros((D, LANES), f32)

    def add(k, v):
        r.acc[l, k] += folded(v)

    def body(j):
        dup = wide(r.dup[:, lanes_at(j)])
        unit = r.unit1[l, :, tile_at(j)]
        add(8, dup)
        add(1, dup * unit)
        dlocal = r.local[:, tile_at(j)] + norm_pullback(
            dup * wide(r.par[l, 1]), unit, r.rates[l, 0:1, tile_at(j)]
        )
        r.local[:, tile_at(j)] = dlocal
        add(7, dlocal)
        pair = split(dlocal)
        r.dl2[:, tile_at(j)] = pair
        yield
        out = mapped(r.second_n[l], pair)
        add(6, out)
        after, same, before = shifted_maps(r)
        same[:, padded_tile_at(j)] = out
        for x in range(2):
            column = out[:, x * LANES : (x + 1) * LANES]
            place = slice((2 * j + x + 1) * LANES, (2 * j + x + 2) * LANES)
            after[:, place] = from_row_after(column, lane)
            before[:, place] = from_row_before(column, lane)
        yield
        yield
        v = convolved_back(r, l, j) * r.mask[0:1, tile_at(j)]
        add(5, v)
        pair = split(v)
        r.df2[:, tile_at(j)] = pair
        yield
        dnormed = mapped(r.first_n[l], pair)
        r.temp[:, tile_at(j)] = dnormed
        r.acc[l, 4] += folded(dnormed)
        r.acc[l, 0] += folded(dnormed * (r.x[l, :, tile_at(j)] - wide(r.centre[l])))

    staggered(8, body)


def convolved_back(r, l, j):
    groups = []
    for g in range(12):
        rows = slice(g * 8, (g + 1) * 8)
        value = [r.fmap[l, rows, (2 * j + x + 1) * LANES : (2 * j + x + 2) * LANES] for x in range(2)]
        columns = [0.0, 0.0]
        for q, shifted in enumerate(shifted_maps(r)):
            source = [shifted[rows, (2 * j + x) * LANES : (2 * j + x + 1) * LANES] for x in range(4)]
            for c in range(3):
                tap = r.par[l, 16 + 3 * q + c, rows, :]
                for x in range(2):
                    columns[x] = columns[x] + tap * source[x + 2 - c]
                r.acc[l, 16 + 3 * q + c, rows, :] += sum(source[x + 2 - c] * value[x] for x in range(2))
        groups.append(jnp.concatenate(columns, axis=1))
    return jnp.concatenate(groups, axis=0)


def statistics_grad_partial(r, l):
    pad = jnp.zeros((LANES - D, LANES), f32)
    return lane_sums(
        jnp.concatenate([r.acc[l, 4], pad], axis=0), jnp.concatenate([r.acc[l, 0], pad], axis=0), r
    )


def backward_input(r, l):
    def body(j):
        v = r.x[l, :, tile_at(j)]
        r.dy[:, tile_at(j)] = (
            r.temp[:, tile_at(j)] * wide(r.rate[l] * r.par[l, 0])
            + r.local[:, tile_at(j)]
            + r.mask[0:1, tile_at(j)] * (wide(r.dstat[0]) + v * wide(r.dstat[1]))
        )

    loop(8, body)


def partial_input(r, l):
    def body(j):
        r.dy[:, tile_at(j)] = (
            r.temp[:, tile_at(j)] * wide(r.rate[l] * r.par[l, 0]) + r.local[:, tile_at(j)]
        )

    loop(8, body)


def big_product(r, l, a, b, place):
    both = joined(dot(a, b, NT))
    both = both[:, 0:D] + both[:, D:]
    for t in range(3):
        r.grads[l, place + t * D : place + (t + 1) * D] = jnp.transpose(both[t * LANES : (t + 1) * LANES])


def small_product(a, b):
    both = joined(dot(a, b, NT))
    return both[:, 0:D] + both[:, D:]


def feed_forward_grads(r, l):
    big_product(r, l, r.dp2[...], r.e2[l], 0)
    big_product(r, l, r.h2[l], r.dy2[...], 288)
    r.grads[l, 576:672, 0:D] = small_product(r.s2[l], r.dm2[...])


def mixer_grads(r, l):
    queries, keys, values = (
        small_product(
            r.g2[l], jnp.concatenate([r.dq2[t * D : (t + 1) * D], r.dq2[(3 + t) * D : (4 + t) * D]], axis=0)
        )
        for t in range(3)
    )
    r.grads[l, 768:864, 0:D] = queries
    r.grads[l, 864:960, 0:D] = keys
    for t, place in enumerate(VALUE_PLACES):
        r.grads[l, place : place + D, D:] = values[:, t * 32 : (t + 1) * 32]


def local_grads(r, l):
    r.grads[l, 1024:1120, 0:D] = small_product(r.n2[l], r.df2[...])
    r.grads[l, 1120:1216, 0:D] = small_product(r.d2[l], r.dl2[...])


def vector_grads(r, l):
    r.acc[l, 0] = r.acc[l, 0] * r.rate[l]
    ones = jnp.ones((8, TILE), f32)
    even = ((lane_iota((8, TILE), 1) & 1) == 0).astype(f32)
    odd = (ones - even).astype(bf16)
    ones, even = ones.astype(bf16), even.astype(bf16)

    def row(kind, v, place, count):
        total = dot(kind, jnp.concatenate(halves(v), axis=1), NT)
        r.grads[l, 1216 + place : 1217 + place, 0:count] = total[0:1]

    for k in range(25):
        row(ones, r.acc[l, k], k, D)
    for b in range(2):
        row(even, r.acc[l, 25 + b], 25 + b, D)
        row(odd, r.acc[l, 25 + b], 27 + b, D)
    for t in range(3):
        row(ones, r.eacc[l, t * LANES : (t + 1) * LANES], 29 + t, LANES)


def weight_grads(r, l):
    feed_forward_grads(r, l)
    mixer_grads(r, l)
    local_grads(r, l)
    vector_grads(r, l)


def scratch_list():
    L = LAYERS
    v = pltpu.VMEM
    return [
        ("first_t", v((L, 192, 192), bf16)),
        ("first_n", v((L, 192, 192), bf16)),
        ("second_t", v((L, 192, 192), bf16)),
        ("second_n", v((L, 192, 192), bf16)),
        ("mixer_t", v((L, 576, 192), bf16)),
        ("mixer_n", v((L, 192, 576), bf16)),
        ("output_t", v((L, 192, 192), bf16)),
        ("output_n", v((L, 192, 192), bf16)),
        ("expand_t", v((L, 768, 192), bf16)),
        ("expand_n", v((L, 192, 768), bf16)),
        ("reduce_t", v((L, 192, 768), bf16)),
        ("reduce_n", v((L, 768, 192), bf16)),
        ("rows", v((PARAM_ROWS, LANES), f32)),
        ("par", v((L, 29, D, LANES), f32)),
        ("epar", v((L, FF, LANES), f32)),
        ("taps", v((L, 2, D, LANES), f32)),
        ("acc", v((L, 27, D, LANES), f32)),
        ("eacc", v((L, FF, LANES), f32)),
        ("mask", v((8, CELLS), f32)),
        ("counts", v((8, LANES), f32)),
        ("summing", v((16, 6 * LANES), bf16)),
        ("placing", v((32, TILE), bf16)),
        ("keep", v((4, LANES, LANES), f32)),
        ("pool", v((8 * LANES, DELEGATES), bf16)),
        ("sums", v((2, D, LANES), f32)),
        ("own", v((32, 4, SIDE * D), f32)),
        ("by_slot", v((8, 32), f32)),
        ("row_limit", v((LANES, LANES), f32)),
        ("row_onehot", v((16, LANES), f32)),
        ("row_counts", v((8, LANES), f32)),
        ("row_columns", v((2, LANES, 32), bf16)),
        ("row_sums", v((8, SIDE * D), f32)),
        ("dstat_rows", v((8, LANES), f32)),
        ("stat_rows", v((L, 8, LANES), f32)),
        ("count_rows", v((4, LANES), f32)),
        ("centre", v((L, D, LANES), f32)),
        ("rate", v((L, D, LANES), f32)),
        ("dstat", v((2, D, LANES), f32)),
        ("x", v((L, D, CELLS), f32)),
        ("n2", v((L, 2 * D, CELLS), bf16)),
        ("fmap", v((L, D, CELLS + 2 * LANES), f32)),
        ("temp", v((D, CELLS), f32)),
        ("d2", v((L, 2 * D, CELLS), bf16)),
        ("local", v((D, CELLS), f32)),
        ("unit1", v((L, D, CELLS), f32)),
        ("rates", v((L, 1, CELLS), f32)),
        ("pooled", v((2 * D, 8 * LANES), bf16)),
        ("g2", v((L, 2 * D, DELEGATES), bf16)),
        ("qkv", v((L, 3 * D, DELEGATES), f32)),
        ("probs", v((L, 4, LANES, TILE), f32)),
        ("mixture", v((D, DELEGATES), f32)),
        ("mix2", v((2 * D, DELEGATES), bf16)),
        ("up", v((L, D, 8 * LANES), f32)),
        ("unit2", v((D, CELLS), f32)),
        ("s2", v((L, 2 * D, CELLS), bf16)),
        ("unit3", v((D, CELLS), f32)),
        ("rates2", v((8, CELLS), f32)),
        ("e2", v((L, 2 * D, CELLS), bf16)),
        ("slope", v((FF, CELLS), f32)),
        ("h2", v((L, 2 * FF, CELLS), bf16)),
        ("dy", v((D, CELLS + 2 * LANES), f32)),
        ("dy2", v((2 * D, CELLS), bf16)),
        ("dp2", v((2 * FF, CELLS), bf16)),
        ("dm2", v((2 * D, CELLS), bf16)),
        ("dqkv", v((3 * D, DELEGATES), f32)),
        ("dq2", v((6 * D, DELEGATES), bf16)),
        ("dup", v((D, 8 * LANES), f32)),
        ("dl2", v((2 * D, CELLS), bf16)),
        ("dmap", v((2, D, CELLS + 2 * LANES), f32)),
        ("df2", v((2 * D, CELLS), bf16)),
        ("grads", v((L, GRAD_ROWS, LANES), f32)),
    ]


PARAMS = (
    "gains", "biases", "depth", "spread", "first", "second", "mixer", "output", "expand", "ebias", "reduce",
)

OTHERS = 15
GROUP = 7
PARCELS = ((0, 0, 1024), (1, 0, 1280), (0, 1024, 256))


class Place:
    def __init__(self):
        dp = lax.axis_index("dp")
        self.z = lax.axis_index("segment")
        self.core = lax.rem(dp, 2)
        self.chip = lax.div(dp, 2)
        self.member = self.z * 2 + self.core

    def chip_at(self, d):
        step = lax.rem(d + 8, 15) + 1
        x, y = lax.div(self.chip, 4) + lax.div(step, 4), lax.rem(self.chip, 4) + lax.rem(step, 4)
        return lax.rem(x, 4) * 4 + lax.rem(y, 4)

    def chip_after(self, d):
        return (self.z, self.chip_at(d) * 2 + self.core)

    def member_after(self, d):
        member = lax.rem(self.member + d, 8)
        return (lax.div(member, 2), self.chip * 2 + lax.rem(member, 2))

    def z_after(self, d):
        return (lax.rem(self.z + d, 4), self.chip * 2 + self.core)

    def sibling(self):
        return (self.z, self.chip * 2 + 1 - self.core)


def remote(src, dst, sends, receives, index, device):
    return pltpu.make_async_remote_copy(
        src_ref=src,
        dst_ref=dst,
        send_sem=sends.at[index],
        recv_sem=receives.at[index],
        device_id=device,
        device_id_type=pl.DeviceIdType.MESH,
    )


def greet(me):
    barrier = pltpu.get_barrier_semaphore()


    def signal(device):
        pl.semaphore_signal(barrier, inc=1, device_id=device, device_id_type=pl.DeviceIdType.MESH)

    counted(1, 16, lambda d: signal(me.chip_after(d)))
    counted(1, 8, lambda d: signal(me.member_after(d)))
    return barrier


class Exchange:
    def __init__(self, count, make, urgent=False):
        self.count, self.make, self.urgent = count, make, urgent

    def each(self, act):
        if self.urgent:
            for d in range(1, self.count + 1):
                act(self.make(d))
        else:
            counted(1, self.count + 1, lambda d: act(self.make(d)))

    def start(self):
        self.each(lambda copy: copy.start())

    def wait(self):
        self.each(lambda copy: copy.wait())


class RowsIn:
    def __init__(self, r, me, src, dst, number):
        self.own = pltpu.make_async_copy(src.at[pl.ds(me.z * 8, 8)], dst.at[me.z], r.row_own.at[number])
        self.copies = [
            remote(
                src.at[pl.ds(lax.rem(me.z + d, 4) * 8, 8)], dst.at[me.z],
                r.row_send, r.row_recv, (number, d), me.z_after(d),
            )
            for d in range(1, 4)
        ]

    def start(self):
        for copy in self.copies:
            copy.start()
        self.own.start()

    def wait(self):
        self.own.wait()
        for copy in self.copies:
            copy.wait()


class RowsOut(RowsIn):
    def __init__(self, r, me, src, dst, number):
        self.own = pltpu.make_async_copy(src.at[me.z], dst, r.row_own.at[number])
        self.copies = [
            remote(
                src.at[lax.rem(me.z + d, 4)], dst,
                r.row_send, r.row_recv, (number, d), me.z_after(d),
            )
            for d in range(1, 4)
        ]


class SmallSum:
    def __init__(self, r, me, number):
        self.r, self.me, self.number = r, me, number
        mine = r.chip_parts.at[number, me.chip]
        self.first = Exchange(
            OTHERS,
            lambda d: remote(mine, mine, r.chip_send, r.chip_recv, (number, d), me.chip_after(d)),
            number in (1, 2),
        )
        group = r.group_parts.at[number, me.member]
        self.second = Exchange(
            GROUP,
            lambda d: remote(group, group, r.group_send, r.group_recv, (number, d), me.member_after(d)),
            number in (1, 2),
        )

    def put(self, value):
        self.r.chip_parts[self.number, self.me.chip] = value

    def start(self):
        self.first.start()

    def step(self):
        self.first.wait()
        total = self.r.chip_parts[self.number, 0]
        for k in range(1, 16):
            total = total + self.r.chip_parts[self.number, k]
        self.r.group_parts[self.number, self.me.member] = total
        self.second.start()

    def finish(self):
        self.second.wait()
        total = self.r.group_parts[self.number, 0]
        for k in range(1, 8):
            total = total + self.r.group_parts[self.number, k]
        return total


class WeightSum:
    def __init__(self, r, me, number):
        self.r, self.me, self.number = r, me, number
        layer, start, rows = PARCELS[number]
        count, size = rows // 2, rows // 32
        grads, totals = r.grads.at[layer], r.totals.at[layer]
        self.half, self.parts, self.planes = (
            getattr(r, kind + str(number)) for kind in ("half", "parts", "planes")
        )

        def half_of(core):
            return pl.ds(pl.multiple_of(start + core * count, 8), count)

        def piece_of(chip):
            return pl.ds(pl.multiple_of(chip * size, 8), size)

        self.mine = grads.at[half_of(me.core)]
        self.own_piece = self.half.at[piece_of(me.chip)]
        self.halves = remote(
            grads.at[half_of(1 - me.core)], self.half, r.half_send, r.half_recv, (number, 0), me.sibling()
        )
        self.pieces = Exchange(
            OTHERS,
            lambda d: remote(
                self.half.at[piece_of(me.chip_at(d))], self.parts.at[me.chip],
                r.piece_send, r.piece_recv, (number, 0, d), me.chip_after(d),
            ),
        )
        plane = self.planes.at[me.z]
        self.exchange = Exchange(
            3, lambda d: remote(plane, plane, r.plane_send, r.plane_recv, (number, d), me.z_after(d))
        )
        self.total = totals.at[pl.ds(pl.multiple_of(start + me.core * count + me.chip * size, 8), size)]
        self.gathers = Exchange(
            OTHERS,
            lambda d: remote(
                self.total, self.total, r.piece_send, r.piece_recv, (number, 1, d), me.chip_after(d)
            ),
        )
        whole = totals.at[half_of(me.core)]
        self.last = remote(whole, whole, r.half_send, r.half_recv, (number, 1), me.sibling())

    def step(self, number):
        me = self.me
        if number == 0:
            self.halves.start()
        elif number == 1:
            self.halves.wait()
            self.half[...] = self.half[...] + self.mine[...]
            self.parts[me.chip] = self.own_piece[...]
            self.pieces.start()
        elif number == 2:
            self.pieces.wait()
            total = self.parts[0]
            for k in range(1, 16):
                total = total + self.parts[k]
            self.planes[me.z] = total
            self.exchange.start()
        elif number == 3:
            self.exchange.wait()
            self.total[...] = (self.planes[0] + self.planes[1]) + (self.planes[2] + self.planes[3])
            self.gathers.start()
        elif number == 4:
            self.gathers.wait()
            self.last.start()
        else:
            self.last.wait()


def comm_scratch():
    L = LAYERS
    v = pltpu.VMEM
    s = pltpu.SemaphoreType.DMA
    return [
        ("rows_in", v((2, 4, 8, 4, SIDE * D), f32)),
        ("chip_parts", v((4, 16, 8, LANES), f32)),
        ("group_parts", v((4, 8, 8, LANES), f32)),
        ("totals", v((L, GRAD_ROWS, LANES), f32)),
        ("row_own", s((5,))),
        ("row_send", s((4, 4))),
        ("row_recv", s((4, 4))),
        ("chip_send", s((4, 16))),
        ("chip_recv", s((4, 16))),
        ("group_send", s((4, 8))),
        ("group_recv", s((4, 8))),
        ("half_send", s((len(PARCELS), 2))),
        ("half_recv", s((len(PARCELS), 2))),
        ("piece_send", s((len(PARCELS), 2, 16))),
        ("piece_recv", s((len(PARCELS), 2, 16))),
        ("plane_send", s((len(PARCELS), 4))),
        ("plane_recv", s((len(PARCELS), 4))),
        ("member_send", s((len(PARCELS), 8))),
        ("member_recv", s((len(PARCELS), 8))),
        ("out_sem", s((2,))),
        ("param_sem", s((12,))),
    ] + [
        (kind + str(number), v(lead + (PARCELS[number][2] // share, LANES), f32))
        for number in range(len(PARCELS))
        for kind, lead, share in (("half", (), 2), ("parts", (16,), 32), ("planes", (4,), 32))
    ]


def layers_kernel(names, *refs):
    r = SimpleNamespace(**dict(zip(names, refs)))
    me = Place()
    barrier = greet(me)
    own_rows = pltpu.make_async_copy(r.tokens, r.own, r.row_own.at[4])
    loads = [
        pltpu.make_async_copy(getattr(r, name + "_in"), getattr(r, name), r.param_sem.at[k])
        for k, name in enumerate(("sizes",) + PARAMS)
    ]
    loads[0].start()
    own_rows.start()
    for load in loads[1:]:
        load.start()
    mine = pl.ds(me.z * 8, 8)
    tokens_in = RowsIn(r, me, r.tokens, r.rows_in.at[0], 0)
    upstream_in = RowsIn(r, me, r.cotangent, r.rows_in.at[1], 1)
    act_out = RowsOut(r, me, r.rows_in.at[1], r.act.at[mine], 2)
    grad_out = RowsOut(r, me, r.rows_in.at[1], r.rows_in.at[0, me.z], 3)
    sums = [SmallSum(r, me, number) for number in range(4)]
    outer, early, last = (WeightSum(r, me, number) for number in range(3))

    def run(work):
        pl.when(me.z >= 0)(work)

    pl.semaphore_wait(barrier, OTHERS + GROUP)
    tokens_in.start()
    loads[0].wait()
    own_rows.wait()

    @run
    def first_statistics():
        prepare_rows(r, me.z)
        sums[0].put(row_statistics(r))

    sums[0].start()

    @run
    def masks():
        prepare_masks(r, me.z)

    for load in loads[1:]:
        load.wait()

    @run
    def first_weights():
        counted(0, LAYERS, functools.partial(prepare_weights, r))
        r.grads[...] = jnp.zeros_like(r.grads)

    sums[0].step()
    tokens_in.wait()

    @run
    def tokens():
        take_rows(r.rows_in.at[0], r.x.at[0], r.mask)

    use_statistics(r, 0, sums[0].finish())
    upstream_in.start()

    @run
    def first_layer():
        forward_local(r, 0)
        forward_mixer(r, 0)
        forward_rest(r, 0)
        sums[1].put(statistics_partial(r))

    sums[1].start()

    sums[1].step()
    upstream_in.wait()

    @run
    def upstream():
        take_rows(r.rows_in.at[1], r.dy, r.mask)

    use_statistics(r, 1, sums[1].finish())

    @run
    def second_layer():
        forward_local(r, 1)
        forward_mixer(r, 1)
        turn_rest(r, 1)
        give_rows(r.temp, r.rows_in.at[1])


    @run
    def second_backward():
        backward_mixer(r, 1)
        backward_local(r, 1)
        sums[2].put(statistics_grad_partial(r, 1))

    sums[2].start()

    @run
    def second_products():
        feed_forward_grads(r, 1)
        mixer_grads(r, 1)

    sums[2].step()
    act_out.start()

    @run
    def second_local_products():
        local_grads(r, 1)
        vector_grads(r, 1)

    early.step(0)
    use_statistics_grad(r, 1, sums[2].finish())

    @run
    def between():
        backward_input(r, 1)

    early.step(1)

    @run
    def first_backward():
        backward_rest(r, 0)
        backward_mixer(r, 0)
        feed_forward_grads(r, 0)
        mixer_grads(r, 0)

    outer.step(0)
    early.step(2)

    @run
    def first_local_backward():
        backward_local(r, 0)
        sums[3].put(statistics_grad_partial(r, 0))

    sums[3].start()
    outer.step(1)

    @run
    def first_local_products():
        local_grads(r, 0)
        vector_grads(r, 0)

    last.step(0)
    early.step(3)
    act_out.wait()

    @run
    def input_grad():
        partial_input(r, 0)
        give_rows(r.dy, r.rows_in.at[1])

    grad_out.start()
    last.step(1)
    sums[3].step()
    outer.step(2)
    last.step(2)
    early.step(4)
    use_statistics_grad(r, 0, sums[3].finish())
    outer.step(3)
    last.step(3)
    grad_out.wait()

    @run
    def correction():
        corrected_rows(r, r.own)

    copy = pltpu.make_async_copy(r.own, r.grad, r.out_sem.at[0])
    copy.start()
    early.step(5)
    last.step(4)
    outer.step(4)
    last.step(5)
    outer.step(5)
    totals = pltpu.make_async_copy(r.totals, r.grad_sums, r.out_sem.at[1])
    totals.start()
    copy.wait()
    totals.wait()


def unpack_kernel(act_in, grad_in, totals_in, act, grad, *refs):
    count = len(PARAMS)
    outs, parts, (rows, totals, sems) = refs[:count], refs[count : 2 * count], refs[2 * count :]
    loads = [
        pltpu.make_async_copy(src, dst, sems.at[0, k])
        for k, (src, dst) in enumerate(
            ((totals_in.at[0], totals.at[0]), (totals_in.at[1], totals.at[1]), (act_in, rows.at[0]),
             (grad_in, rows.at[1]))
        )
    ]
    stores = [
        pltpu.make_async_copy(src, dst, sems.at[1, k])
        for k, (src, dst) in enumerate(
            ((rows.at[0], act), (rows.at[1], grad)) + tuple(zip(parts, outs))
        )
    ]
    for load in loads:
        load.start()
    gains, biases, depth, spread, first, second, mixer, output, expand, ebias, reduce = parts
    for l in range(LAYERS):
        loads[l].wait()

        def taken(place, count, width=D, start=0):
            return totals[l, place : place + count, start : start + width]

        gains[l] = taken(1216, 4)
        biases[:, l] = taken(1220, 12)
        depth[:, l] = taken(1232, 9)
        spread[l] = taken(1241, 4)
        first[l] = taken(1024, D)
        second[l] = taken(1120, D)
        output[l] = taken(576, D)
        mixer[l, :, 0:D] = taken(768, D)
        mixer[l, :, D : 2 * D] = taken(864, D)
        for t, place in enumerate(VALUE_PLACES):
            mixer[l, :, 2 * D + t * 32 : 2 * D + (t + 1) * 32] = taken(place, D, 32, D)
        for t in range(3):
            at = slice(t * LANES, (t + 1) * LANES)
            expand[l, :, at] = taken(t * D, D, LANES)
            reduce[l, :, at] = taken(288 + t * D, D, LANES)
            ebias[l : l + 1, at] = taken(1245 + t, 1, LANES)
    for store in stores[2:]:
        store.start()
    for load, store in zip(loads[2:], stores[:2]):
        load.wait()
        store.start()
    for store in stores:
        store.wait()


def turned(params):
    gains, biases, depth, spread, *maps, ebias, reduce = params
    return (gains, jnp.swapaxes(biases, 0, 1), jnp.swapaxes(depth, 0, 1), spread, *maps, ebias,
            jnp.swapaxes(reduce, 1, 2))


def shards(tokens, cotangent, image_size, slot_image, slot_batch, *params):
    params = turned(params)
    sizes = image_size.T
    scratch = scratch_list() + comm_scratch()
    scratch += [
        (name, pltpu.VMEM(p.shape, p.dtype)) for name, p in zip(("sizes",) + PARAMS, (sizes,) + params)
    ]
    ins = ("tokens", "cotangent", "slot_image", "slot_batch", "sizes_in")
    ins += tuple(name + "_in" for name in PARAMS)
    outs = ("act", "grad", "grad_sums")
    names = ins + outs + tuple(name for name, _ in scratch)
    anywhere = pl.BlockSpec(memory_space=pl.ANY)
    smem = pl.BlockSpec(memory_space=pltpu.SMEM)
    rows = jax.ShapeDtypeStruct(tokens.shape, f32)
    act, grad, totals = pl.pallas_call(
        functools.partial(layers_kernel, names),
        out_shape=[rows, rows, jax.ShapeDtypeStruct((LAYERS, GRAD_ROWS, LANES), f32)],
        in_specs=[anywhere, anywhere, smem, smem, anywhere] + [anywhere] * len(params),
        out_specs=[anywhere] * 3,
        scratch_shapes=[shape for _, shape in scratch],
        compiler_params=pltpu.CompilerParams(
            collective_id=0, has_side_effects=True, vmem_limit_bytes=63 * 2**20
        ),
        name="layers",
    )(tokens, cotangent, slot_image, slot_batch, sizes, *params)
    act, grad, *grads = pl.pallas_call(
        unpack_kernel,
        out_shape=[rows, rows] + [jax.ShapeDtypeStruct(p.shape, f32) for p in params],
        in_specs=[anywhere] * 3,
        out_specs=[anywhere] * (2 + len(params)),
        scratch_shapes=[pltpu.VMEM(p.shape, f32) for p in params]
        + [
            pltpu.VMEM((2,) + tokens.shape, f32),
            pltpu.VMEM(totals.shape, f32),
            pltpu.SemaphoreType.DMA((2, 2 + len(params))),
        ],
        compiler_params=pltpu.CompilerParams(vmem_limit_bytes=60 * 2**20),
        name="unpack",
    )(act, grad, totals)
    return (act, grad) + turned(grads)


def solution(mesh):
    rows = P("dp", "segment", None)
    return jax.shard_map(
        shards,
        mesh=mesh,
        in_specs=(rows, rows, P(), P("dp"), P("dp")) + (P(),) * len(PARAMS),
        out_specs=(rows, rows) + (P(),) * len(PARAMS),
        check_vma=False,
    )
```
